32 devices in a mesh: ctx: 8 (over y, x, core), fsdp: 4 (over z).
Axes of the slice: x: 2, y: 2, z: 4, core: 2. Of those that a mesh axis runs over, the one named last changes fastest.
Arguments:
- tokens: bfloat16 [2, 8, 1024, 1536], P(None, 'fsdp', 'ctx'), may hold values from -6 to 6
- lengths: int32 [2, 8], P(None, 'fsdp'), may hold values from 256 to 1024, as said below
- expert_picks: int32 [2, 8, 1024, 4], P(None, 'fsdp', 'ctx'), may hold values from 0 to 31, all different within a row; in each aligned block of 128 rows (0 to 127, 128 to 255, ..., all dimensions but the last counted through in order) at most 20 rows name the same one
- router_weights: float32 [2, 8, 1024, 4], P(None, 'fsdp', 'ctx'), may hold values from 0.12 to 0.36
- first_gain: bfloat16 [1536], P('fsdp'), may hold values from 0.5 to 1.5
- second_gain: bfloat16 [1536], P('fsdp'), may hold values from 0.5 to 1.5
- query_weight: bfloat16 [1536, 1536], P('fsdp'), may hold values from -0.15625 to 0.15625
- key_weight: bfloat16 [1536, 256], P('fsdp'), may hold values from -0.15625 to 0.15625
- value_weight: bfloat16 [1536, 256], P('fsdp'), may hold values from -0.15625 to 0.15625
- output_weight: bfloat16 [1536, 1536], P('fsdp'), may hold values from -2 to 2
- up_weight: bfloat16 [32, 1536, 1536], P('ctx', 'fsdp'), may hold values from -0.15625 to 0.15625
- down_weight: bfloat16 [32, 768, 1536], P('ctx', 'fsdp'), may hold values from -0.3125 to 0.3125
- cotangent: bfloat16 [2, 8, 1024, 1536], P(None, 'fsdp', 'ctx'), may hold values from -6 to 6
Outputs:
- block_output: bfloat16 [2, 8, 1024, 1536], P(None, 'fsdp', 'ctx')
- grad_tokens: float32 [2, 8, 1024, 1536], P(None, 'fsdp', 'ctx')
- grad_router: float32 [2, 8, 1024, 4], P(None, 'fsdp', 'ctx')
- grad_first: float32 [1536], P('fsdp')
- grad_second: float32 [1536], P('fsdp')
- grad_query: float32 [1536, 1536], P('fsdp')
- grad_key: float32 [1536, 256], P('fsdp')
- grad_value: float32 [1536, 256], P('fsdp')
- grad_projection: float32 [1536, 1536], P('fsdp')
- grad_up: float32 [32, 1536, 1536], P('ctx', 'fsdp')
- grad_down: float32 [32, 768, 1536], P('ctx', 'fsdp')
The draws below stay inside these ranges and needn't reach their ends.
Inputs may be any that keep to these rules, and one draw needn't show every extreme that they name: `lengths`: in each micro-batch, one of the 2 sequences of each index of fsdp has the full length 1024. `expert_picks`: A row names 4 different experts. Among the 128 rows of one sequence that lie on one device, no expert is named by more than 20 rows, a bound that some block reaches.
All inputs are finite; a program needn't handle non-finite values.
Results may differ from the reference program's by a relative error of at most 0.02.
Values may be sent and summed in bfloat16 or wider, within the bound.
No kernel may reach another device: no remote copies, remote signals or barrier semaphores. Data moves between devices by JAX's collectives and lax.ppermute only.
A program may use at most 200 MiB of HBM per device.

```python
import math
import jax
import jax.numpy as jnp
import numpy as np
from jax import lax

D = 1536
H = 12
KV = 2
HD = 128
FF = 768
TOP = 4
EXPERTS = 32
MB = 2
SEQS = 2
TOK = 128
LEN = 1024
SEQ_ALL = 8
WSPLIT = 1
CAP = 20


def draw_lengths(key, part):
    key = jax.random.fold_in(key, 11)
    first_key, second_key = jax.random.split(key)
    group_count = SEQ_ALL // SEQS
    base = jax.random.randint(first_key, (MB, group_count, SEQS), LEN // 4, LEN + 1)
    longest = jax.random.randint(second_key, (MB, group_count, 1), 0, SEQS)
    filled = jnp.where(jnp.arange(SEQS)[None, None, :] == longest, LEN, base)
    return filled.reshape(MB, SEQ_ALL).astype(jnp.int32)


def block_scale(rng, shape, pieces, low, top_value):
    factor_of, own = 1.0, jax.random.fold_in(rng, 6)
    for position, blocks in pieces:
        heights = jnp.exp(jax.random.uniform(jax.random.fold_in(own, position), (blocks,), jnp.float32, low / len(pieces), top_value / len(pieces)))
        factor_of = factor_of * jnp.repeat(heights, shape[position] // blocks).reshape([-1 if axis == position else 1 for axis in range(len(shape))])
    return factor_of


def routed_block(own_key, own, number, rows, number_of, top, most, skew):
    ranking = jax.random.permutation(own_key, number_of)
    packed, usual = portions_of(number_of, rows * top, most, skew, True), portions_of(number_of, rows * top, most, skew, False)
    places = jnp.arange(number_of)

    def named(sizes, rotation):
        used = int((sizes > 0).sum())
        fixed = max(1, used // 4)
        moved = fixed + (places - fixed + rotation * (used - fixed)) % max(1, number_of - fixed)
        return jnp.zeros((number_of,), jnp.int32).at[ranking[jnp.where(places < fixed, places, moved)]].set(jnp.asarray(sizes, jnp.int32))

    sizes = jnp.where(number % 4 == 0, named(packed, number // 4), named(usual, number - number // 4 - 1))
    mixed = jax.random.permutation(jax.random.fold_in(own, 3), number_of)
    source_of, receiver = mixed[0:number_of // 2 * 2:2], mixed[1:number_of // 2 * 2:2]
    room = jnp.minimum(sizes[source_of] - 1, most - sizes[receiver]) // 2
    room = jnp.where((source_of == ranking[0]) | (receiver == ranking[0]) | (sizes[receiver] == 0), 0, jnp.maximum(room, 0))
    moved = jax.random.randint(jax.random.fold_in(own, 4), (number_of // 2,), 0, 1 << 20) % (room + 1)
    sizes = sizes.at[source_of].add(-moved).at[receiver].add(moved)
    members = jnp.searchsorted(jnp.cumsum(sizes), jnp.arange(rows * top), side="right").astype(jnp.int32)
    listing = members.reshape(top, rows).T
    listing = listing[jax.random.permutation(jax.random.fold_in(own, 1), rows)]
    rotation = jax.random.randint(jax.random.fold_in(own, 2), (rows, 1), 0, top)
    return jnp.take_along_axis(listing, (jnp.arange(top)[None, :] + rotation) % top, axis=1)


def portions_of(count, total, limit, skew, full):
    weights = [(1 << 20) // math.isqrt(standing ** skew) + 1 for standing in range(1, count + 1)]
    largest = limit if full else min(limit, max(-(-total // count), total * weights[0] // sum(weights)))
    least = 1 if total - largest >= count - 1 else 0
    given, surplus = [largest] + [least] * (count - 1), total - largest - least * (count - 1)
    while surplus > 0:
        movable = [i for i in range(1, count) if given[i] < largest] or [i for i in range(1, count) if given[i] < limit]
        mass, remaining = sum([weights[i] for i in movable]), surplus
        for i in movable:
            extra = min(limit - given[i], max(1, remaining * weights[i] // mass), surplus)
            given[i] = given[i] + extra
            surplus = surplus - extra
    return np.array(given)


def bell_draw(rng, dims, scale, bound, cuts=(), held_as=jnp.bfloat16):
    drawn = scale * jax.random.normal(rng, dims, jnp.float32)
    if cuts:
        drawn = drawn * block_scale(rng, dims, cuts, -0.22, 0.18)
    return jnp.clip(drawn, -bound, bound).astype(held_as)


def setup_inputs(seed: int = 0) -> dict:
    key_list = jax.random.split(jax.random.key(seed), 14)
    tokens = bell_draw(key_list[0], (MB, SEQ_ALL, LEN, D), 1.0, 6.0, ((1, 4), (2, 8)))
    lengths = draw_lengths(jax.random.fold_in(key_list[13], 71), 0)
    expert_picks_keys = jax.random.split(jax.random.fold_in(key_list[2], 1), MB * SEQ_ALL * LEN // TOK)
    expert_picks_turns = jax.random.permutation(jax.random.fold_in(key_list[2], 3), MB * SEQ_ALL * LEN // TOK)
    expert_picks = jax.vmap(lambda own, number: routed_block(jax.random.fold_in(key_list[2], 2), own, number, TOK, EXPERTS, TOP, CAP, 2))(expert_picks_keys, expert_picks_turns).reshape((MB, SEQ_ALL, LEN, TOP))
    router_weights = jnp.clip(jnp.exp(math.log(0.36) - 1.09861235 * jax.random.uniform(key_list[3], (MB, SEQ_ALL, LEN, TOP), jnp.float32) ** block_scale(key_list[3], (MB, SEQ_ALL, LEN, TOP), ((1, 4), (2, 8)), -0.2, 0.2)), 0.12, 0.36)
    first_gain = jnp.clip(1.0 + 0.1 * jax.random.normal(key_list[4], (D,), jnp.float32), 0.5, 1.5).astype(jnp.bfloat16)
    second_gain = jnp.clip(1.0 + 0.1 * jax.random.normal(key_list[5], (D,), jnp.float32), 0.5, 1.5).astype(jnp.bfloat16)
    query_weight = bell_draw(key_list[6], (D, H * HD), D ** -0.5, 0.15625, ((0, 4),))
    key_weight = bell_draw(key_list[7], (D, KV * HD), D ** -0.5, 0.15625, ((0, 4),))
    value_weight = bell_draw(key_list[8], (D, KV * HD), D ** -0.5, 0.15625, ((0, 4),))
    output_weight = bell_draw(key_list[9], (H * HD, D), (max(1, H * HD * 5 // LEN)) ** -0.5, 2.0, ((0, 4),))
    up_weight = bell_draw(key_list[10], (EXPERTS * WSPLIT, D, 2 * FF // WSPLIT), D ** -0.5, 0.15625, ((0, 8), (1, 4)))
    down_weight = bell_draw(key_list[11], (EXPERTS * WSPLIT, FF // WSPLIT, D), (FF // 2) ** -0.5, 0.3125, ((0, 8), (1, 4)))
    cotangent = bell_draw(key_list[12], (MB, SEQ_ALL, LEN, D), 1.0, 6.0, ((1, 4), (2, 8)))
    return dict(tokens=tokens, lengths=lengths, expert_picks=expert_picks, router_weights=router_weights, first_gain=first_gain, second_gain=second_gain, query_weight=query_weight, key_weight=key_weight, value_weight=value_weight, output_weight=output_weight, up_weight=up_weight, down_weight=down_weight, cotangent=cotangent)


EPSILON = 1e-06
ROPE_BASE = 10000.0
HIGHEST = lax.Precision.HIGHEST

@jax.custom_vjp
def low(v):
    return lax.optimization_barrier(v.astype(jnp.bfloat16)).astype(jnp.float32)

@jax.custom_vjp
def low_back(v):
    return v

def low_keep(v):
    return (low(v), None)

def low_pass(kept, grad):
    return (grad,)

def back_keep(v):
    return (v, None)

def back_low(kept, grad):
    return (low(grad),)
low.defvjp(low_keep, low_pass)
low_back.defvjp(back_keep, back_low)

def rotate(vectors, positions):
    half_dim = HD // 2
    frequency = ROPE_BASE ** (-(jnp.arange(half_dim, dtype=jnp.float32) * 2.0 / HD))
    angles = positions.astype(jnp.float32)[:, None] * frequency[None, :]
    cosine_part = jnp.cos(angles)[:, None, :]
    sine_part = jnp.sin(angles)[:, None, :]
    leading = vectors[..., :half_dim]
    trailing = vectors[..., half_dim:]
    return jnp.concatenate([leading * cosine_part - trailing * sine_part, trailing * cosine_part + leading * sine_part], axis=-1)

def norm_apply(values, gain_row):
    inverse = lax.rsqrt(lax.optimization_barrier(jnp.mean(values * values, axis=-1, keepdims=True)) + EPSILON)
    return values * inverse * gain_row

def one_sequence(params, values, gate_weights, length, chosen):
    first_gain, second_gain, query_weight, key_weight, value_weight, output_weight, up_weight, down_weight = params
    block_width = FF // WSPLIT
    up_full = up_weight.reshape(EXPERTS, WSPLIT, D, 2, block_width).transpose(0, 2, 3, 1, 4).reshape(EXPERTS, D, 2 * FF)
    down_full = down_weight.reshape(EXPERTS, FF, D)
    positions = jnp.arange(LEN)
    live_rows = (positions < length).astype(jnp.float32)[:, None]
    normed = low(norm_apply(values, first_gain))
    queries = low_back(jnp.dot(normed, query_weight, precision=HIGHEST))
    key_rows = low_back(jnp.dot(normed, key_weight, precision=HIGHEST))
    value_rows = low_back(jnp.dot(normed, value_weight, precision=HIGHEST))
    turned_queries = low(rotate(queries.reshape(LEN, H, HD), positions))
    turned_keys = low(rotate(key_rows.reshape(LEN, KV, HD), positions))
    values_low = low(value_rows.reshape(LEN, KV, HD))
    grouped = turned_queries.reshape(LEN, KV, H // KV, HD)
    scores = jnp.einsum('qkgd,nkd->kgqn', grouped, turned_keys, precision=HIGHEST) * HD ** (-0.5)
    scores = low_back(scores)
    allowed = (positions[None, :] <= positions[:, None]) & (positions[None, :] < length)
    scores = jnp.where(allowed[None, None], scores, -1e+30)
    weights = low(jax.nn.softmax(scores, axis=-1))
    attended = jnp.einsum('kgqn,nkd->qkgd', weights, values_low, precision=HIGHEST).reshape(LEN, H * HD)
    attended = low(low_back(attended))
    branch = low_back(jnp.dot(attended, output_weight, precision=HIGHEST))
    hidden = values + live_rows * branch
    expert_in = low(norm_apply(hidden, second_gain))
    spread = low_back(jnp.broadcast_to(expert_in[None], (EXPERTS, LEN, D)))
    gate_up = low_back(jnp.einsum('etd,edf->etf', spread, up_full, precision=HIGHEST))
    active = low(jax.nn.silu(gate_up[..., :FF]) * gate_up[..., FF:])
    returned = low(low_back(jnp.einsum('etf,efd->etd', active, down_full, precision=HIGHEST)))
    choose = (chosen[:, :, None] == jnp.arange(EXPERTS)[None, None, :]).astype(jnp.float32)
    combine = lax.optimization_barrier(jnp.sum(gate_weights[:, :, None] * choose, axis=1)) * live_rows
    return hidden + jnp.einsum('te,etd->td', combine, returned, precision=HIGHEST)

def reference(tokens, lengths, expert_picks, router_weights, first_gain, second_gain, query_weight, key_weight, value_weight, output_weight, up_weight, down_weight, cotangent):
    params = tuple((member.astype(jnp.float32) for member in (first_gain, second_gain, query_weight, key_weight, value_weight, output_weight, up_weight, down_weight)))
    seq_count = MB * SEQ_ALL
    inputs = tokens.astype(jnp.float32).reshape(seq_count, LEN, D)
    gate_values = router_weights.astype(jnp.float32).reshape(seq_count, LEN, TOP)
    all_lengths = lengths.reshape(seq_count).astype(jnp.int32)
    all_picks = expert_picks.reshape(seq_count, LEN, TOP).astype(jnp.int32)
    sequence_step = jax.checkpoint(one_sequence)

    def forward(params, inputs, gate_values):
        return lax.map(lambda element: sequence_step(params, element[0], element[1], element[2], element[3]), (inputs, gate_values, all_lengths, all_picks))
    outputs, pullback = jax.vjp(forward, params, inputs, gate_values)
    param_grads, input_grads, gate_grads = pullback(cotangent.astype(jnp.float32).reshape(seq_count, LEN, D))
    return (outputs.astype(jnp.bfloat16).reshape(MB, SEQ_ALL, LEN, D), input_grads.reshape(MB, SEQ_ALL, LEN, D), gate_grads.reshape(MB, SEQ_ALL, LEN, TOP), param_grads[0], param_grads[1], param_grads[2], param_grads[3], param_grads[4], param_grads[5], param_grads[6], param_grads[7])
```

```python
import jax
import jax.numpy as jnp
from jax import lax
from jax.experimental import pallas as pl
from jax.experimental.pallas import tpu as pltpu
from jax.sharding import PartitionSpec as P

H = 12
KV = 2
HD = 128
TOP = 4
EXPERTS = 32
EPSILON = 1e-06
ROPE_BASE = 10000.0
NEGATIVE = -1e30
F32 = jnp.float32
BF16 = jnp.bfloat16


def angle_tables(positions):
    half_dim = HD // 2
    frequency = ROPE_BASE ** (-(jnp.arange(half_dim, dtype=F32) * 2.0 / HD))
    angles = positions.astype(F32)[:, None] * frequency[None, :]
    return jnp.cos(angles), jnp.sin(angles)


def rotate(vectors, cosine, sine):
    half_dim = HD // 2
    leading = vectors[..., :half_dim]
    trailing = vectors[..., half_dim:]
    cosine, sine = cosine[:, None, :], sine[:, None, :]
    return jnp.concatenate(
        [leading * cosine - trailing * sine, trailing * cosine + leading * sine], axis=-1
    )


def norm_forward(values, gain_row):
    inverse = lax.rsqrt(jnp.mean(values * values, axis=-1, keepdims=True) + EPSILON)
    return values * inverse * gain_row, inverse


def norm_backward(values, inverse, gain_row, upstream):
    gain_grad = jnp.sum(upstream * values * inverse, axis=0)
    scaled = upstream * gain_row
    projected = jnp.mean(scaled * values, axis=-1, keepdims=True)
    return inverse * scaled - values * inverse**3 * projected, gain_grad


def mm(a, b):
    return jnp.dot(a, b, preferred_element_type=F32)


def mm_nt(a, b):
    return lax.dot_general(a, b, (((1,), (1,)), ((), ())), preferred_element_type=F32)


def mm_tn(a, b):
    return lax.dot_general(a, b, (((0,), (0,)), ((), ())), preferred_element_type=F32)


VMEM_LIMIT = 60 * 1024 * 1024


def stack_heads(block, groups):
    return jnp.concatenate([block[:, h * HD : (h + 1) * HD] for h in range(groups)], axis=0)


def masked_scores(stacked, keys, first, length, groups):
    tl = stacked.shape[0] // groups
    total = keys.shape[0]
    scores = mm_nt(stacked, keys) * HD ** (-0.5)
    key_at = lax.broadcasted_iota(jnp.int32, (tl, total), 1)
    query_at = lax.broadcasted_iota(jnp.int32, (tl, total), 0) + first
    allowed = (key_at <= query_at) & (key_at < length)
    scores = scores.reshape(groups, tl, total)
    return jnp.where(allowed[None], scores, NEGATIVE).reshape(groups * tl, total)


def attend_kernel(groups, info, q_ref, kv_ref, att_ref, lse_ref):
    tl = q_ref.shape[1]
    stacked = stack_heads(q_ref[0], groups)
    scores = masked_scores(
        stacked, kv_ref[0, :, :HD], info[0], info[1 + pl.program_id(0)], groups
    )
    top = jnp.max(scores, axis=-1, keepdims=True)
    shares = jnp.exp(scores - top)
    total = jnp.sum(shares, axis=-1, keepdims=True)
    out = mm(shares.astype(BF16), kv_ref[0, :, HD:]) / total
    lse = top + jnp.log(total)
    for h in range(groups):
        at = slice(h * tl, (h + 1) * tl)
        att_ref[0, :, h * HD : (h + 1) * HD] = out[at].astype(BF16)
        lse_ref[0, 0, :, h : h + 1] = lse[at]


def attend_back_kernel(groups, info, q_ref, kv_ref, da_ref, lse_ref, dq_ref, dkv_ref):
    tl = q_ref.shape[1]
    keys, values = kv_ref[0, :, :HD], kv_ref[0, :, HD:]
    stacked = stack_heads(q_ref[0], groups)
    scores = masked_scores(stacked, keys, info[0], info[1 + pl.program_id(0)], groups)
    lse = jnp.concatenate([lse_ref[0, 0, :, h : h + 1] for h in range(groups)], axis=0)
    probs = jnp.exp(scores - lse)
    grads = stack_heads(da_ref[0], groups)
    d_probs = mm_nt(grads, values)
    delta = jnp.sum(probs * d_probs, axis=-1, keepdims=True)
    d_scores = (probs * (d_probs - delta)).astype(BF16)
    dq = mm(d_scores, keys) * HD ** (-0.5)
    for h in range(groups):
        dq_ref[0, :, h * HD : (h + 1) * HD] = dq[h * tl : (h + 1) * tl]
    dk = mm_tn(d_scores, stacked) * HD ** (-0.5)
    dv = mm_tn(probs.astype(BF16), grads)
    shape = dkv_ref.shape[:1] + (tl, HD)
    dkv_ref[:, 0, :, :HD] = dk.reshape(shape).astype(BF16)
    dkv_ref[:, 0, :, HD:] = dv.reshape(shape).astype(BF16)


def attention(queries, kv_all, info):
    nseq, tl, width = queries.shape
    total = kv_all.shape[1]
    groups = H // KV
    return pl.pallas_call(
        lambda *refs: attend_kernel(groups, *refs),
        grid_spec=pltpu.PrefetchScalarGridSpec(
            num_scalar_prefetch=1,
            grid=(nseq, KV),
            in_specs=[
                pl.BlockSpec((1, tl, groups * HD), lambda s, n, info: (s, 0, n)),
                pl.BlockSpec((1, total, 2 * HD), lambda s, n, info: (s, 0, n)),
            ],
            out_specs=[
                pl.BlockSpec((1, tl, groups * HD), lambda s, n, info: (s, 0, n)),
                pl.BlockSpec((1, 1, tl, HD), lambda s, n, info: (s, n, 0, 0)),
            ],
        ),
        out_shape=[
            jax.ShapeDtypeStruct((nseq, tl, width), BF16),
            jax.ShapeDtypeStruct((nseq, KV, tl, HD), F32),
        ],
        compiler_params=pltpu.CompilerParams(vmem_limit_bytes=VMEM_LIMIT),
        cost_estimate=pl.CostEstimate(
            flops=28 * nseq * tl * width * total,
            bytes_accessed=4 * queries.size * 2 + 2 * kv_all.size,
            transcendentals=nseq * H * tl * total,
        ),
    )(info, queries, kv_all)


def attention_back(queries, kv_all, d_att, lse, info, ctx_count):
    nseq, tl, width = queries.shape
    total = kv_all.shape[1]
    groups = H // KV
    return pl.pallas_call(
        lambda *refs: attend_back_kernel(groups, *refs),
        grid_spec=pltpu.PrefetchScalarGridSpec(
            num_scalar_prefetch=1,
            grid=(nseq, KV),
            in_specs=[
                pl.BlockSpec((1, tl, groups * HD), lambda s, n, info: (s, 0, n)),
                pl.BlockSpec((1, total, 2 * HD), lambda s, n, info: (s, 0, n)),
                pl.BlockSpec((1, tl, groups * HD), lambda s, n, info: (s, 0, n)),
                pl.BlockSpec((1, 1, tl, HD), lambda s, n, info: (s, n, 0, 0)),
            ],
            out_specs=[
                pl.BlockSpec((1, tl, groups * HD), lambda s, n, info: (s, 0, n)),
                pl.BlockSpec((ctx_count, 1, tl, 2 * HD), lambda s, n, info: (0, s, 0, n)),
            ],
        ),
        out_shape=[
            jax.ShapeDtypeStruct((nseq, tl, width), F32),
            jax.ShapeDtypeStruct((ctx_count, nseq, tl, KV * 2 * HD), BF16),
        ],
        compiler_params=pltpu.CompilerParams(vmem_limit_bytes=VMEM_LIMIT),
        cost_estimate=pl.CostEstimate(
            flops=36 * nseq * tl * width * total,
            bytes_accessed=6 * queries.size * 2 + 4 * kv_all.size,
            transcendentals=nseq * H * tl * total,
        ),
    )(info, queries, kv_all, d_att, lse)


def expert_kernel(sides, merged, *refs):
    info = refs[0]
    xs = refs[1 : 1 + sides]
    gs = refs[1 + sides : 1 + 2 * sides]
    count = 11 if merged else 2
    weights = refs[1 + 2 * sides : 1 + 2 * sides + count]
    at = 1 + 2 * sides + count
    din_ref, wy_ref = refs[at : at + 2]
    at = at + 2
    out_refs = refs[at : at + (1 if merged else 2)]
    at = at + (1 if merged else 2)
    up, down, x_t, act_t, dgu, dy, act_s, pre, wide, gup, gdn, sems = refs[at:]
    step, steps = pl.program_id(0), pl.num_programs(0)
    D, W = up.shape[0], down.shape[0]
    tile = wide.shape[0]
    tw = 256 if W % 256 == 0 else 128
    td = 256

    wl = W // 4

    def shard_rows(source, chunk):
        if chunk == 2:
            return down, gdn, pl.ds(pl.multiple_of(source * wl, 16), wl)
        return up, gup, pl.ds(pl.multiple_of((2 * source + chunk) * wl, 16), wl)

    def loads():
        if not merged:
            pairs = [(weights[0].at[info[2]], up), (weights[1].at[info[2]], down)]
        else:
            pairs = []
            for k in range(4):
                for chunk in range(3):
                    to, _, at = shard_rows(lax.rem(info[0] + 4 - k, 4), chunk)
                    if k:
                        block = weights[2 + 3 * (k - 1) + chunk]
                    elif chunk < 2:
                        block = weights[0].at[info[2], pl.ds(chunk * wl, wl)]
                    else:
                        block = weights[1].at[info[2]]
                    pairs.append((block, to.at[at]))
        return [pltpu.make_async_copy(a, b, sems.at[i]) for i, (a, b) in enumerate(pairs)]

    def put(ref, columns, block):
        per = tile // sides
        shape = (ref.shape[0], ref.shape[2], block.shape[1])
        for i in range(sides):
            ref[:, i, :, columns] = block[i * per : (i + 1) * per].reshape(shape)

    @pl.when(step == 0)
    def _():
        copies = loads()
        for copy in copies:
            copy.start()
        for copy in copies:
            copy.wait()

    rows = pl.ds(pl.multiple_of(step * tile, 128), tile)
    x = jnp.concatenate([r[...].reshape(-1, D) for r in xs], axis=0)
    g_aug = jnp.concatenate([r[...].reshape(-1, D + HD) for r in gs], axis=0)
    x_t[:, rows] = x.T
    lane = lax.broadcasted_iota(jnp.int32, (tile, HD), 1)
    picked = (lane == info[1]) | (lane == info[1] + HD // 2)
    w = jnp.sum(jnp.where(picked, g_aug[:, D:].astype(F32), 0.0), axis=1, keepdims=True)
    wide[...] = g_aug[:, :D]
    dy[rows, :] = (g_aug[:, :D].astype(F32) * w).astype(BF16)

    @pl.loop(0, W // tw)
    def _(t):
        a = pl.ds(pl.multiple_of(t * tw, 128), tw)
        b = pl.ds(pl.multiple_of(W + t * tw, 128), tw)
        gate = mm(x, up[:, a])
        lift = mm(x, up[:, b])
        pre[:, a] = gate
        pre[:, b] = lift
        act = gate / (1.0 + jnp.exp(-gate)) * lift
        act = act.astype(BF16)
        act_s[:, a] = act
        act_t[a, rows] = act.T

    def out_step(t, total):
        a = pl.ds(pl.multiple_of(t * td, 128), td)
        y = mm(act_s[...], down[:, a])
        put(wy_ref, a, (y * w).astype(BF16))
        return total + jnp.sum(y * wide[:, a].astype(F32), axis=1, keepdims=True)

    router = lax.fori_loop(0, D // td, out_step, jnp.zeros((tile, 1), F32))
    extra = jnp.where(lane == info[1], router, 0.0).astype(BF16)
    put(wy_ref, pl.ds(D, HD), extra)

    @pl.loop(0, W // tw)
    def _(t):
        a = pl.ds(pl.multiple_of(t * tw, 128), tw)
        b = pl.ds(pl.multiple_of(W + t * tw, 128), tw)
        d_act = mm_nt(dy[rows, :], down[a, :])
        gate, lift = pre[:, a], pre[:, b]
        sig = 1.0 / (1.0 + jnp.exp(-gate))
        dgu[rows, a] = (d_act * lift * sig * (1.0 + gate * (1.0 - sig))).astype(BF16)
        dgu[rows, b] = (d_act * gate * sig).astype(BF16)

    @pl.loop(0, D // td)
    def _(t):
        a = pl.ds(pl.multiple_of(t * td, 128), td)
        put(din_ref, a, mm_nt(dgu[rows, :], up[a, :]).astype(BF16))

    @pl.when(step == steps - 1)
    def _():
        @pl.loop(0, D // td)
        def _(t):
            a = pl.ds(pl.multiple_of(t * td, 128), td)
            gup[a, :] = mm(x_t[a, :], dgu[...]).astype(BF16)

        @pl.loop(0, W // tw)
        def _(t):
            a = pl.ds(pl.multiple_of(t * tw, 128), tw)
            gdn[a, :] = mm(act_t[a, :], dy[...]).astype(BF16)

        if merged:
            pairs = []
            for k in range(4):
                for chunk in range(3):
                    _, block, at = shard_rows(lax.rem(info[0] + k, 4), chunk)
                    pairs.append((block.at[at], out_refs[0].at[k, chunk]))
        else:
            pairs = [(gup, out_refs[0]), (gdn, out_refs[1])]
        copies = [pltpu.make_async_copy(a, b, sems.at[i]) for i, (a, b) in enumerate(pairs)]
        for copy in copies:
            copy.start()
        for copy in copies:
            copy.wait()


def run_expert(piece, xs, gs, weights, info, merged):
    C, mine, slots, D = xs[0].shape
    sides = len(xs)
    W = weights[0].shape[2] // 2
    per_step = C
    while per_step > 1 and (per_step * sides * slots > 640 or C % per_step):
        per_step -= 1
    tile = per_step * sides * slots
    rows = C * sides * slots

    def spec(width, at):
        return pl.BlockSpec((per_step, 1, slots, width), lambda i, info: (i, at, 0, 0))

    def out_spec(width):
        return pl.BlockSpec((per_step, sides, slots, width), lambda i, info: (i, 0, 0, 0))

    any_spec = pl.BlockSpec(memory_space=pl.ANY)
    if merged:
        grads = [jax.ShapeDtypeStruct((4, 3) + weights[2].shape, BF16)]
    else:
        grads = [jax.ShapeDtypeStruct((D, 2 * W), BF16), jax.ShapeDtypeStruct((W, D), BF16)]
    return pl.pallas_call(
        lambda *refs: expert_kernel(sides, merged, *refs),
        grid_spec=pltpu.PrefetchScalarGridSpec(
            num_scalar_prefetch=1,
            grid=(C // per_step,),
            in_specs=[spec(D, piece)] * sides
            + [spec(D + HD, piece)] * sides
            + [any_spec] * len(weights),
            out_specs=[out_spec(D), out_spec(D + HD)] + [any_spec] * len(grads),
            scratch_shapes=[
                pltpu.VMEM((D, 2 * W), BF16),
                pltpu.VMEM((W, D), BF16),
                pltpu.VMEM((D, rows), BF16),
                pltpu.VMEM((W, rows), BF16),
                pltpu.VMEM((rows, 2 * W), BF16),
                pltpu.VMEM((rows, D), BF16),
                pltpu.VMEM((tile, W), BF16),
                pltpu.VMEM((tile, 2 * W), F32),
                pltpu.VMEM((tile, D), BF16),
                pltpu.VMEM((D, 2 * W), BF16),
                pltpu.VMEM((W, D), BF16),
                pltpu.SemaphoreType.DMA((12,)),
            ],
        ),
        out_shape=[jax.ShapeDtypeStruct((C, sides, slots, n), BF16) for n in (D, D + HD)]
        + grads,
        compiler_params=pltpu.CompilerParams(vmem_limit_bytes=VMEM_LIMIT),
        cost_estimate=pl.CostEstimate(
            flops=38 * rows * D * W,
            bytes_accessed=8 * rows * D + 24 * D * W,
            transcendentals=2 * rows * W,
        ),
    )(info, *xs, *gs, *weights)


def local(
    tokens,
    lengths,
    expert_picks,
    router_weights,
    first_gain,
    second_gain,
    query_weight,
    key_weight,
    value_weight,
    output_weight,
    up_weight,
    down_weight,
    cotangent,
):
    batches, seqs_here, tl, D = tokens.shape
    C = lax.axis_size("ctx")
    F = lax.axis_size("fsdp")
    c = lax.axis_index("ctx")
    f = lax.axis_index("fsdp")
    split = max(1, C // EXPERTS)
    pieces = up_weight.shape[0]
    W = up_weight.shape[2] // 2
    merged = pieces % 2 == 0 and F == 4 and 2 * W == D
    share = 2 if merged else 1
    mine = pieces // share
    role = f % share
    nseq = batches * seqs_here
    cap = max(2, (5 * tl * TOP + 4 * EXPERTS - 1) // (4 * EXPERTS))
    while nseq * cap % 16:
        cap += 1
    slots = nseq * cap
    rows = nseq * tl
    L = C * tl
    width = H * HD
    Dl = query_weight.shape[0]
    cut = Dl // C

    positions = c * tl + jnp.arange(tl, dtype=jnp.int32)
    cosine, sine = angle_tables(positions)
    lens = lengths.reshape(nseq)
    live = (positions[None, :] < lens[:, None]).reshape(rows)
    live_rows = live.astype(F32)[:, None]

    def gate(*values):
        return lax.optimization_barrier(values)

    def shift(block, k):
        return lax.ppermute(block, "fsdp", [(i, (i + k) % F) for i in range(F)])

    def fsdp_gather(block):
        got = [shift(block, k) for k in range(F - 1, 0, -1)]
        ring = jnp.stack(got + [block] + got)
        return lax.dynamic_slice_in_dim(ring, F - 1 - f, F, 0)

    def fsdp_scatter_sum(parts):
        total = lax.dynamic_index_in_dim(parts, f, 0, keepdims=False).astype(F32)
        for k in range(1, F):
            block = lax.dynamic_index_in_dim(parts, (f + k) % F, 0, keepdims=False)
            total = total + shift(block, k).astype(F32)
        return total

    def swap(block):
        return lax.ppermute(block, "fsdp", [(i, i ^ 1) for i in range(F)])

    def exchange(blocks):
        return lax.all_to_all(blocks, "ctx", 0, 0, tiled=True)

    def ctx_gather(lines):
        return lax.all_gather(lines, "ctx", axis=1, tiled=True).reshape(D, -1)

    def part_of(weight):
        return lax.dynamic_slice_in_dim(weight, c * cut, cut, 0)

    key_value = jnp.concatenate(
        [
            w[:, h * HD : (h + 1) * HD]
            for h in range(KV)
            for w in (key_weight, value_weight)
        ],
        axis=1,
    )
    query_part, out_part = part_of(query_weight), part_of(output_weight)
    gains = fsdp_gather(jnp.stack([first_gain, second_gain]))
    first_scale = gains[:, 0].reshape(D).astype(F32)
    second_scale = gains[:, 1].reshape(D).astype(F32)
    kv_lines, query_lines = fsdp_gather(part_of(key_value)), fsdp_gather(query_part)

    messages = {}
    grads_out = []

    def operand(name):
        kind, j, chunk, k = name
        if kind == "g":
            return grads_out[j][k, chunk]
        at = ((f + k) % share) * mine + j
        size = (1, W // F, up_weight.shape[2])
        if chunk == 2:
            return lax.dynamic_slice(down_weight, (at, 0, 0), size)[0]
        return lax.dynamic_slice(up_weight, (at, chunk * (W // F), 0), size)[0]

    def step(need, values, go):
        if not merged:
            return lax.optimization_barrier(values)
        fresh = tuple(operand(name) for name in go)
        got, values, fresh = lax.optimization_barrier(
            (tuple(messages[name] for name in need), values, fresh)
        )
        messages.update(zip(need, got))
        messages.update((name, shift(block, name[3])) for name, block in zip(go, fresh))
        return values

    def names(kind, j, *codes):
        return [(kind, j, "abc".index(code[0]), int(code[1])) for code in codes]

    picks = expert_picks.reshape(rows, TOP)
    gates = router_weights.reshape(rows, TOP)
    cot = cotangent.reshape(rows, D)
    expert_ids = jnp.arange(EXPERTS, dtype=jnp.int32)
    hit = picks[:, :, None] == expert_ids
    by_expert = jnp.sum(jnp.where(hit, gates[:, :, None], 0.0), axis=1) * live_rows
    high = by_expert.astype(BF16)
    low = (by_expert - high.astype(F32)).astype(BF16)
    gap = jnp.zeros((rows, HD // 2 - EXPERTS), BF16)
    cot_wide = jnp.concatenate([cot, high, gap, low, gap], axis=1)
    number = jnp.arange(C)[:, None] * pieces + role * mine + jnp.arange(mine)[None, :]
    expert_of = (number // split).reshape(C * mine)
    earlier = jnp.tril(jnp.ones((tl, tl), BF16), -1)
    pick_map = (expert_ids[:, None] == expert_of[None, :]).astype(BF16)

    def route(wide):
        match = wide[:, D : D + EXPERTS] > 0
        ranks = jnp.einsum(
            "ab,sbe->sae",
            earlier,
            match.astype(BF16).reshape(nseq, tl, -1),
            preferred_element_type=F32,
        )
        base = (jnp.arange(nseq) * cap)[:, None, None]
        code = jnp.where(match, (ranks + base).reshape(rows, -1), -1.0).astype(BF16)
        code = mm_tn(pick_map, code.T)
        chosen = code[:, None, :] == jnp.arange(slots, dtype=F32)[None, :, None]
        return chosen.astype(BF16).reshape(C, mine, slots, rows)

    def to_slots(sel, source):
        out = mm(sel.reshape(C * mine * slots, rows), source)
        return out.astype(BF16).reshape(C, mine, slots, -1)

    sels = [route(cot_wide)]

    inputs = tokens.reshape(rows, D).astype(F32)
    normed, inverse_one = norm_forward(inputs, first_scale)
    normed_low = normed.astype(BF16)
    now = names("w", 0, "a1", "b1")
    kv_lines, query_lines = step([], (kv_lines, query_lines), now)
    kv_full = ctx_gather(kv_lines)
    then, now = now, names("w", 0, "c1", "a3")
    kv_full, query_lines, out_part, cot_wide = step(
        then, (kv_full, query_lines, out_part, cot_wide), now
    )
    query_full = ctx_gather(query_lines)
    out_lines = fsdp_gather(out_part)
    g_in = [exchange(to_slots(sels[0], cot_wide))]
    kv_pre = mm(normed_low, kv_full).reshape(nseq, tl, KV, 2, HD)
    turned_key = rotate(kv_pre[..., 0, :], cosine, sine).astype(BF16)
    kv_low = jnp.stack([turned_key, kv_pre[..., 1, :].astype(BF16)], axis=3)
    kv_low = kv_low.reshape(nseq, tl, KV * 2 * HD)
    then, now = now, names("w", 0, "a2")
    query_full, kv_low, out_lines, cot_wide = step(
        then, (query_full, kv_low, out_lines, cot_wide), now
    )
    kv_all = lax.all_gather(kv_low, "ctx", axis=1, tiled=True)
    far_cot = swap(cot_wide) if share == 2 else cot_wide
    query_pre = mm(normed_low, query_full).reshape(nseq, tl, H, HD)
    queries = rotate(query_pre, cosine, sine).astype(BF16).reshape(nseq, tl, width)
    info = jnp.concatenate([(c * tl)[None], lens])
    then, now = now, names("w", 0, "b2")
    kv_all, queries, far_cot, g_in[0], out_lines = step(
        then, (kv_all, queries, far_cot, g_in[0], out_lines), now
    )
    out_full = ctx_gather(out_lines)
    attended, lse = attention(queries, kv_all, info)
    then, now = now, names("w", 0, "b3", "c3")
    attended, far_cot = step(then, (attended, far_cot), now)
    if share == 2:
        sels.append(route(far_cot))
        g_in.append(exchange(to_slots(sels[1], far_cot)))
    attended_low = attended.reshape(rows, width)
    hidden = inputs + live_rows * mm(attended_low, out_full)
    second, inverse_two = norm_forward(hidden, second_scale)
    second_low = second.astype(BF16)

    then, now = now, names("w", 0, "c2") + names("w", 1, "a2")
    (second_low,) = step(then, (second_low,), now)
    x_in = [exchange(to_slots(sels[0], second_low))]
    if share == 2:
        far = swap(second_low)
        then, now = now, names("w", 1, "a1", "b1", "c1")
        x_in[0], g_in[1], far = step(then, (x_in[0], g_in[1], far), now)
        x_in.append(exchange(to_slots(sels[1], far)))

    def expert(j):
        number_here = c * pieces + role * mine + j
        at = role * mine + j
        expert_info = jnp.stack([f, number_here // split, at])
        if merged:
            weights = [up_weight, down_weight]
            weights += [messages["w", j, chunk, k] for k in range(1, F) for chunk in range(3)]
        else:
            weights = [up_full, down_full]
        out = run_expert(j, x_in, g_in, weights, expert_info, merged)
        if merged:
            grads_out.append(out[2])
        return out

    if merged:
        then, now = now, names("w", 1, "b2", "c2")
        (x_in[1],) = step(then, (x_in[1],), now)
        outs = [expert(0)]
        then, now = now, names("w", 1, "a3", "b3", "c3")
        d_in, mixed = [outs[0][0]], [outs[0][1]]
        d_in[0], mixed[0], grads_out[0] = step(then, (d_in[0], mixed[0], grads_out[0]), now)
        d_in[0] = exchange(d_in[0])
        then, now = now, names("g", 0, "a2", "b2")
        d_in[0], mixed[0], x_in[0] = step(then, (d_in[0], mixed[0], x_in[0]), now)
        mixed[0] = exchange(mixed[0])
        outs.append(expert(1))
        then, now = now, names("g", 0, "c2", "a1")
        last, mixed[0], later, grads_out[1] = step(
            then, (outs[1][0], mixed[0], outs[1][1], grads_out[1]), now
        )
        d_in.append(exchange(last))
        mixed.append(later)
    else:
        up_full = lax.all_gather(up_weight, "fsdp", axis=1, tiled=True)
        down_full = lax.all_gather(down_weight, "fsdp", axis=1, tiled=True)
        outs = [expert(j) for j in range(mine)]
        d_in = [exchange(out[0]) for out in outs]
        mixed = [exchange(out[1]) for out in outs]

    def collect(backs):
        sums = []
        for i, sel in enumerate(sels):
            total = 0.0
            for j, back in enumerate(backs):
                total = total + mm_tn(
                    sel[:, j].reshape(C * slots, rows), back[:, i].reshape(C * slots, -1)
                )
            sums.append(total)
        return sums

    sums = collect(d_in)
    dispatch_grad = sums[0]
    if share == 2:
        then, now = now, names("g", 1, "a2")
        (far,) = step(then, (sums[1].astype(BF16),), now)
        dispatch_grad = dispatch_grad + swap(far).astype(F32)
        then, now = now, names("g", 0, "b1")
        dispatch_grad, mixed[1] = step(then, (dispatch_grad, mixed[1]), now)
        mixed[1] = exchange(mixed[1])

    upstream = cot.astype(F32)
    norm_grad, second_grads = norm_backward(hidden, inverse_two, second_scale, dispatch_grad)
    hidden_grad = upstream + norm_grad
    branch_grad = (live_rows * hidden_grad).astype(BF16)
    d_att = mm_nt(branch_grad, out_full).astype(BF16)
    then, now = now, names("g", 0, "c1", "a3")
    (d_att,) = step(then, (d_att,), now)
    query_grad, terms = attention_back(
        queries, kv_all, d_att.reshape(nseq, tl, width), lse, info, C
    )
    then, now = now, names("g", 0, "b3", "c3") + names("g", 1, "b2")
    (terms,) = step(then, (terms,), now)
    own_terms = lax.psum_scatter(terms, "ctx", scatter_dimension=0, tiled=False).astype(F32)
    own_terms = own_terms.reshape(nseq, tl, KV, 2, HD)

    def by_target(grad):
        return grad.astype(BF16).reshape(F, C, cut, -1).transpose(1, 0, 2, 3)

    def over_ctx(blocks):
        return jnp.sum(exchange(blocks).astype(F32), axis=0).astype(BF16)

    query_back = (
        rotate(query_grad.reshape(nseq, tl, H, HD), cosine, -sine)
        .astype(BF16)
        .reshape(rows, width)
    )
    projection_blocks = by_target(mm_tn(attended_low, branch_grad))
    query_blocks = by_target(mm_tn(normed_low, query_back))
    then, now = now, names("g", 1, "c2", "a1", "b1")
    own_terms, mixed, projection_blocks, query_blocks = step(
        then, (own_terms, mixed, projection_blocks, query_blocks), now
    )
    projection_rows = lax.psum_scatter(projection_blocks, "ctx", scatter_dimension=0, tiled=True)
    query_rows = over_ctx(query_blocks)
    key_back = rotate(own_terms[..., 0, :], cosine, -sine)
    kv_back = (
        jnp.stack([key_back, own_terms[..., 1, :]], axis=3).astype(BF16).reshape(rows, KV * 2 * HD)
    )
    normed_grad = mm_nt(query_back, query_full) + mm_nt(kv_back, kv_full)
    entry_grad, first_grads = norm_backward(inputs, inverse_one, first_scale, normed_grad)
    grad_tokens = hidden_grad + entry_grad
    gains_wide = jnp.pad(
        jnp.stack([first_grads, second_grads], axis=1), ((0, 0), (0, 2 * HD - 2))
    )
    kv_blocks = by_target(jnp.concatenate([mm_tn(normed_low, kv_back), gains_wide], axis=1))
    sums = collect(mixed)
    mixed_rows = sums[0]
    then, now = now, names("g", 1, "c1", "a3")
    far, query_rows, kv_blocks = step(then, (sums[-1].astype(BF16), query_rows, kv_blocks), now)
    if share == 2:
        mixed_rows = mixed_rows + swap(far).astype(F32)
    kv_rows = over_ctx(kv_blocks)
    query_rows = fsdp_scatter_sum(query_rows)
    then, now = now, []
    kv_rows, projection_rows = step(then, (kv_rows, projection_rows.reshape(F, cut, -1)), now)
    kv_rows, projection_rows = fsdp_scatter_sum(kv_rows), fsdp_scatter_sum(projection_rows)
    now = names("g", 1, "b3", "c3")
    query_rows, projection_rows, kv_rows = step([], (query_rows, projection_rows, kv_rows), now)
    wide = jnp.concatenate([query_rows, projection_rows, kv_rows], axis=1).astype(BF16)
    wide = lax.all_gather(wide, "ctx", axis=0, tiled=True).astype(F32)
    grad_query, grad_projection = wide[:, :width], wide[:, width : width + D]
    small = wide[:, width + D :]
    pair_width = 2 * KV * HD
    grad_pairs = small[:, :pair_width].reshape(Dl, KV, 2, HD)
    grad_first, grad_second = small[:, pair_width], small[:, pair_width + 1]

    block_rows = (hidden + mixed_rows[:, :D]).astype(BF16)
    router_by_expert = mixed_rows[:, D : D + EXPERTS]
    grad_router = jnp.sum(jnp.where(hit, router_by_expert[:, None, :], 0.0), axis=2)

    if merged:
        def both(k, own):
            parts = []
            for j in range(mine):
                first = grads_out[j][0] if own else jnp.stack(
                    [messages["g", j, chunk, 1] for chunk in range(3)]
                )
                other = jnp.stack([messages["g", j, chunk, k] for chunk in range(3)])
                parts.append(first.astype(F32) + other.astype(F32))
            return jnp.stack(parts).reshape(mine, -1, D)

        same, other = both(2, True), both(3, False)
        low_part = jnp.where(role == 0, same, other)
        high_part = jnp.where(role == 0, other, same)
        grad_both = jnp.concatenate([low_part, high_part], axis=0)
        grad_up, grad_down = grad_both[:, :Dl], grad_both[:, Dl:]
    else:
        grad_up, grad_down = [
            lax.psum_scatter(
                jnp.stack([out[2 + i] for out in outs]), "fsdp", scatter_dimension=1, tiled=True
            ).astype(F32)
            for i in range(2)
        ]

    shape = (batches, seqs_here, tl)
    return (
        block_rows.reshape(shape + (D,)),
        grad_tokens.reshape(shape + (D,)),
        grad_router.reshape(shape + (TOP,)),
        grad_first,
        grad_second,
        grad_query,
        grad_pairs[:, :, 0].reshape(Dl, KV * HD),
        grad_pairs[:, :, 1].reshape(Dl, KV * HD),
        grad_projection,
        grad_up,
        grad_down,
    )


def solution(mesh):
    rows = P(None, "fsdp", "ctx", None)
    weight = P("fsdp", None)
    expert = P("ctx", "fsdp", None)
    placed = (rows, P(None, "fsdp"), rows, rows, P("fsdp"), P("fsdp"))
    placed = placed + (weight,) * 4 + (expert,) * 2 + (rows,)
    outs = (rows, rows, rows, P("fsdp"), P("fsdp")) + (weight,) * 4 + (expert,) * 2
    return jax.shard_map(local, mesh=mesh, in_specs=placed, out_specs=outs, check_vma=False)
```

```python
import jax
import jax.numpy as jnp
from jax import lax
from jax.experimental import pallas as pl
from jax.experimental.pallas import tpu as pltpu
from jax.sharding import PartitionSpec as P

H = 12
KV = 2
HD = 128
TOP = 4
EXPERTS = 32
EPSILON = 1e-06
ROPE_BASE = 10000.0
NEGATIVE = -1e30
F32 = jnp.float32
BF16 = jnp.bfloat16


def angle_tables(positions):
    frequency = ROPE_BASE ** (-(jnp.arange(HD // 2, dtype=F32) * 2.0 / HD))
    angles = positions.astype(F32)[:, None] * frequency[None, :]
    cosine, sine = jnp.cos(angles), jnp.sin(angles)
    return jnp.concatenate([cosine, cosine], 1), jnp.concatenate([-sine, sine], 1)


def turn(vectors, cosine, sine):
    return vectors * cosine + pltpu.roll(vectors, HD // 2, 1) * sine


def norm_forward(values, gain_row):
    inverse = lax.rsqrt(jnp.mean(values * values, axis=-1, keepdims=True) + EPSILON)
    return values * inverse * gain_row, inverse


def norm_backward(values, inverse, gain_row, upstream):
    gain_grad = jnp.sum(upstream * values * inverse, axis=0)
    scaled = upstream * gain_row
    projected = jnp.mean(scaled * values, axis=-1, keepdims=True)
    return inverse * scaled - values * inverse**3 * projected, gain_grad


def mm(a, b):
    return jnp.dot(a, b, preferred_element_type=F32)


def mm_nt(a, b):
    return lax.dot_general(a, b, (((1,), (1,)), ((), ())), preferred_element_type=F32)


def mm_tn(a, b):
    return lax.dot_general(a, b, (((0,), (0,)), ((), ())), preferred_element_type=F32)


VMEM_LIMIT = 60 * 1024 * 1024


def stack_heads(block, groups):
    return jnp.concatenate([block[:, h * HD : (h + 1) * HD] for h in range(groups)], axis=0)


def masked_scores(stacked, keys, first, length, groups):
    tl = stacked.shape[0] // groups
    total = keys.shape[0]
    scores = mm_nt(stacked, keys) * HD ** (-0.5)
    key_at = lax.broadcasted_iota(jnp.int32, (tl, total), 1)
    query_at = lax.broadcasted_iota(jnp.int32, (tl, total), 0) + first
    allowed = (key_at <= query_at) & (key_at < length)
    scores = scores.reshape(groups, tl, total)
    return jnp.where(allowed[None], scores, NEGATIVE).reshape(groups * tl, total)


def key_value_kernel(x_ref, w_ref, cos_ref, sin_ref, out_ref):
    both = mm(x_ref[...], w_ref[...])
    cosine, sine = cos_ref[...], sin_ref[...]
    for h in range(KV):
        key = turn(both[:, 2 * h * HD : (2 * h + 1) * HD], cosine, sine)
        out_ref[0, :, 2 * h * HD : (2 * h + 1) * HD] = key.astype(BF16)
        value = both[:, (2 * h + 1) * HD : (2 * h + 2) * HD]
        out_ref[0, :, (2 * h + 1) * HD : (2 * h + 2) * HD] = value.astype(BF16)


def key_values(normed_low, qkv_full, tables, nseq):
    rows, D = normed_low.shape
    tl, wide = rows // nseq, 2 * KV * HD
    return pl.pallas_call(
        key_value_kernel,
        grid=(nseq,),
        in_specs=[
            pl.BlockSpec((tl, D), lambda s: (s, 0)),
            pl.BlockSpec((D, wide), lambda s: (0, H * HD // wide)),
            pl.BlockSpec((tl, HD), lambda s: (0, 0)),
            pl.BlockSpec((tl, HD), lambda s: (0, 0)),
        ],
        out_specs=pl.BlockSpec((1, tl, wide), lambda s: (s, 0, 0)),
        out_shape=jax.ShapeDtypeStruct((nseq, tl, wide), BF16),
        compiler_params=pltpu.CompilerParams(vmem_limit_bytes=VMEM_LIMIT),
        cost_estimate=pl.CostEstimate(
            flops=4 * rows * D * wide, bytes_accessed=2 * D * wide, transcendentals=0
        ),
    )(normed_low, qkv_full, *tables)


def attend_kernel(groups, info, q_ref, kv_ref, cos_ref, sin_ref, att_ref, lse_ref, turned_ref):
    tl = q_ref.shape[1]
    cosine, sine = cos_ref[...], sin_ref[...]
    for h in range(groups):
        at = slice(h * HD, (h + 1) * HD)
        turned_ref[0, :, at] = turn(q_ref[0, :, at], cosine, sine).astype(BF16)
    stacked = stack_heads(turned_ref[0], groups)
    scores = masked_scores(
        stacked, kv_ref[0, :, :HD], info[0], info[1 + pl.program_id(0)], groups
    )
    top = jnp.max(scores, axis=-1, keepdims=True)
    shares = jnp.exp(scores - top)
    total = jnp.sum(shares, axis=-1, keepdims=True)
    out = mm(shares.astype(BF16), kv_ref[0, :, HD:]) / total
    lse = top + jnp.log(total)
    for h in range(groups):
        at = slice(h * tl, (h + 1) * tl)
        att_ref[0, :, h * HD : (h + 1) * HD] = out[at].astype(BF16)
        lse_ref[0, 0, :, h : h + 1] = lse[at]


def attend_back_kernel(
    groups, info, q_ref, kv_ref, da_ref, lse_ref, cos_ref, sin_ref, dq_ref, dkv_ref
):
    tl = q_ref.shape[1]
    keys, values = kv_ref[0, :, :HD], kv_ref[0, :, HD:]
    stacked = stack_heads(q_ref[0], groups)
    scores = masked_scores(stacked, keys, info[0], info[1 + pl.program_id(0)], groups)
    lse = jnp.concatenate([lse_ref[0, 0, :, h : h + 1] for h in range(groups)], axis=0)
    probs = jnp.exp(scores - lse)
    grads = stack_heads(da_ref[0], groups)
    d_probs = mm_nt(grads, values)
    delta = jnp.sum(probs * d_probs, axis=-1, keepdims=True)
    d_scores = (probs * (d_probs - delta)).astype(BF16)
    dq = mm(d_scores, keys) * HD ** (-0.5)
    here = pl.ds(pl.multiple_of(info[0], 8), tl)
    cosine, sine = cos_ref[here, :], -sin_ref[here, :]
    for h in range(groups):
        turned = turn(dq[h * tl : (h + 1) * tl], cosine, sine)
        dq_ref[0, :, h * HD : (h + 1) * HD] = turned.astype(BF16)
    dk = mm_tn(d_scores, stacked) * HD ** (-0.5)
    dk = turn(dk, cos_ref[...], -sin_ref[...])
    dv = mm_tn(probs.astype(BF16), grads)
    shape = dkv_ref.shape[:1] + (tl, HD)
    dkv_ref[:, 0, :, :HD] = dk.reshape(shape).astype(BF16)
    dkv_ref[:, 0, :, HD:] = dv.reshape(shape).astype(BF16)


def attention(queries, kv_all, info, tables):
    nseq, tl, width = queries.shape
    total = kv_all.shape[1]
    groups = H // KV
    return pl.pallas_call(
        lambda *refs: attend_kernel(groups, *refs),
        grid_spec=pltpu.PrefetchScalarGridSpec(
            num_scalar_prefetch=1,
            grid=(nseq, KV),
            in_specs=[
                pl.BlockSpec((1, tl, groups * HD), lambda s, n, info: (s, 0, n)),
                pl.BlockSpec((1, total, 2 * HD), lambda s, n, info: (s, 0, n)),
                pl.BlockSpec((tl, HD), lambda s, n, info: (0, 0)),
                pl.BlockSpec((tl, HD), lambda s, n, info: (0, 0)),
            ],
            out_specs=[
                pl.BlockSpec((1, tl, groups * HD), lambda s, n, info: (s, 0, n)),
                pl.BlockSpec((1, 1, tl, HD), lambda s, n, info: (s, n, 0, 0)),
                pl.BlockSpec((1, tl, groups * HD), lambda s, n, info: (s, 0, n)),
            ],
        ),
        out_shape=[
            jax.ShapeDtypeStruct((nseq, tl, width), BF16),
            jax.ShapeDtypeStruct((nseq, KV, tl, HD), F32),
            jax.ShapeDtypeStruct((nseq, tl, width), BF16),
        ],
        compiler_params=pltpu.CompilerParams(vmem_limit_bytes=VMEM_LIMIT),
        cost_estimate=pl.CostEstimate(
            flops=28 * nseq * tl * width * total,
            bytes_accessed=4 * queries.size * 2 + 2 * kv_all.size,
            transcendentals=nseq * H * tl * total,
        ),
    )(info, queries, kv_all, *tables)


def attention_back(queries, kv_all, d_att, lse, info, tables, ctx_count):
    nseq, tl, width = queries.shape
    total = kv_all.shape[1]
    groups = H // KV
    return pl.pallas_call(
        lambda *refs: attend_back_kernel(groups, *refs),
        grid_spec=pltpu.PrefetchScalarGridSpec(
            num_scalar_prefetch=1,
            grid=(nseq, KV),
            in_specs=[
                pl.BlockSpec((1, tl, groups * HD), lambda s, n, info: (s, 0, n)),
                pl.BlockSpec((1, total, 2 * HD), lambda s, n, info: (s, 0, n)),
                pl.BlockSpec((1, tl, groups * HD), lambda s, n, info: (s, 0, n)),
                pl.BlockSpec((1, 1, tl, HD), lambda s, n, info: (s, n, 0, 0)),
                pl.BlockSpec((total, HD), lambda s, n, info: (0, 0)),
                pl.BlockSpec((total, HD), lambda s, n, info: (0, 0)),
            ],
            out_specs=[
                pl.BlockSpec((1, tl, groups * HD), lambda s, n, info: (s, 0, n)),
                pl.BlockSpec((ctx_count, 1, tl, 2 * HD), lambda s, n, info: (0, s, 0, n)),
            ],
        ),
        out_shape=[
            jax.ShapeDtypeStruct((nseq, tl, width), BF16),
            jax.ShapeDtypeStruct((ctx_count, nseq, tl, KV * 2 * HD), BF16),
        ],
        compiler_params=pltpu.CompilerParams(vmem_limit_bytes=VMEM_LIMIT),
        cost_estimate=pl.CostEstimate(
            flops=36 * nseq * tl * width * total,
            bytes_accessed=6 * queries.size * 2 + 4 * kv_all.size,
            transcendentals=nseq * H * tl * total,
        ),
    )(info, queries, kv_all, d_att, lse, *tables)


def expert_kernel(sides, w_mode, g_mode, *refs):
    info = refs[0]
    ins = refs[1 : 1 + sides]
    count = MODE_REFS[w_mode]
    weights = refs[1 + sides : 1 + sides + count]
    at = 1 + sides + count
    din_ref, wy_ref = refs[at : at + 2]
    at = at + 2
    out_refs = refs[at : at + GRAD_REFS[g_mode]]
    at = at + GRAD_REFS[g_mode]
    up, down, x_t, act_t, dgu, dy, act_s, pre, wide, gup, gdn, sems = refs[at:]
    step, steps = pl.program_id(0), pl.num_programs(0)
    D, W = up.shape[0], down.shape[0]
    tile = wide.shape[0]
    tw = 256 if W % 256 == 0 else 128
    td = 256

    wl = W // 4
    dl = 2 * wl

    def shard(up_side, down_side, source, block, first=0):
        pairs, count = [], block.shape[0]
        ups = min(count, dl - first)
        if ups > 0:
            at = pl.ds(pl.multiple_of(source * dl + first, 16), ups)
            pairs.append((up_side.at[at], block.at[pl.ds(0, ups)]))
        if ups < count:
            skip = max(0, ups)
            at = pl.ds(pl.multiple_of(source * wl + first + skip - dl, 16), count - skip)
            pairs.append((down_side.at[at], block.at[pl.ds(skip, count - skip)]))
        return pairs

    def by_distance(up_side, down_side, blocks, sign):
        pairs = []
        for block, k, first in zip(blocks, (1, 2, 2, 2, 3), (0, 0, wl, 2 * wl, 0)):
            source = lax.rem(info[0] + 4 + sign * k, 4)
            pairs += shard(up_side, down_side, source, block, first)
        return pairs

    def copies_of(pairs):
        return [pltpu.make_async_copy(a, b, sems.at[i]) for i, (a, b) in enumerate(pairs)]

    def loads():
        if w_mode == "whole":
            return copies_of([(weights[0].at[info[2]], up), (weights[1].at[info[2]], down)])
        pairs = by_distance(up, down, weights[2:], -1)
        own_up = up.at[pl.ds(pl.multiple_of(info[0] * dl, 16), dl)]
        own_down = down.at[pl.ds(pl.multiple_of(info[0] * wl, 16), wl)]
        pairs += [(own_up, weights[0].at[info[2]]), (own_down, weights[1].at[info[2]])]
        return copies_of([(b, a) for a, b in pairs])

    def put(ref, columns, block):
        per = tile // sides
        shape = (ref.shape[0], ref.shape[2], block.shape[1])
        for i in range(sides):
            ref[:, i, :, columns] = block[i * per : (i + 1) * per].reshape(shape)

    @pl.when(step == 0)
    def _():
        copies = loads()
        for copy in copies:
            copy.start()
        for copy in copies:
            copy.wait()

    rows = pl.ds(pl.multiple_of(step * tile, 128), tile)
    x = jnp.concatenate([r[:, :, :, :D].reshape(-1, D) for r in ins], axis=0)
    g_aug = jnp.concatenate([r[:, :, :, D:].reshape(-1, D + HD) for r in ins], axis=0)
    x_t[:, rows] = x.T
    lane = lax.broadcasted_iota(jnp.int32, (tile, HD), 1)
    picked = (lane == info[1]) | (lane == info[1] + HD // 2)
    w = jnp.sum(jnp.where(picked, g_aug[:, D:].astype(F32), 0.0), axis=1, keepdims=True)
    wide[...] = g_aug[:, :D]
    dy[rows, :] = (g_aug[:, :D].astype(F32) * w).astype(BF16)

    @pl.loop(0, W // tw)
    def _(t):
        a = pl.ds(pl.multiple_of(t * tw, 128), tw)
        b = pl.ds(pl.multiple_of(W + t * tw, 128), tw)
        gate = mm(x, up[:, a])
        lift = mm(x, up[:, b])
        pre[:, a] = gate
        pre[:, b] = lift
        act = gate / (1.0 + jnp.exp(-gate)) * lift
        act = act.astype(BF16)
        act_s[:, a] = act
        act_t[a, rows] = act.T

    def out_step(t, total):
        a = pl.ds(pl.multiple_of(t * td, 128), td)
        y = mm(act_s[...], down[:, a])
        put(wy_ref, a, (y * w).astype(BF16))
        return total + jnp.sum(y * wide[:, a].astype(F32), axis=1, keepdims=True)

    router = lax.fori_loop(0, D // td, out_step, jnp.zeros((tile, 1), F32))
    extra = jnp.where(lane == info[1], router, 0.0).astype(BF16)
    put(wy_ref, pl.ds(D, HD), extra)

    @pl.loop(0, W // tw)
    def _(t):
        a = pl.ds(pl.multiple_of(t * tw, 128), tw)
        b = pl.ds(pl.multiple_of(W + t * tw, 128), tw)
        d_act = mm_nt(dy[rows, :], down[a, :])
        gate, lift = pre[:, a], pre[:, b]
        sig = 1.0 / (1.0 + jnp.exp(-gate))
        dgu[rows, a] = (d_act * lift * sig * (1.0 + gate * (1.0 - sig))).astype(BF16)
        dgu[rows, b] = (d_act * gate * sig).astype(BF16)

    @pl.loop(0, D // td)
    def _(t):
        a = pl.ds(pl.multiple_of(t * td, 128), td)
        put(din_ref, a, mm_nt(dgu[rows, :], up[a, :]).astype(BF16))

    @pl.when(step == steps - 1)
    def _():
        @pl.loop(0, D // td)
        def _(t):
            a = pl.ds(pl.multiple_of(t * td, 128), td)
            gup[a, :] = mm(x_t[a, :], dgu[...]).astype(BF16)

        @pl.loop(0, W // tw)
        def _(t):
            a = pl.ds(pl.multiple_of(t * tw, 128), tw)
            gdn[a, :] = mm(act_t[a, :], dy[...]).astype(BF16)

        if g_mode == "whole":
            pairs = [(gup, out_refs[0]), (gdn, out_refs[1])]
        else:
            pairs = shard(gup, gdn, info[0], out_refs[0])
            pairs += by_distance(gup, gdn, out_refs[1:], 1)
        copies = copies_of(pairs)
        for copy in copies:
            copy.start()
        for copy in copies:
            copy.wait()


def weight_grad_kernel(
    planes, att_ref, db_ref, x_ref, dq_ref, all_ref, pair_ref, out_ref, total, grads, sems
):
    step = pl.program_id(0)
    D, width = x_ref.shape[1], dq_ref.shape[1]
    td = 256

    @pl.when(step == 0)
    def _():
        total[...] = jnp.zeros_like(total)

        @pl.loop(0, D // td)
        def _(t):
            a = pl.ds(pl.multiple_of(t * td, 128), td)
            grads[a, :D] = mm_tn(att_ref[:, a], db_ref[...]).astype(BF16)
            grads[a, D : D + width] = mm_tn(x_ref[:, a], dq_ref[...]).astype(BF16)

    total[...] += mm_tn(pair_ref[...], all_ref[...])

    @pl.when(step == pl.num_programs(0) - 1)
    def _():
        @pl.loop(0, D // td)
        def _(t):
            a = pl.ds(pl.multiple_of(t * td, 128), td)
            grads[a, D + width :] = total[:, a].T.astype(BF16)

        ctx = sems.shape[0] // planes
        cut = D // (planes * ctx)
        copies = []
        for f in range(planes):
            for c in range(ctx):
                source = grads.at[pl.ds((f * ctx + c) * cut, cut)]
                target = out_ref.at[pl.ds((c * planes + f) * cut, cut)]
                copies.append(pltpu.make_async_copy(source, target, sems.at[len(copies)]))
        for copy in copies:
            copy.start()
        for copy in copies:
            copy.wait()


def weight_grads(att, db, x, dq, every_x, pairs, ctx_count, planes):
    rows, D = x.shape
    width, wide = dq.shape[1], pairs.shape[1]
    return pl.pallas_call(
        lambda *refs: weight_grad_kernel(planes, *refs),
        grid=(ctx_count,),
        in_specs=[
            pl.BlockSpec((rows, D), lambda i: (0, 0)),
            pl.BlockSpec((rows, D), lambda i: (0, 0)),
            pl.BlockSpec((rows, D), lambda i: (0, 0)),
            pl.BlockSpec((rows, width), lambda i: (0, 0)),
            pl.BlockSpec((rows, D), lambda i: (i, 0)),
            pl.BlockSpec((rows, wide), lambda i: (i, 0)),
        ],
        out_specs=pl.BlockSpec(memory_space=pl.ANY),
        out_shape=jax.ShapeDtypeStruct((D, D + width + wide), BF16),
        scratch_shapes=[
            pltpu.VMEM((wide, D), F32),
            pltpu.VMEM((D, D + width + wide), BF16),
            pltpu.SemaphoreType.DMA((planes * ctx_count,)),
        ],
        compiler_params=pltpu.CompilerParams(vmem_limit_bytes=VMEM_LIMIT),
        cost_estimate=pl.CostEstimate(
            flops=4 * rows * D * (D + width + ctx_count * wide),
            bytes_accessed=2 * ctx_count * rows * D,
            transcendentals=0,
        ),
    )(att, db, x, dq, every_x, pairs)


def blank(shapes):
    return pl.pallas_call(
        lambda *refs: None,
        out_specs=[pl.BlockSpec(memory_space=pl.ANY)] * len(shapes),
        out_shape=[jax.ShapeDtypeStruct(shape, F32) for shape in shapes],
    )()


MODE_REFS = {"whole": 2, "parts": 7}
GRAD_REFS = {"whole": 2, "parts": 6}


def run_expert(piece, W, ins, weights, info, w_mode, g_mode):
    C, mine, slots, wide = ins[0].shape
    D = (wide - HD) // 2
    sides = len(ins)
    per_step = C
    while per_step > 1 and (per_step * sides * slots > 640 or C % per_step):
        per_step -= 1
    tile = per_step * sides * slots
    rows = C * sides * slots

    def spec(width, at):
        return pl.BlockSpec((per_step, 1, slots, width), lambda i, info: (i, at, 0, 0))

    def out_spec(width):
        return pl.BlockSpec((per_step, sides, slots, width), lambda i, info: (i, 0, 0, 0))

    any_spec = pl.BlockSpec(memory_space=pl.ANY)
    if g_mode == "whole":
        grads = [(D, 2 * W), (W, D)]
    else:
        grads = [(n * W // 4, D) for n in (3, 3, 1, 1, 1, 3)]
    grads = [jax.ShapeDtypeStruct(shape, BF16) for shape in grads]
    return pl.pallas_call(
        lambda *refs: expert_kernel(sides, w_mode, g_mode, *refs),
        grid_spec=pltpu.PrefetchScalarGridSpec(
            num_scalar_prefetch=1,
            grid=(C // per_step,),
            in_specs=[spec(wide, piece)] * sides
            + [any_spec] * len(weights),
            out_specs=[out_spec(D), out_spec(D + HD)] + [any_spec] * len(grads),
            scratch_shapes=[
                pltpu.VMEM((D, 2 * W), BF16),
                pltpu.VMEM((W, D), BF16),
                pltpu.VMEM((D, rows), BF16),
                pltpu.VMEM((W, rows), BF16),
                pltpu.VMEM((rows, 2 * W), BF16),
                pltpu.VMEM((rows, D), BF16),
                pltpu.VMEM((tile, W), BF16),
                pltpu.VMEM((tile, 2 * W), F32),
                pltpu.VMEM((tile, D), BF16),
                pltpu.VMEM((D, 2 * W), BF16),
                pltpu.VMEM((W, D), BF16),
                pltpu.SemaphoreType.DMA((12,)),
            ],
        ),
        out_shape=[jax.ShapeDtypeStruct((C, sides, slots, n), BF16) for n in (D, D + HD)]
        + grads,
        compiler_params=pltpu.CompilerParams(vmem_limit_bytes=VMEM_LIMIT),
        cost_estimate=pl.CostEstimate(
            flops=38 * rows * D * W,
            bytes_accessed=8 * rows * D + 24 * D * W,
            transcendentals=2 * rows * W,
        ),
    )(info, *ins, *weights)


def local(
    tokens,
    lengths,
    expert_picks,
    router_weights,
    first_gain,
    second_gain,
    query_weight,
    key_weight,
    value_weight,
    output_weight,
    up_weight,
    down_weight,
    cotangent,
):
    batches, seqs_here, tl, D = tokens.shape
    C = lax.axis_size("ctx")
    F = lax.axis_size("fsdp")
    c = lax.axis_index("ctx")
    f = lax.axis_index("fsdp")
    split = max(1, C // EXPERTS)
    pieces = up_weight.shape[0]
    W = up_weight.shape[2] // 2
    merged = pieces % 2 == 0 and F == 4 and 2 * W == D
    share = 2 if merged else 1
    mine = pieces // share
    role = f % share
    nseq = batches * seqs_here
    cap = max(2, (5 * tl * TOP + 4 * EXPERTS - 1) // (4 * EXPERTS))
    while nseq * cap % 16:
        cap += 1
    slots = nseq * cap
    rows = nseq * tl
    L = C * tl
    width = H * HD
    Dl = query_weight.shape[0]
    cut = Dl // C

    positions = c * tl + jnp.arange(tl, dtype=jnp.int32)
    tables = angle_tables(positions)
    all_tables = angle_tables(jnp.arange(L, dtype=jnp.int32))
    lens = lengths.reshape(nseq)
    live = (positions[None, :] < lens[:, None]).reshape(rows)
    live_rows = live.astype(F32)[:, None]

    def gate(*values):
        return lax.optimization_barrier(values)

    def shift(block, k):
        return lax.ppermute(block, "fsdp", [(i, (i + k) % F) for i in range(F)])

    def fsdp_gather(block):
        got = [shift(block, k) for k in range(F - 1, 0, -1)]
        ring = jnp.stack(got + [block] + got)
        return lax.dynamic_slice_in_dim(ring, F - 1 - f, F, 0)

    def fsdp_scatter_sum(parts):
        total = lax.dynamic_index_in_dim(parts, f, 0, keepdims=False).astype(F32)
        for k in range(1, F):
            block = lax.dynamic_index_in_dim(parts, (f + k) % F, 0, keepdims=False)
            total = total + shift(block, k).astype(F32)
        return total

    def swap(block):
        return lax.ppermute(block, "fsdp", [(i, i ^ 1) for i in range(F)])

    def exchange(blocks):
        return lax.all_to_all(blocks, "ctx", 0, 0, tiled=True)

    def ctx_gather(lines):
        return lax.all_gather(lines, "ctx", axis=1, tiled=True).reshape(D, -1)

    def part_of(weight):
        return lax.dynamic_slice_in_dim(weight, c * cut, cut, 0)

    key_part, value_part = part_of(key_weight), part_of(value_weight)
    qkv_part = [part_of(query_weight)]
    for h in range(KV):
        qkv_part += [part[:, h * HD : (h + 1) * HD] for part in (key_part, value_part)]
    qkv_part = jnp.concatenate(qkv_part, axis=1)
    out_part, gain_parts = part_of(output_weight), jnp.stack([first_gain, second_gain])
    qkv_lines = fsdp_gather(qkv_part)

    messages, operands = {}, {}
    expert_in = [up_weight, down_weight]

    def shard_of(at):
        return jnp.concatenate(
            [lax.dynamic_index_in_dim(x, at, 0, keepdims=False) for x in expert_in]
        )

    def operand(name):
        if name in operands:
            return operands[name]
        j = "wv".index(name[0])
        block = shard_of((role if name[1] == "2" else 1 - role) * mine + j)
        third = block.shape[0] // 3
        at = "abc".find(name[2:]) * third if name[2:] else 0
        return block[at : at + third] if name[2:] else block

    def send(name, block):
        return shift(block, int(name[1]))

    def step(need, values, go):
        if not merged:
            return lax.optimization_barrier(values)
        fresh = tuple(operand(name) for name in go)
        got, values, fresh = lax.optimization_barrier(
            (tuple(messages[name] for name in need), values, fresh)
        )
        messages.update(zip(need, got))
        messages.update((name, send(name, block)) for name, block in zip(go, fresh))
        return values

    picks = expert_picks.reshape(rows, TOP)
    gates = router_weights.reshape(rows, TOP)
    cot = cotangent.reshape(rows, D)
    expert_ids = jnp.arange(EXPERTS, dtype=jnp.int32)
    hit = picks[:, :, None] == expert_ids
    by_expert = jnp.sum(jnp.where(hit, gates[:, :, None], 0.0), axis=1) * live_rows
    high = by_expert.astype(BF16)
    low = (by_expert - high.astype(F32)).astype(BF16)
    gap = jnp.zeros((rows, HD // 2 - EXPERTS), BF16)
    table = jnp.concatenate([high, gap, low, gap], axis=1)
    number = jnp.arange(C)[:, None] * pieces + role * mine + jnp.arange(mine)[None, :]
    expert_of = (number // split).reshape(C * mine)
    earlier = jnp.tril(jnp.ones((tl, tl), BF16), -1)
    pick_map = (expert_ids[:, None] == expert_of[None, :]).astype(BF16)

    def route(table):
        match = table[:, :EXPERTS] > 0
        ranks = jnp.einsum(
            "ab,sbe->sae",
            earlier,
            match.astype(BF16).reshape(nseq, tl, -1),
            preferred_element_type=F32,
        )
        base = (jnp.arange(nseq) * cap)[:, None, None]
        code = jnp.where(match, (ranks + base).reshape(rows, -1), -1.0).astype(BF16)
        code = mm_tn(pick_map, code.T)
        chosen = code[:, None, :] == jnp.arange(slots, dtype=F32)[None, :, None]
        return chosen.astype(BF16).reshape(C, mine, slots, rows)

    def to_slots(sel, source):
        out = mm(sel.reshape(C * mine * slots, rows), source)
        return out.astype(BF16).reshape(C, mine, slots, -1)

    inputs = tokens.reshape(rows, D).astype(F32)
    step([], (qkv_part,), ["w1"])
    _, gain_parts, table, cot, out_part = gate(qkv_lines, gain_parts, table, cot, out_part)
    gains, out_lines = fsdp_gather(gain_parts), fsdp_gather(out_part)
    sels = [route(table)]
    qkv_full, sels[0], table, out_lines, cot_wide, all_tables = step(
        ["w1"],
        (
            ctx_gather(qkv_lines),
            sels[0],
            table,
            out_lines,
            jnp.concatenate([cot, table], axis=1),
            all_tables,
        ),
        ["w3"],
    )
    first_scale = gains[:, 0].reshape(D).astype(F32)
    second_scale = gains[:, 1].reshape(D).astype(F32)
    normed, inverse_one = norm_forward(inputs, first_scale)
    normed_low = normed.astype(BF16)
    kv_low = key_values(normed_low, qkv_full, tables, nseq)
    kv_all = lax.all_gather(kv_low, "ctx", axis=1, tiled=True)
    _, expert_in, qkv_full, table = gate(kv_low, expert_in, qkv_full, table)
    query_pre = mm(normed_low, qkv_full[:, :width]).reshape(nseq, tl, width)
    info = jnp.concatenate([(c * tl)[None], lens])
    kv_all, query_pre, out_lines, table = step(
        ["w3"], (kv_all, query_pre, out_lines, table), ["w2a"]
    )
    far_table = swap(table) if share == 2 else table
    out_full = ctx_gather(out_lines)
    attended, lse, queries = attention(query_pre, kv_all, info, tables)
    attended, cot_wide, far_table = step(["w2a"], (attended, cot_wide, far_table), [])
    attended_low = attended.reshape(rows, width)
    hidden = inputs + live_rows * mm(attended_low, out_full)
    second, inverse_two = norm_forward(hidden, second_scale)
    second_low = second.astype(BF16)

    second_low, cot_wide = step([], (second_low, cot_wide), ["w2b", "w2c"])
    expert_rows = [exchange(to_slots(sels[0], jnp.concatenate([second_low, cot_wide], axis=1)))]
    shards = None
    if merged:
        far, far_cot = swap(second_low), swap(cot_wide[:, :D])
        sels.append(route(far_table))
        shards = list(blank([(pieces, Dl, 2 * W), (pieces, W // F, D)]))
        far, far_cot, expert_rows[0], sels[1], shards = step(
            ["w2b", "w2c"], (far, far_cot, expert_rows[0], sels[1], shards), ["v1", "v3", "v2a"]
        )
        far_rows = jnp.concatenate([far, far_cot, far_table], axis=1)
        expert_rows.append(exchange(to_slots(sels[1], far_rows)))

    def expert(j):
        at = role * mine + j
        expert_info = jnp.stack([f, (c * pieces + at) // split, at])
        if not merged:
            return run_expert(j, W, expert_rows, [up_full, down_full], expert_info, "whole", "whole")
        names = ["wv"[j] + k for k in ("1", "2a", "2b", "2c", "3")]
        weights = [up_weight, down_weight] + [messages[name] for name in names]
        out = run_expert(j, W, expert_rows, weights, expert_info, "parts", "parts")
        for k, grad in zip(("0", "1", "2a", "2b", "2c", "3"), out[2:]):
            operands["pq"[j] + k] = grad
        return out

    if merged:
        expert_rows[1], normed_mine = step(
            ["v1", "v3", "v2a"], (expert_rows[1], normed_low), ["v2b", "v2c"]
        )
        every_normed = lax.all_gather(normed_mine, "ctx", axis=0, tiled=True)
        outs = [expert(0)]
        d_in, mixed = [outs[0][0]], [outs[0][1]]
        d_in[0], expert_rows[0], mixed[0] = step(
            ["v2b", "v2c"], (d_in[0], expert_rows[0], mixed[0]), ["p1", "p2a"]
        )
        d_in[0] = exchange(d_in[0])
        outs.append(expert(1))
        last, d_in[0], later, every_normed = step(
            ["p1", "p2a"], (outs[1][0], d_in[0], outs[1][1], every_normed), ["p3"]
        )
        d_in.append(exchange(last))
        mixed.append(later)
    else:
        up_full = lax.all_gather(up_weight, "fsdp", axis=1, tiled=True)
        down_full = lax.all_gather(down_weight, "fsdp", axis=1, tiled=True)
        outs = [expert(j) for j in range(mine)]
        d_in = [exchange(out[0]) for out in outs]
        mixed = [exchange(out[1]) for out in outs]

    def collect(backs):
        sums = []
        for i, sel in enumerate(sels):
            total = 0.0
            for j, back in enumerate(backs):
                total = total + mm_tn(
                    sel[:, j].reshape(C * slots, rows), back[:, i].reshape(C * slots, -1)
                )
            sums.append(total)
        return sums

    def fill(at, total):
        for i, block in enumerate((total[:Dl], total[Dl:])):
            shards[i] = lax.dynamic_update_slice(shards[i], block[None], (at, 0, 0))

    def pair_sum(first, *others):
        far = jnp.concatenate([messages[name] for name in others])
        return first.astype(F32) + far.astype(F32)

    sums = collect(d_in)
    dispatch_grad = sums[0]
    if share == 2:
        far, mixed[0] = step(["p3"], (sums[1].astype(BF16), mixed[0]), ["p2b"])
        dispatch_grad = dispatch_grad + swap(far).astype(F32)
        mixed[0] = exchange(mixed[0])
        dispatch_grad, mixed[0], mixed[1] = step(["p2b"], (dispatch_grad, mixed[0], mixed[1]), [])
        mixed[1] = exchange(mixed[1])

    upstream = cot.astype(F32)
    norm_grad, second_grads = norm_backward(hidden, inverse_two, second_scale, dispatch_grad)
    hidden_grad = upstream + norm_grad
    branch_grad = (live_rows * hidden_grad).astype(BF16)
    def by_target(grad):
        return grad.astype(BF16).reshape(F, C, cut, -1).transpose(1, 0, 2, 3)

    def over_ctx(blocks):
        return jnp.sum(exchange(blocks).astype(F32), axis=0).astype(BF16)

    def scatter(blocks):
        (blocks,) = gate(blocks.reshape(D, -1))
        total = lax.psum_scatter(blocks, "ctx", scatter_dimension=0, tiled=True)
        return gate(total)[0].reshape(F, cut, -1)

    d_att = mm_nt(branch_grad, out_full).astype(BF16)
    (d_att,) = step([], (d_att,), ["p2c"])
    query_back, terms = attention_back(
        queries, kv_all, d_att.reshape(nseq, tl, width), lse, info, all_tables, C
    )
    query_back = query_back.reshape(rows, width)
    terms, query_back, mixed[-1] = step(["p2c"], (terms, query_back, mixed[-1]), ["q2a"])
    if merged:
        own_terms = over_ctx(terms)
        flat_terms = terms.reshape(C * rows, -1)
        blocks = weight_grads(
            attended_low, branch_grad, normed_low, query_back, every_normed, flat_terms, C, F
        )
        blocks, mixed = step(["q2a"], (blocks, mixed), ["q2b", "q2c"])
        mixed_sums = collect(mixed)
        mixed_rows = mixed_sums[0] + swap(mixed_sums[1].astype(BF16)).astype(F32)
        fill(role * mine, pair_sum(operands["p0"], "p2a", "p2b", "p2c"))
        fill((1 - role) * mine, pair_sum(messages["p1"], "p3"))
        own_terms, shards, mixed_rows = step(
            ["q2b", "q2c"], (own_terms, shards, mixed_rows), ["q1"]
        )
        fill(role * mine + 1, pair_sum(operands["q0"], "q2a", "q2b", "q2c"))
    else:
        own_terms = over_ctx(terms)
        pair_grad = mm_tn(normed_low, own_terms.reshape(rows, 2 * KV * HD))
        query_grad = mm_tn(normed_low, query_back)
        projection_grad = mm_tn(attended_low, branch_grad)
        blocks = by_target(jnp.concatenate([projection_grad, query_grad, pair_grad], axis=1))
        mixed_rows = collect(mixed)[0]
    weight_rows = scatter(blocks)
    kv_back = own_terms.reshape(rows, 2 * KV * HD)
    normed_grad = mm_nt(query_back, qkv_full[:, :width]) + mm_nt(kv_back, qkv_full[:, width:])
    entry_grad, first_grads = norm_backward(inputs, inverse_one, first_scale, normed_grad)
    grad_tokens = hidden_grad + entry_grad
    gain_columns = jnp.stack([first_grads, second_grads]).reshape(2, F, Dl).transpose(1, 0, 2)
    gain_columns = gain_columns.reshape(F, cut, -1)
    gain_count = gain_columns.shape[2]
    gain_columns = jnp.pad(gain_columns, ((0, 0), (0, 0), (0, -gain_count % HD)))
    weight_rows, gain_columns, shards = step(["q1"], (weight_rows, gain_columns, shards), [])
    wide = jnp.concatenate([weight_rows, gain_columns.astype(BF16)], axis=2)
    wide = fsdp_scatter_sum(wide).astype(BF16)
    wide, shards = step([], (wide, shards), ["q3"])
    wide = lax.all_gather(wide, "ctx", axis=0, tiled=False)
    whole = wide[:, :, : D + width + 2 * KV * HD].reshape(Dl, -1).astype(F32)
    grad_projection, grad_query = whole[:, :D], whole[:, D : D + width]
    grad_pairs = whole[:, D + width :].reshape(Dl, KV, 2, HD)
    gain_at = D + width + 2 * KV * HD
    gain_sums = jnp.sum(wide[:, :, gain_at : gain_at + gain_count].astype(F32), axis=0)
    grad_first, grad_second = gain_sums.reshape(2, Dl)

    block_rows = (hidden + mixed_rows[:, :D]).astype(BF16)
    router_by_expert = mixed_rows[:, D : D + EXPERTS]
    grad_router = jnp.sum(jnp.where(hit, router_by_expert[:, None, :], 0.0), axis=2)

    if merged:
        fill((1 - role) * mine + 1, pair_sum(messages["q1"], "q3"))
        grad_up, grad_down = shards
    else:
        grad_up, grad_down = [
            lax.psum_scatter(
                jnp.stack([out[2 + i] for out in outs]), "fsdp", scatter_dimension=1, tiled=True
            ).astype(F32)
            for i in range(2)
        ]

    shape = (batches, seqs_here, tl)
    return (
        block_rows.reshape(shape + (D,)),
        grad_tokens.reshape(shape + (D,)),
        grad_router.reshape(shape + (TOP,)),
        grad_first,
        grad_second,
        grad_query,
        grad_pairs[:, :, 0].reshape(Dl, KV * HD),
        grad_pairs[:, :, 1].reshape(Dl, KV * HD),
        grad_projection,
        grad_up,
        grad_down,
    )


def solution(mesh):
    rows = P(None, "fsdp", "ctx", None)
    weight = P("fsdp", None)
    expert = P("ctx", "fsdp", None)
    placed = (rows, P(None, "fsdp"), rows, rows, P("fsdp"), P("fsdp"))
    placed = placed + (weight,) * 4 + (expert,) * 2 + (rows,)
    outs = (rows, rows, rows, P("fsdp"), P("fsdp")) + (weight,) * 4 + (expert,) * 2
    return jax.shard_map(local, mesh=mesh, in_specs=placed, out_specs=outs, check_vma=False)
```

```python
import jax
import jax.numpy as jnp
from jax import lax
from jax.experimental import pallas as pl
from jax.experimental.pallas import tpu as pltpu
from jax.sharding import PartitionSpec as P

H = 12
KV = 2
HD = 128
TOP = 4
EXPERTS = 32
EPSILON = 1e-06
ROPE_BASE = 10000.0
NEGATIVE = -1e30
F32 = jnp.float32
BF16 = jnp.bfloat16


def angle_tables(positions):
    frequency = ROPE_BASE ** (-(jnp.arange(HD // 2, dtype=F32) * 2.0 / HD))
    angles = positions.astype(F32)[:, None] * frequency[None, :]
    cosine, sine = jnp.cos(angles), jnp.sin(angles)
    return jnp.concatenate([cosine, cosine], 1), jnp.concatenate([-sine, sine], 1)


def turn(vectors, cosine, sine):
    return vectors * cosine + pltpu.roll(vectors, HD // 2, 1) * sine


def norm_forward(values, gain_row):
    inverse = lax.rsqrt(jnp.mean(values * values, axis=-1, keepdims=True) + EPSILON)
    return values * inverse * gain_row, inverse


def norm_backward(values, inverse, gain_row, upstream):
    gain_grad = jnp.sum(upstream * values * inverse, axis=0)
    scaled = upstream * gain_row
    projected = jnp.mean(scaled * values, axis=-1, keepdims=True)
    return inverse * scaled - values * inverse**3 * projected, gain_grad


def mm(a, b):
    return jnp.dot(a, b, preferred_element_type=F32)


def mm_nt(a, b):
    return lax.dot_general(a, b, (((1,), (1,)), ((), ())), preferred_element_type=F32)


def mm_tn(a, b):
    return lax.dot_general(a, b, (((0,), (0,)), ((), ())), preferred_element_type=F32)


VMEM_LIMIT = 60 * 1024 * 1024


def stack_heads(block, groups):
    return jnp.concatenate([block[:, h * HD : (h + 1) * HD] for h in range(groups)], axis=0)


def masked_scores(stacked, keys, first, length, groups):
    tl = stacked.shape[0] // groups
    total = keys.shape[0]
    scores = mm_nt(stacked, keys) * HD ** (-0.5)
    key_at = lax.broadcasted_iota(jnp.int32, (tl, total), 1)
    query_at = lax.broadcasted_iota(jnp.int32, (tl, total), 0) + first
    allowed = (key_at <= query_at) & (key_at < length)
    scores = scores.reshape(groups, tl, total)
    return jnp.where(allowed[None], scores, NEGATIVE).reshape(groups * tl, total)


def key_value_kernel(x_ref, w_ref, cos_ref, sin_ref, out_ref):
    both = mm(x_ref[...], w_ref[...])
    cosine, sine = cos_ref[...], sin_ref[...]
    for h in range(KV):
        key = turn(both[:, 2 * h * HD : (2 * h + 1) * HD], cosine, sine)
        out_ref[0, :, 2 * h * HD : (2 * h + 1) * HD] = key.astype(BF16)
        value = both[:, (2 * h + 1) * HD : (2 * h + 2) * HD]
        out_ref[0, :, (2 * h + 1) * HD : (2 * h + 2) * HD] = value.astype(BF16)


def key_values(normed_low, qkv_full, tables, nseq):
    rows, D = normed_low.shape
    tl, wide = rows // nseq, 2 * KV * HD
    return pl.pallas_call(
        key_value_kernel,
        grid=(nseq,),
        in_specs=[
            pl.BlockSpec((tl, D), lambda s: (s, 0)),
            pl.BlockSpec((D, wide), lambda s: (0, H * HD // wide)),
            pl.BlockSpec((tl, HD), lambda s: (0, 0)),
            pl.BlockSpec((tl, HD), lambda s: (0, 0)),
        ],
        out_specs=pl.BlockSpec((1, tl, wide), lambda s: (s, 0, 0)),
        out_shape=jax.ShapeDtypeStruct((nseq, tl, wide), BF16),
        compiler_params=pltpu.CompilerParams(vmem_limit_bytes=VMEM_LIMIT),
        cost_estimate=pl.CostEstimate(
            flops=4 * rows * D * wide, bytes_accessed=2 * D * wide, transcendentals=0
        ),
    )(normed_low, qkv_full, *tables)


def attend_kernel(groups, info, q_ref, kv_ref, cos_ref, sin_ref, att_ref, lse_ref, turned_ref):
    tl = q_ref.shape[1]
    cosine, sine = cos_ref[...], sin_ref[...]
    for h in range(groups):
        at = slice(h * HD, (h + 1) * HD)
        turned_ref[0, :, at] = turn(q_ref[0, :, at], cosine, sine).astype(BF16)
    stacked = stack_heads(turned_ref[0], groups)
    scores = masked_scores(
        stacked, kv_ref[0, :, :HD], info[0], info[1 + pl.program_id(0)], groups
    )
    top = jnp.max(scores, axis=-1, keepdims=True)
    shares = jnp.exp(scores - top)
    total = jnp.sum(shares, axis=-1, keepdims=True)
    out = mm(shares.astype(BF16), kv_ref[0, :, HD:]) / total
    lse = top + jnp.log(total)
    for h in range(groups):
        at = slice(h * tl, (h + 1) * tl)
        att_ref[0, :, h * HD : (h + 1) * HD] = out[at].astype(BF16)
        lse_ref[0, 0, :, h : h + 1] = lse[at]


def attend_back_kernel(
    groups, info, q_ref, kv_ref, da_ref, lse_ref, cos_ref, sin_ref, dq_ref, dkv_ref
):
    tl = q_ref.shape[1]
    keys, values = kv_ref[0, :, :HD], kv_ref[0, :, HD:]
    stacked = stack_heads(q_ref[0], groups)
    scores = masked_scores(stacked, keys, info[0], info[1 + pl.program_id(0)], groups)
    lse = jnp.concatenate([lse_ref[0, 0, :, h : h + 1] for h in range(groups)], axis=0)
    probs = jnp.exp(scores - lse)
    grads = stack_heads(da_ref[0], groups)
    d_probs = mm_nt(grads, values)
    delta = jnp.sum(probs * d_probs, axis=-1, keepdims=True)
    d_scores = (probs * (d_probs - delta)).astype(BF16)
    dq = mm(d_scores, keys) * HD ** (-0.5)
    here = pl.ds(pl.multiple_of(info[0], 8), tl)
    cosine, sine = cos_ref[here, :], -sin_ref[here, :]
    for h in range(groups):
        turned = turn(dq[h * tl : (h + 1) * tl], cosine, sine)
        dq_ref[0, :, h * HD : (h + 1) * HD] = turned.astype(BF16)
    dk = mm_tn(d_scores, stacked) * HD ** (-0.5)
    dk = turn(dk, cos_ref[...], -sin_ref[...])
    dv = mm_tn(probs.astype(BF16), grads)
    shape = dkv_ref.shape[:1] + (tl, HD)
    dkv_ref[:, 0, :, :HD] = dk.reshape(shape).astype(BF16)
    dkv_ref[:, 0, :, HD:] = dv.reshape(shape).astype(BF16)


def attention(queries, kv_all, info, tables):
    nseq, tl, width = queries.shape
    total = kv_all.shape[1]
    groups = H // KV
    return pl.pallas_call(
        lambda *refs: attend_kernel(groups, *refs),
        grid_spec=pltpu.PrefetchScalarGridSpec(
            num_scalar_prefetch=1,
            grid=(nseq, KV),
            in_specs=[
                pl.BlockSpec((1, tl, groups * HD), lambda s, n, info: (s, 0, n)),
                pl.BlockSpec((1, total, 2 * HD), lambda s, n, info: (s, 0, n)),
                pl.BlockSpec((tl, HD), lambda s, n, info: (0, 0)),
                pl.BlockSpec((tl, HD), lambda s, n, info: (0, 0)),
            ],
            out_specs=[
                pl.BlockSpec((1, tl, groups * HD), lambda s, n, info: (s, 0, n)),
                pl.BlockSpec((1, 1, tl, HD), lambda s, n, info: (s, n, 0, 0)),
                pl.BlockSpec((1, tl, groups * HD), lambda s, n, info: (s, 0, n)),
            ],
        ),
        out_shape=[
            jax.ShapeDtypeStruct((nseq, tl, width), BF16),
            jax.ShapeDtypeStruct((nseq, KV, tl, HD), F32),
            jax.ShapeDtypeStruct((nseq, tl, width), BF16),
        ],
        compiler_params=pltpu.CompilerParams(vmem_limit_bytes=VMEM_LIMIT),
        cost_estimate=pl.CostEstimate(
            flops=28 * nseq * tl * width * total,
            bytes_accessed=4 * queries.size * 2 + 2 * kv_all.size,
            transcendentals=nseq * H * tl * total,
        ),
    )(info, queries, kv_all, *tables)


def attention_back(queries, kv_all, d_att, lse, info, tables, ctx_count):
    nseq, tl, width = queries.shape
    total = kv_all.shape[1]
    groups = H // KV
    return pl.pallas_call(
        lambda *refs: attend_back_kernel(groups, *refs),
        grid_spec=pltpu.PrefetchScalarGridSpec(
            num_scalar_prefetch=1,
            grid=(nseq, KV),
            in_specs=[
                pl.BlockSpec((1, tl, groups * HD), lambda s, n, info: (s, 0, n)),
                pl.BlockSpec((1, total, 2 * HD), lambda s, n, info: (s, 0, n)),
                pl.BlockSpec((1, tl, groups * HD), lambda s, n, info: (s, 0, n)),
                pl.BlockSpec((1, 1, tl, HD), lambda s, n, info: (s, n, 0, 0)),
                pl.BlockSpec((total, HD), lambda s, n, info: (0, 0)),
                pl.BlockSpec((total, HD), lambda s, n, info: (0, 0)),
            ],
            out_specs=[
                pl.BlockSpec((1, tl, groups * HD), lambda s, n, info: (s, 0, n)),
                pl.BlockSpec((ctx_count, 1, tl, 2 * HD), lambda s, n, info: (0, s, 0, n)),
            ],
        ),
        out_shape=[
            jax.ShapeDtypeStruct((nseq, tl, width), BF16),
            jax.ShapeDtypeStruct((ctx_count, nseq, tl, KV * 2 * HD), BF16),
        ],
        compiler_params=pltpu.CompilerParams(vmem_limit_bytes=VMEM_LIMIT),
        cost_estimate=pl.CostEstimate(
            flops=36 * nseq * tl * width * total,
            bytes_accessed=6 * queries.size * 2 + 4 * kv_all.size,
            transcendentals=nseq * H * tl * total,
        ),
    )(info, queries, kv_all, d_att, lse, *tables)


def expert_kernel(sides, w_mode, g_mode, *refs):
    info = refs[0]
    ins = refs[1 : 1 + sides]
    count = MODE_REFS[w_mode]
    weights = refs[1 + sides : 1 + sides + count]
    at = 1 + sides + count
    din_ref, wy_ref = refs[at : at + 2]
    at = at + 2
    out_refs = refs[at : at + GRAD_REFS[g_mode]]
    at = at + GRAD_REFS[g_mode]
    up, down, x_t, act_t, dgu, dy, act_s, pre, wide, gup, gdn, sems = refs[at:]
    step, steps = pl.program_id(0), pl.num_programs(0)
    D, W = up.shape[0], down.shape[0]
    tile = wide.shape[0]
    tw = 256 if W % 256 == 0 else 128
    td = 256

    wl = W // 4
    dl = 2 * wl

    def shard(up_side, down_side, source, block, first=0):
        pairs, count = [], block.shape[0]
        ups = min(count, dl - first)
        if ups > 0:
            at = pl.ds(pl.multiple_of(source * dl + first, 16), ups)
            pairs.append((up_side.at[at], block.at[pl.ds(0, ups)]))
        if ups < count:
            skip = max(0, ups)
            at = pl.ds(pl.multiple_of(source * wl + first + skip - dl, 16), count - skip)
            pairs.append((down_side.at[at], block.at[pl.ds(skip, count - skip)]))
        return pairs

    def by_distance(up_side, down_side, blocks, sign):
        pairs = []
        for block, k, first in zip(blocks, (1, 2, 2, 2, 3), (0, 0, wl, 2 * wl, 0)):
            source = lax.rem(info[0] + 4 + sign * k, 4)
            pairs += shard(up_side, down_side, source, block, first)
        return pairs

    def copies_of(pairs):
        return [pltpu.make_async_copy(a, b, sems.at[i]) for i, (a, b) in enumerate(pairs)]

    def loads():
        if w_mode == "whole":
            return copies_of([(weights[0].at[info[2]], up), (weights[1].at[info[2]], down)])
        pairs = by_distance(up, down, weights[2:], -1)
        own_up = up.at[pl.ds(pl.multiple_of(info[0] * dl, 16), dl)]
        own_down = down.at[pl.ds(pl.multiple_of(info[0] * wl, 16), wl)]
        pairs += [(own_up, weights[0].at[info[2]]), (own_down, weights[1].at[info[2]])]
        return copies_of([(b, a) for a, b in pairs])

    def put(ref, columns, block):
        per = tile // sides
        shape = (ref.shape[0], ref.shape[2], block.shape[1])
        for i in range(sides):
            ref[:, i, :, columns] = block[i * per : (i + 1) * per].reshape(shape)

    @pl.when(step == 0)
    def _():
        copies = loads()
        for copy in copies:
            copy.start()
        for copy in copies:
            copy.wait()

    rows = pl.ds(pl.multiple_of(step * tile, 128), tile)
    x = jnp.concatenate([r[:, :, :, :D].reshape(-1, D) for r in ins], axis=0)
    g_aug = jnp.concatenate([r[:, :, :, D:].reshape(-1, D + HD) for r in ins], axis=0)
    x_t[:, rows] = x.T
    lane = lax.broadcasted_iota(jnp.int32, (tile, HD), 1)
    picked = (lane == info[1]) | (lane == info[1] + HD // 2)
    w = jnp.sum(jnp.where(picked, g_aug[:, D:].astype(F32), 0.0), axis=1, keepdims=True)
    wide[...] = g_aug[:, :D]
    dy[rows, :] = (g_aug[:, :D].astype(F32) * w).astype(BF16)

    @pl.loop(0, W // tw)
    def _(t):
        a = pl.ds(pl.multiple_of(t * tw, 128), tw)
        b = pl.ds(pl.multiple_of(W + t * tw, 128), tw)
        gate = mm(x, up[:, a])
        lift = mm(x, up[:, b])
        pre[:, a] = gate
        pre[:, b] = lift
        act = gate / (1.0 + jnp.exp(-gate)) * lift
        act = act.astype(BF16)
        act_s[:, a] = act
        act_t[a, rows] = act.T

    def out_step(t, total):
        a = pl.ds(pl.multiple_of(t * td, 128), td)
        y = mm(act_s[...], down[:, a])
        put(wy_ref, a, (y * w).astype(BF16))
        return total + jnp.sum(y * wide[:, a].astype(F32), axis=1, keepdims=True)

    router = lax.fori_loop(0, D // td, out_step, jnp.zeros((tile, 1), F32))
    extra = jnp.where(lane == info[1], router, 0.0).astype(BF16)
    put(wy_ref, pl.ds(D, HD), extra)

    @pl.loop(0, W // tw)
    def _(t):
        a = pl.ds(pl.multiple_of(t * tw, 128), tw)
        b = pl.ds(pl.multiple_of(W + t * tw, 128), tw)
        d_act = mm_nt(dy[rows, :], down[a, :])
        gate, lift = pre[:, a], pre[:, b]
        sig = 1.0 / (1.0 + jnp.exp(-gate))
        dgu[rows, a] = (d_act * lift * sig * (1.0 + gate * (1.0 - sig))).astype(BF16)
        dgu[rows, b] = (d_act * gate * sig).astype(BF16)

    @pl.loop(0, D // td)
    def _(t):
        a = pl.ds(pl.multiple_of(t * td, 128), td)
        put(din_ref, a, mm_nt(dgu[rows, :], up[a, :]).astype(BF16))

    @pl.when(step == steps - 1)
    def _():
        @pl.loop(0, D // td)
        def _(t):
            a = pl.ds(pl.multiple_of(t * td, 128), td)
            gup[a, :] = mm(x_t[a, :], dgu[...]).astype(BF16)

        @pl.loop(0, W // tw)
        def _(t):
            a = pl.ds(pl.multiple_of(t * tw, 128), tw)
            gdn[a, :] = mm(act_t[a, :], dy[...]).astype(BF16)

        if g_mode == "whole":
            pairs = [(gup, out_refs[0]), (gdn, out_refs[1])]
        else:
            pairs = shard(gup, gdn, info[0], out_refs[0])
            pairs += by_distance(gup, gdn, out_refs[1:], 1)
        copies = copies_of(pairs)
        for copy in copies:
            copy.start()
        for copy in copies:
            copy.wait()


def weight_grad_kernel(
    planes, att_ref, db_ref, x_ref, dq_ref, all_ref, pair_ref, out_ref, total, grads, sems
):
    step = pl.program_id(0)
    D, width = x_ref.shape[1], dq_ref.shape[1]
    td = 256

    @pl.when(step == 0)
    def _():
        total[...] = jnp.zeros_like(total)

        @pl.loop(0, D // td)
        def _(t):
            a = pl.ds(pl.multiple_of(t * td, 128), td)
            grads[a, :D] = mm_tn(att_ref[:, a], db_ref[...]).astype(BF16)
            grads[a, D : D + width] = mm_tn(x_ref[:, a], dq_ref[...]).astype(BF16)

    total[...] += mm_tn(pair_ref[...], all_ref[...])

    @pl.when(step == pl.num_programs(0) - 1)
    def _():
        @pl.loop(0, D // td)
        def _(t):
            a = pl.ds(pl.multiple_of(t * td, 128), td)
            grads[a, D + width :] = total[:, a].T.astype(BF16)

        ctx = sems.shape[0] // planes
        cut = D // (planes * ctx)
        copies = []
        for f in range(planes):
            for c in range(ctx):
                source = grads.at[pl.ds((f * ctx + c) * cut, cut)]
                target = out_ref.at[pl.ds((c * planes + f) * cut, cut)]
                copies.append(pltpu.make_async_copy(source, target, sems.at[len(copies)]))
        for copy in copies:
            copy.start()
        for copy in copies:
            copy.wait()


def weight_grads(att, db, x, dq, every_x, pairs, ctx_count, planes):
    rows, D = x.shape
    width, wide = dq.shape[1], pairs.shape[1]
    return pl.pallas_call(
        lambda *refs: weight_grad_kernel(planes, *refs),
        grid=(ctx_count,),
        in_specs=[
            pl.BlockSpec((rows, D), lambda i: (0, 0)),
            pl.BlockSpec((rows, D), lambda i: (0, 0)),
            pl.BlockSpec((rows, D), lambda i: (0, 0)),
            pl.BlockSpec((rows, width), lambda i: (0, 0)),
            pl.BlockSpec((rows, D), lambda i: (i, 0)),
            pl.BlockSpec((rows, wide), lambda i: (i, 0)),
        ],
        out_specs=pl.BlockSpec(memory_space=pl.ANY),
        out_shape=jax.ShapeDtypeStruct((D, D + width + wide), BF16),
        scratch_shapes=[
            pltpu.VMEM((wide, D), F32),
            pltpu.VMEM((D, D + width + wide), BF16),
            pltpu.SemaphoreType.DMA((planes * ctx_count,)),
        ],
        compiler_params=pltpu.CompilerParams(vmem_limit_bytes=VMEM_LIMIT),
        cost_estimate=pl.CostEstimate(
            flops=4 * rows * D * (D + width + ctx_count * wide),
            bytes_accessed=2 * ctx_count * rows * D,
            transcendentals=0,
        ),
    )(att, db, x, dq, every_x, pairs)


def input_back_kernel(
    dq_ref, terms_ref, w_ref, x_ref, inverse_ref, gain_ref, upstream_ref, out_ref, gain_out
):
    width = dq_ref.shape[1]
    pairs = jnp.sum(terms_ref[:, 0].astype(F32), axis=0).astype(BF16)
    grad = mm_nt(dq_ref[...], w_ref[:, :width]) + mm_nt(pairs, w_ref[:, width:])
    values, inverse = x_ref[...].astype(F32), inverse_ref[...]

    @pl.when(pl.program_id(0) == 0)
    def _():
        gain_out[...] = jnp.zeros_like(gain_out)

    gain_out[...] += jnp.sum(grad * values * inverse, axis=0, keepdims=True)
    scaled = grad * gain_ref[...]
    projected = jnp.mean(scaled * values, axis=-1, keepdims=True)
    out_ref[...] = upstream_ref[...] + inverse * scaled - values * inverse**3 * projected


def input_back(dq, terms, w, x, inverse, gain, upstream):
    ctx_count, nseq, tl, wide = terms.shape
    rows, D = x.shape
    return pl.pallas_call(
        input_back_kernel,
        grid=(nseq,),
        in_specs=[
            pl.BlockSpec((tl, dq.shape[1]), lambda i: (i, 0)),
            pl.BlockSpec((ctx_count, 1, tl, wide), lambda i: (0, i, 0, 0)),
            pl.BlockSpec(w.shape, lambda i: (0, 0)),
            pl.BlockSpec((tl, D), lambda i: (i, 0)),
            pl.BlockSpec((tl, 1), lambda i: (i, 0)),
            pl.BlockSpec((1, D), lambda i: (0, 0)),
            pl.BlockSpec((tl, D), lambda i: (i, 0)),
        ],
        out_specs=[
            pl.BlockSpec((tl, D), lambda i: (i, 0)),
            pl.BlockSpec((1, D), lambda i: (0, 0)),
        ],
        out_shape=[
            jax.ShapeDtypeStruct((rows, D), F32),
            jax.ShapeDtypeStruct((1, D), F32),
        ],
        compiler_params=pltpu.CompilerParams(vmem_limit_bytes=VMEM_LIMIT),
        cost_estimate=pl.CostEstimate(
            flops=8 * rows * w.size, bytes_accessed=16 * rows * D, transcendentals=0
        ),
    )(dq, terms, w, x, inverse, gain, upstream)


def blank(shapes):
    return pl.pallas_call(
        lambda *refs: None,
        out_specs=[pl.BlockSpec(memory_space=pl.ANY)] * len(shapes),
        out_shape=[jax.ShapeDtypeStruct(shape, F32) for shape in shapes],
    )()


MODE_REFS = {"whole": 2, "parts": 7}
GRAD_REFS = {"whole": 2, "parts": 6}


def run_expert(piece, W, ins, weights, info, w_mode, g_mode):
    C, mine, slots, wide = ins[0].shape
    D = (wide - HD) // 2
    sides = len(ins)
    per_step = C
    while per_step > 1 and (per_step * sides * slots > 640 or C % per_step):
        per_step -= 1
    tile = per_step * sides * slots
    rows = C * sides * slots

    def spec(width, at):
        return pl.BlockSpec((per_step, 1, slots, width), lambda i, info: (i, at, 0, 0))

    def out_spec(width):
        return pl.BlockSpec((per_step, sides, slots, width), lambda i, info: (i, 0, 0, 0))

    any_spec = pl.BlockSpec(memory_space=pl.ANY)
    if g_mode == "whole":
        grads = [(D, 2 * W), (W, D)]
    else:
        grads = [(n * W // 4, D) for n in (3, 3, 1, 1, 1, 3)]
    grads = [jax.ShapeDtypeStruct(shape, BF16) for shape in grads]
    return pl.pallas_call(
        lambda *refs: expert_kernel(sides, w_mode, g_mode, *refs),
        grid_spec=pltpu.PrefetchScalarGridSpec(
            num_scalar_prefetch=1,
            grid=(C // per_step,),
            in_specs=[spec(wide, piece)] * sides
            + [any_spec] * len(weights),
            out_specs=[out_spec(D), out_spec(D + HD)] + [any_spec] * len(grads),
            scratch_shapes=[
                pltpu.VMEM((D, 2 * W), BF16),
                pltpu.VMEM((W, D), BF16),
                pltpu.VMEM((D, rows), BF16),
                pltpu.VMEM((W, rows), BF16),
                pltpu.VMEM((rows, 2 * W), BF16),
                pltpu.VMEM((rows, D), BF16),
                pltpu.VMEM((tile, W), BF16),
                pltpu.VMEM((tile, 2 * W), F32),
                pltpu.VMEM((tile, D), BF16),
                pltpu.VMEM((D, 2 * W), BF16),
                pltpu.VMEM((W, D), BF16),
                pltpu.SemaphoreType.DMA((12,)),
            ],
        ),
        out_shape=[jax.ShapeDtypeStruct((C, sides, slots, n), BF16) for n in (D, D + HD)]
        + grads,
        compiler_params=pltpu.CompilerParams(vmem_limit_bytes=VMEM_LIMIT),
        cost_estimate=pl.CostEstimate(
            flops=38 * rows * D * W,
            bytes_accessed=8 * rows * D + 24 * D * W,
            transcendentals=2 * rows * W,
        ),
    )(info, *ins, *weights)


def local(
    tokens,
    lengths,
    expert_picks,
    router_weights,
    first_gain,
    second_gain,
    query_weight,
    key_weight,
    value_weight,
    output_weight,
    up_weight,
    down_weight,
    cotangent,
):
    batches, seqs_here, tl, D = tokens.shape
    C = lax.axis_size("ctx")
    F = lax.axis_size("fsdp")
    c = lax.axis_index("ctx")
    f = lax.axis_index("fsdp")
    split = max(1, C // EXPERTS)
    pieces = up_weight.shape[0]
    W = up_weight.shape[2] // 2
    merged = pieces % 2 == 0 and F == 4 and 2 * W == D
    share = 2 if merged else 1
    mine = pieces // share
    role = f % share
    nseq = batches * seqs_here
    cap = max(2, (5 * tl * TOP + 4 * EXPERTS - 1) // (4 * EXPERTS))
    while nseq * cap % 16:
        cap += 1
    slots = nseq * cap
    rows = nseq * tl
    L = C * tl
    width = H * HD
    Dl = query_weight.shape[0]
    cut = Dl // C

    positions = c * tl + jnp.arange(tl, dtype=jnp.int32)
    tables = angle_tables(positions)
    all_tables = angle_tables(jnp.arange(L, dtype=jnp.int32))
    lens = lengths.reshape(nseq)
    live = (positions[None, :] < lens[:, None]).reshape(rows)
    live_rows = live.astype(F32)[:, None]

    def gate(*values):
        return lax.optimization_barrier(values)

    def shift(block, k):
        return lax.ppermute(block, "fsdp", [(i, (i + k) % F) for i in range(F)])

    def fsdp_gather(block):
        got = [shift(block, k) for k in range(F - 1, 0, -1)]
        ring = jnp.stack(got + [block] + got)
        return lax.dynamic_slice_in_dim(ring, F - 1 - f, F, 0)

    def fsdp_scatter_sum(parts):
        total = lax.dynamic_index_in_dim(parts, f, 0, keepdims=False).astype(F32)
        for k in range(1, F):
            block = lax.dynamic_index_in_dim(parts, (f + k) % F, 0, keepdims=False)
            total = total + shift(block, k).astype(F32)
        return total

    def swap(block):
        return lax.ppermute(block, "fsdp", [(i, i ^ 1) for i in range(F)])

    def exchange(blocks):
        return lax.all_to_all(blocks, "ctx", 0, 0, tiled=True)

    def ctx_gather(lines):
        return lax.all_gather(lines, "ctx", axis=1, tiled=True).reshape(D, -1)

    def part_of(weight):
        return lax.dynamic_slice_in_dim(weight, c * cut, cut, 0)

    key_part, value_part = part_of(key_weight), part_of(value_weight)
    qkv_part = [part_of(query_weight)]
    for h in range(KV):
        qkv_part += [part[:, h * HD : (h + 1) * HD] for part in (key_part, value_part)]
    qkv_part = jnp.concatenate(qkv_part, axis=1)
    out_part, gain_parts = part_of(output_weight), jnp.stack([first_gain, second_gain])
    qkv_lines = fsdp_gather(qkv_part)

    messages, operands = {}, {}
    expert_in = [up_weight, down_weight]

    def shard_of(at):
        return jnp.concatenate(
            [lax.dynamic_index_in_dim(x, at, 0, keepdims=False) for x in expert_in]
        )

    def operand(name):
        if name in operands:
            return operands[name]
        j = "wv".index(name[0])
        block = shard_of((role if name[1] == "2" else 1 - role) * mine + j)
        third = block.shape[0] // 3
        at = "abc".find(name[2:]) * third if name[2:] else 0
        return block[at : at + third] if name[2:] else block

    def send(name, block):
        return shift(block, int(name[1]))

    def step(need, values, go):
        if not merged:
            return lax.optimization_barrier(values)
        fresh = tuple(operand(name) for name in go)
        got, values, fresh = lax.optimization_barrier(
            (tuple(messages[name] for name in need), values, fresh)
        )
        messages.update(zip(need, got))
        messages.update((name, send(name, block)) for name, block in zip(go, fresh))
        return values

    picks = expert_picks.reshape(rows, TOP)
    gates = router_weights.reshape(rows, TOP)
    cot = cotangent.reshape(rows, D)
    expert_ids = jnp.arange(EXPERTS, dtype=jnp.int32)
    hit = picks[:, :, None] == expert_ids
    by_expert = jnp.sum(jnp.where(hit, gates[:, :, None], 0.0), axis=1) * live_rows
    high = by_expert.astype(BF16)
    low = (by_expert - high.astype(F32)).astype(BF16)
    gap = jnp.zeros((rows, HD // 2 - EXPERTS), BF16)
    table = jnp.concatenate([high, gap, low, gap], axis=1)
    number = jnp.arange(C)[:, None] * pieces + role * mine + jnp.arange(mine)[None, :]
    expert_of = (number // split).reshape(C * mine)
    earlier = jnp.tril(jnp.ones((tl, tl), BF16), -1)
    pick_map = (expert_ids[:, None] == expert_of[None, :]).astype(BF16)

    def route(table):
        match = table[:, :EXPERTS] > 0
        ranks = jnp.einsum(
            "ab,sbe->sae",
            earlier,
            match.astype(BF16).reshape(nseq, tl, -1),
            preferred_element_type=F32,
        )
        base = (jnp.arange(nseq) * cap)[:, None, None]
        code = jnp.where(match, (ranks + base).reshape(rows, -1), -1.0).astype(BF16)
        code = mm_tn(pick_map, code.T)
        chosen = code[:, None, :] == jnp.arange(slots, dtype=F32)[None, :, None]
        return chosen.astype(BF16).reshape(C, mine, slots, rows)

    def to_slots(sel, source):
        out = mm(sel.reshape(C * mine * slots, rows), source)
        return out.astype(BF16).reshape(C, mine, slots, -1)

    inputs = tokens.reshape(rows, D).astype(F32)
    step([], (qkv_part,), ["w1"])
    _, gain_parts, table, cot, out_part = gate(qkv_lines, gain_parts, table, cot, out_part)
    gains, out_lines = fsdp_gather(gain_parts), fsdp_gather(out_part)
    sels = [route(table)]
    qkv_full, sels[0], table, out_lines, cot_wide, all_tables = step(
        ["w1"],
        (
            ctx_gather(qkv_lines),
            sels[0],
            table,
            out_lines,
            jnp.concatenate([cot, table], axis=1),
            all_tables,
        ),
        ["w3"],
    )
    first_scale = gains[:, 0].reshape(D).astype(F32)
    second_scale = gains[:, 1].reshape(D).astype(F32)
    normed, inverse_one = norm_forward(inputs, first_scale)
    normed_low = normed.astype(BF16)
    kv_low = key_values(normed_low, qkv_full, tables, nseq)
    kv_all = lax.all_gather(kv_low, "ctx", axis=1, tiled=True)
    _, expert_in, qkv_full, table = gate(kv_low, expert_in, qkv_full, table)
    query_pre = mm(normed_low, qkv_full[:, :width]).reshape(nseq, tl, width)
    info = jnp.concatenate([(c * tl)[None], lens])
    kv_all, query_pre, out_lines, table = step(
        ["w3"], (kv_all, query_pre, out_lines, table), ["w2a"]
    )
    far_table = swap(table) if share == 2 else table
    out_full = ctx_gather(out_lines)
    attended, lse, queries = attention(query_pre, kv_all, info, tables)
    attended, cot_wide, far_table = step(["w2a"], (attended, cot_wide, far_table), [])
    attended_low = attended.reshape(rows, width)
    hidden = inputs + live_rows * mm(attended_low, out_full)
    second, inverse_two = norm_forward(hidden, second_scale)
    second_low = second.astype(BF16)

    second_low, cot_wide = step([], (second_low, cot_wide), ["w2b", "w2c"])
    wide_rows = jnp.concatenate([second_low, cot_wide], axis=1)
    expert_rows = [exchange(to_slots(sels[0], wide_rows))]
    shards = None
    if merged:
        far_rows = swap(wide_rows)
        sels.append(route(far_table))
        shards = list(blank([(pieces, Dl, 2 * W), (pieces, W // F, D)]))
        far_rows, expert_rows[0], sels[1], shards = step(
            ["w2b", "w2c"], (far_rows, expert_rows[0], sels[1], shards), ["v1", "v3", "v2a"]
        )
        expert_rows.append(exchange(to_slots(sels[1], far_rows)))

    def expert(j):
        at = role * mine + j
        expert_info = jnp.stack([f, (c * pieces + at) // split, at])
        if not merged:
            return run_expert(j, W, expert_rows, [up_full, down_full], expert_info, "whole", "whole")
        names = ["wv"[j] + k for k in ("1", "2a", "2b", "2c", "3")]
        weights = [up_weight, down_weight] + [messages[name] for name in names]
        out = run_expert(j, W, expert_rows, weights, expert_info, "parts", "parts")
        for k, grad in zip(("0", "1", "2a", "2b", "2c", "3"), out[2:]):
            operands["pq"[j] + k] = grad
        return out

    if merged:
        expert_rows[1], normed_mine = step(
            ["v1", "v3", "v2a"], (expert_rows[1], normed_low), ["v2b", "v2c"]
        )
        every_normed = lax.all_gather(normed_mine, "ctx", axis=0, tiled=True)
        outs = [expert(0)]
        d_in, mixed = [outs[0][0]], [outs[0][1]]
        d_in[0], expert_rows[0], mixed[0] = step(
            ["v2b", "v2c"], (d_in[0], expert_rows[0], mixed[0]), ["p1", "p2a"]
        )
        d_in[0] = exchange(d_in[0])
        outs.append(expert(1))
        last, d_in[0], later, every_normed = step(
            ["p1", "p2a"], (outs[1][0], d_in[0], outs[1][1], every_normed), ["p3"]
        )
        d_in.append(exchange(last))
        mixed.append(later)
    else:
        up_full = lax.all_gather(up_weight, "fsdp", axis=1, tiled=True)
        down_full = lax.all_gather(down_weight, "fsdp", axis=1, tiled=True)
        outs = [expert(j) for j in range(mine)]
        d_in = [exchange(out[0]) for out in outs]
        mixed = [exchange(out[1]) for out in outs]

    def collect(backs):
        sums = []
        for i, sel in enumerate(sels):
            total = 0.0
            for j, back in enumerate(backs):
                total = total + mm_tn(
                    sel[:, j].reshape(C * slots, rows), back[:, i].reshape(C * slots, -1)
                )
            sums.append(total)
        return sums

    def fill(at, total):
        for i, block in enumerate((total[:Dl], total[Dl:])):
            shards[i] = lax.dynamic_update_slice(shards[i], block[None], (at, 0, 0))

    def pair_sum(first, *others):
        far = jnp.concatenate([messages[name] for name in others])
        return first.astype(F32) + far.astype(F32)

    sums = collect(d_in)
    dispatch_grad = sums[0]
    if share == 2:
        far, mixed[0] = step(["p3"], (sums[1].astype(BF16), mixed[0]), ["p2b"])
        dispatch_grad = dispatch_grad + swap(far).astype(F32)
        mixed[0] = exchange(mixed[0])
        (dispatch_grad,) = step(["p2b"], (dispatch_grad,), [])

    upstream = cot.astype(F32)
    norm_grad, second_grads = norm_backward(hidden, inverse_two, second_scale, dispatch_grad)
    hidden_grad = upstream + norm_grad
    branch_grad = (live_rows * hidden_grad).astype(BF16)
    def by_target(grad):
        return grad.astype(BF16).reshape(F, C, cut, -1).transpose(1, 0, 2, 3)

    def over_ctx(blocks):
        return jnp.sum(exchange(blocks).astype(F32), axis=0).astype(BF16)

    def scatter(blocks):
        (blocks,) = gate(blocks.reshape(D, -1))
        total = lax.psum_scatter(blocks, "ctx", scatter_dimension=0, tiled=True)
        return gate(total)[0].reshape(F, cut, -1)

    d_att = mm_nt(branch_grad, out_full).astype(BF16)
    if merged:
        d_att, mixed[0], mixed[1] = step([], (d_att, mixed[0], mixed[1]), ["p2c"])
        mixed[1] = exchange(mixed[1])
    query_back, terms = attention_back(
        queries, kv_all, d_att.reshape(nseq, tl, width), lse, info, all_tables, C
    )
    query_back = query_back.reshape(rows, width)
    terms, query_back = step(["p2c"], (terms, query_back), ["q2a"])
    if merged:
        own_terms = exchange(terms)
        flat_terms = terms.reshape(C * rows, -1)
        blocks = weight_grads(
            attended_low, branch_grad, normed_low, query_back, every_normed, flat_terms, C, F
        )
        blocks, mixed = step(["q2a"], (blocks, mixed), ["q2b", "q2c"])
        mixed_sums = collect(mixed)
        far = swap(mixed_sums[1].astype(BF16))
        own_terms, shards, far = step(["q2b", "q2c"], (own_terms, shards, far), ["q1"])
    else:
        own_terms = over_ctx(terms)
        pair_grad = mm_tn(normed_low, own_terms.reshape(rows, 2 * KV * HD))
        query_grad = mm_tn(normed_low, query_back)
        projection_grad = mm_tn(attended_low, branch_grad)
        blocks = by_target(jnp.concatenate([projection_grad, query_grad, pair_grad], axis=1))
        mixed_rows = collect(mixed)[0]
    weight_rows = scatter(blocks)
    if not merged:
        own_terms = own_terms.reshape((1,) + terms.shape[1:])
    grad_tokens, first_grads = input_back(
        query_back,
        own_terms,
        qkv_full,
        tokens.reshape(rows, D),
        inverse_one,
        first_scale[None],
        hidden_grad,
    )
    first_grads = first_grads[0]
    if merged:
        first_grads, mixed_sums[0] = step(["q1"], (first_grads, mixed_sums[0]), [])
        fill(role * mine, pair_sum(operands["p0"], "p2a", "p2b", "p2c"))
        fill((1 - role) * mine, pair_sum(messages["p1"], "p3"))
    gain_columns = jnp.stack([first_grads, second_grads]).reshape(2, F, Dl).transpose(1, 0, 2)
    gain_columns = gain_columns.reshape(F, cut, -1)
    gain_count = gain_columns.shape[2]
    gain_columns = jnp.pad(gain_columns, ((0, 0), (0, 0), (0, -gain_count % HD)))
    weight_rows, gain_columns = gate(weight_rows, gain_columns)
    wide = jnp.concatenate([weight_rows, gain_columns.astype(BF16)], axis=2)
    wide = fsdp_scatter_sum(wide).astype(BF16)
    if merged:
        wide, far = step([], (wide, far), ["q3"])
        mixed_rows = mixed_sums[0] + far.astype(F32)
        fill(role * mine + 1, pair_sum(operands["q0"], "q2a", "q2b", "q2c"))
    wide = lax.all_gather(wide, "ctx", axis=0, tiled=False)
    whole = wide[:, :, : D + width + 2 * KV * HD].reshape(Dl, -1).astype(F32)
    grad_projection, grad_query = whole[:, :D], whole[:, D : D + width]
    grad_pairs = whole[:, D + width :].reshape(Dl, KV, 2, HD)
    gain_at = D + width + 2 * KV * HD
    gain_sums = jnp.sum(wide[:, :, gain_at : gain_at + gain_count].astype(F32), axis=0)
    grad_first, grad_second = gain_sums.reshape(2, Dl)

    grads = (grad_projection, grad_query, grad_pairs, grad_first, grad_second)
    grads = step(["q3"], grads, [])
    grad_projection, grad_query, grad_pairs, grad_first, grad_second = grads
    block_rows = (hidden + mixed_rows[:, :D]).astype(BF16)
    router_by_expert = mixed_rows[:, D : D + EXPERTS]
    grad_router = jnp.sum(jnp.where(hit, router_by_expert[:, None, :], 0.0), axis=2)

    if merged:
        fill((1 - role) * mine + 1, pair_sum(messages["q1"], "q3"))
        grad_up, grad_down = shards
    else:
        grad_up, grad_down = [
            lax.psum_scatter(
                jnp.stack([out[2 + i] for out in outs]), "fsdp", scatter_dimension=1, tiled=True
            ).astype(F32)
            for i in range(2)
        ]

    shape = (batches, seqs_here, tl)
    return (
        block_rows.reshape(shape + (D,)),
        grad_tokens.reshape(shape + (D,)),
        grad_router.reshape(shape + (TOP,)),
        grad_first,
        grad_second,
        grad_query,
        grad_pairs[:, :, 0].reshape(Dl, KV * HD),
        grad_pairs[:, :, 1].reshape(Dl, KV * HD),
        grad_projection,
        grad_up,
        grad_down,
    )


def solution(mesh):
    rows = P(None, "fsdp", "ctx", None)
    weight = P("fsdp", None)
    expert = P("ctx", "fsdp", None)
    placed = (rows, P(None, "fsdp"), rows, rows, P("fsdp"), P("fsdp"))
    placed = placed + (weight,) * 4 + (expert,) * 2 + (rows,)
    outs = (rows, rows, rows, P("fsdp"), P("fsdp")) + (weight,) * 4 + (expert,) * 2
    return jax.shard_map(local, mesh=mesh, in_specs=placed, out_specs=outs, check_vma=False)
```

```python
import jax
import jax.numpy as jnp
from jax import lax
from jax.experimental import pallas as pl
from jax.experimental.pallas import tpu as pltpu
from jax.sharding import PartitionSpec as P

H = 12
KV = 2
HD = 128
TOP = 4
EXPERTS = 32
EPSILON = 1e-06
ROPE_BASE = 10000.0
NEGATIVE = -1e30
F32 = jnp.float32
BF16 = jnp.bfloat16


def angle_tables(positions):
    frequency = ROPE_BASE ** (-(jnp.arange(HD // 2, dtype=F32) * 2.0 / HD))
    angles = positions.astype(F32)[:, None] * frequency[None, :]
    cosine, sine = jnp.cos(angles), jnp.sin(angles)
    return jnp.concatenate([cosine, cosine], 1), jnp.concatenate([-sine, sine], 1)


def turn(vectors, cosine, sine):
    return vectors * cosine + pltpu.roll(vectors, HD // 2, 1) * sine


def norm_forward(values, gain_row):
    inverse = lax.rsqrt(jnp.mean(values * values, axis=-1, keepdims=True) + EPSILON)
    return values * inverse * gain_row, inverse


def norm_backward(values, inverse, gain_row, upstream):
    gain_grad = jnp.sum(upstream * values * inverse, axis=0)
    scaled = upstream * gain_row
    projected = jnp.mean(scaled * values, axis=-1, keepdims=True)
    return inverse * scaled - values * inverse**3 * projected, gain_grad


def mm(a, b):
    return jnp.dot(a, b, preferred_element_type=F32)


def mm_nt(a, b):
    return lax.dot_general(a, b, (((1,), (1,)), ((), ())), preferred_element_type=F32)


def mm_tn(a, b):
    return lax.dot_general(a, b, (((0,), (0,)), ((), ())), preferred_element_type=F32)


VMEM_LIMIT = 60 * 1024 * 1024


def stack_heads(block, groups):
    return jnp.concatenate([block[:, h * HD : (h + 1) * HD] for h in range(groups)], axis=0)


def masked_scores(stacked, keys, first, length, groups):
    tl = stacked.shape[0] // groups
    total = keys.shape[0]
    scores = mm_nt(stacked, keys) * HD ** (-0.5)
    key_at = lax.broadcasted_iota(jnp.int32, (tl, total), 1)
    query_at = lax.broadcasted_iota(jnp.int32, (tl, total), 0) + first
    allowed = (key_at <= query_at) & (key_at < length)
    scores = scores.reshape(groups, tl, total)
    return jnp.where(allowed[None], scores, NEGATIVE).reshape(groups * tl, total)


def key_value_kernel(x_ref, w_ref, cos_ref, sin_ref, out_ref):
    both = mm(x_ref[...], w_ref[...])
    cosine, sine = cos_ref[...], sin_ref[...]
    for h in range(KV):
        key = turn(both[:, 2 * h * HD : (2 * h + 1) * HD], cosine, sine)
        out_ref[0, :, 2 * h * HD : (2 * h + 1) * HD] = key.astype(BF16)
        value = both[:, (2 * h + 1) * HD : (2 * h + 2) * HD]
        out_ref[0, :, (2 * h + 1) * HD : (2 * h + 2) * HD] = value.astype(BF16)


def key_values(normed_low, qkv_full, tables, nseq):
    rows, D = normed_low.shape
    tl, wide = rows // nseq, 2 * KV * HD
    return pl.pallas_call(
        key_value_kernel,
        grid=(nseq,),
        in_specs=[
            pl.BlockSpec((tl, D), lambda s: (s, 0)),
            pl.BlockSpec((D, wide), lambda s: (0, H * HD // wide)),
            pl.BlockSpec((tl, HD), lambda s: (0, 0)),
            pl.BlockSpec((tl, HD), lambda s: (0, 0)),
        ],
        out_specs=pl.BlockSpec((1, tl, wide), lambda s: (s, 0, 0)),
        out_shape=jax.ShapeDtypeStruct((nseq, tl, wide), BF16),
        compiler_params=pltpu.CompilerParams(vmem_limit_bytes=VMEM_LIMIT),
        cost_estimate=pl.CostEstimate(
            flops=4 * rows * D * wide, bytes_accessed=2 * D * wide, transcendentals=0
        ),
    )(normed_low, qkv_full, *tables)


def attend_kernel(groups, info, q_ref, kv_ref, cos_ref, sin_ref, att_ref, lse_ref, turned_ref):
    tl = q_ref.shape[1]
    cosine, sine = cos_ref[...], sin_ref[...]
    for h in range(groups):
        at = slice(h * HD, (h + 1) * HD)
        turned_ref[0, :, at] = turn(q_ref[0, :, at], cosine, sine).astype(BF16)
    stacked = stack_heads(turned_ref[0], groups)
    scores = masked_scores(
        stacked, kv_ref[0, :, :HD], info[0], info[1 + pl.program_id(0)], groups
    )
    top = jnp.max(scores, axis=-1, keepdims=True)
    shares = jnp.exp(scores - top)
    total = jnp.sum(shares, axis=-1, keepdims=True)
    out = mm(shares.astype(BF16), kv_ref[0, :, HD:]) / total
    lse = top + jnp.log(total)
    for h in range(groups):
        at = slice(h * tl, (h + 1) * tl)
        att_ref[0, :, h * HD : (h + 1) * HD] = out[at].astype(BF16)
        lse_ref[0, 0, :, h : h + 1] = lse[at]


def attend_back_kernel(
    groups, info, q_ref, kv_ref, da_ref, lse_ref, cos_ref, sin_ref, dq_ref, dkv_ref
):
    tl = q_ref.shape[1]
    keys, values = kv_ref[0, :, :HD], kv_ref[0, :, HD:]
    stacked = stack_heads(q_ref[0], groups)
    scores = masked_scores(stacked, keys, info[0], info[1 + pl.program_id(0)], groups)
    lse = jnp.concatenate([lse_ref[0, 0, :, h : h + 1] for h in range(groups)], axis=0)
    probs = jnp.exp(scores - lse)
    grads = stack_heads(da_ref[0], groups)
    d_probs = mm_nt(grads, values)
    delta = jnp.sum(probs * d_probs, axis=-1, keepdims=True)
    d_scores = (probs * (d_probs - delta)).astype(BF16)
    dq = mm(d_scores, keys) * HD ** (-0.5)
    here = pl.ds(pl.multiple_of(info[0], 8), tl)
    cosine, sine = cos_ref[here, :], -sin_ref[here, :]
    for h in range(groups):
        turned = turn(dq[h * tl : (h + 1) * tl], cosine, sine)
        dq_ref[0, :, h * HD : (h + 1) * HD] = turned.astype(BF16)
    dk = mm_tn(d_scores, stacked) * HD ** (-0.5)
    dk = turn(dk, cos_ref[...], -sin_ref[...])
    dv = mm_tn(probs.astype(BF16), grads)
    shape = dkv_ref.shape[:1] + (tl, HD)
    dkv_ref[:, 0, :, :HD] = dk.reshape(shape).astype(BF16)
    dkv_ref[:, 0, :, HD:] = dv.reshape(shape).astype(BF16)


def attention(queries, kv_all, info, tables):
    nseq, tl, width = queries.shape
    total = kv_all.shape[1]
    groups = H // KV
    return pl.pallas_call(
        lambda *refs: attend_kernel(groups, *refs),
        grid_spec=pltpu.PrefetchScalarGridSpec(
            num_scalar_prefetch=1,
            grid=(nseq, KV),
            in_specs=[
                pl.BlockSpec((1, tl, groups * HD), lambda s, n, info: (s, 0, n)),
                pl.BlockSpec((1, total, 2 * HD), lambda s, n, info: (s, 0, n)),
                pl.BlockSpec((tl, HD), lambda s, n, info: (0, 0)),
                pl.BlockSpec((tl, HD), lambda s, n, info: (0, 0)),
            ],
            out_specs=[
                pl.BlockSpec((1, tl, groups * HD), lambda s, n, info: (s, 0, n)),
                pl.BlockSpec((1, 1, tl, HD), lambda s, n, info: (s, n, 0, 0)),
                pl.BlockSpec((1, tl, groups * HD), lambda s, n, info: (s, 0, n)),
            ],
        ),
        out_shape=[
            jax.ShapeDtypeStruct((nseq, tl, width), BF16),
            jax.ShapeDtypeStruct((nseq, KV, tl, HD), F32),
            jax.ShapeDtypeStruct((nseq, tl, width), BF16),
        ],
        compiler_params=pltpu.CompilerParams(vmem_limit_bytes=VMEM_LIMIT),
        cost_estimate=pl.CostEstimate(
            flops=28 * nseq * tl * width * total,
            bytes_accessed=4 * queries.size * 2 + 2 * kv_all.size,
            transcendentals=nseq * H * tl * total,
        ),
    )(info, queries, kv_all, *tables)


def attention_back(queries, kv_all, d_att, lse, info, tables, ctx_count):
    nseq, tl, width = queries.shape
    total = kv_all.shape[1]
    groups = H // KV
    return pl.pallas_call(
        lambda *refs: attend_back_kernel(groups, *refs),
        grid_spec=pltpu.PrefetchScalarGridSpec(
            num_scalar_prefetch=1,
            grid=(nseq, KV),
            in_specs=[
                pl.BlockSpec((1, tl, groups * HD), lambda s, n, info: (s, 0, n)),
                pl.BlockSpec((1, total, 2 * HD), lambda s, n, info: (s, 0, n)),
                pl.BlockSpec((1, tl, groups * HD), lambda s, n, info: (s, 0, n)),
                pl.BlockSpec((1, 1, tl, HD), lambda s, n, info: (s, n, 0, 0)),
                pl.BlockSpec((total, HD), lambda s, n, info: (0, 0)),
                pl.BlockSpec((total, HD), lambda s, n, info: (0, 0)),
            ],
            out_specs=[
                pl.BlockSpec((1, tl, groups * HD), lambda s, n, info: (s, 0, n)),
                pl.BlockSpec((ctx_count, 1, tl, 2 * HD), lambda s, n, info: (0, s, 0, n)),
            ],
        ),
        out_shape=[
            jax.ShapeDtypeStruct((nseq, tl, width), BF16),
            jax.ShapeDtypeStruct((ctx_count, nseq, tl, KV * 2 * HD), BF16),
        ],
        compiler_params=pltpu.CompilerParams(vmem_limit_bytes=VMEM_LIMIT),
        cost_estimate=pl.CostEstimate(
            flops=36 * nseq * tl * width * total,
            bytes_accessed=6 * queries.size * 2 + 4 * kv_all.size,
            transcendentals=nseq * H * tl * total,
        ),
    )(info, queries, kv_all, d_att, lse, *tables)


def expert_kernel(sides, w_mode, g_mode, *refs):
    info = refs[0]
    ins = refs[1 : 1 + sides]
    count = MODE_REFS[w_mode]
    weights = refs[1 + sides : 1 + sides + count]
    at = 1 + sides + count
    din_ref, wy_ref = refs[at : at + 2]
    at = at + 2
    out_refs = refs[at : at + GRAD_REFS[g_mode]]
    at = at + GRAD_REFS[g_mode]
    up, down, x_t, act_t, dgu, dy, act_s, pre, wide, gup, gdn, sems = refs[at:]
    step, steps = pl.program_id(0), pl.num_programs(0)
    D, W = up.shape[0], down.shape[0]
    tile = wide.shape[0]
    tw = 256 if W % 256 == 0 else 128
    td = 256

    wl = W // 4
    dl = 2 * wl

    def shard(up_side, down_side, source, block, first=0):
        pairs, count = [], block.shape[0]
        ups = min(count, dl - first)
        if ups > 0:
            at = pl.ds(pl.multiple_of(source * dl + first, 16), ups)
            pairs.append((up_side.at[at], block.at[pl.ds(0, ups)]))
        if ups < count:
            skip = max(0, ups)
            at = pl.ds(pl.multiple_of(source * wl + first + skip - dl, 16), count - skip)
            pairs.append((down_side.at[at], block.at[pl.ds(skip, count - skip)]))
        return pairs

    def by_distance(up_side, down_side, blocks, sign):
        pairs = []
        for block, k, first in zip(blocks, (1, 2, 2, 2, 3), (0, 0, wl, 2 * wl, 0)):
            source = lax.rem(info[0] + 4 + sign * k, 4)
            pairs += shard(up_side, down_side, source, block, first)
        return pairs

    def copies_of(pairs):
        return [pltpu.make_async_copy(a, b, sems.at[i]) for i, (a, b) in enumerate(pairs)]

    def loads():
        if w_mode == "whole":
            return copies_of([(weights[0].at[info[2]], up), (weights[1].at[info[2]], down)])
        pairs = by_distance(up, down, weights[2:], -1)
        own_up = up.at[pl.ds(pl.multiple_of(info[0] * dl, 16), dl)]
        own_down = down.at[pl.ds(pl.multiple_of(info[0] * wl, 16), wl)]
        pairs += [(own_up, weights[0].at[info[2]]), (own_down, weights[1].at[info[2]])]
        return copies_of([(b, a) for a, b in pairs])

    def put(ref, columns, block):
        per = tile // sides
        shape = (ref.shape[0], ref.shape[2], block.shape[1])
        for i in range(sides):
            ref[:, i, :, columns] = block[i * per : (i + 1) * per].reshape(shape)

    @pl.when(step == 0)
    def _():
        copies = loads()
        for copy in copies:
            copy.start()
        for copy in copies:
            copy.wait()

    rows = pl.ds(pl.multiple_of(step * tile, 128), tile)
    x = jnp.concatenate([r[:, :, :, :D].reshape(-1, D) for r in ins], axis=0)
    g_aug = jnp.concatenate([r[:, :, :, D:].reshape(-1, D + HD) for r in ins], axis=0)
    x_t[:, rows] = x.T
    lane = lax.broadcasted_iota(jnp.int32, (tile, HD), 1)
    picked = (lane == info[1]) | (lane == info[1] + HD // 2)
    w = jnp.sum(jnp.where(picked, g_aug[:, D:].astype(F32), 0.0), axis=1, keepdims=True)
    wide[...] = g_aug[:, :D]
    dy[rows, :] = (g_aug[:, :D].astype(F32) * w).astype(BF16)

    @pl.loop(0, W // tw)
    def _(t):
        a = pl.ds(pl.multiple_of(t * tw, 128), tw)
        b = pl.ds(pl.multiple_of(W + t * tw, 128), tw)
        gate = mm(x, up[:, a])
        lift = mm(x, up[:, b])
        pre[:, a] = gate
        pre[:, b] = lift
        act = gate / (1.0 + jnp.exp(-gate)) * lift
        act = act.astype(BF16)
        act_s[:, a] = act
        act_t[a, rows] = act.T

    def out_step(t, total):
        a = pl.ds(pl.multiple_of(t * td, 128), td)
        y = mm(act_s[...], down[:, a])
        put(wy_ref, a, (y * w).astype(BF16))
        return total + jnp.sum(y * wide[:, a].astype(F32), axis=1, keepdims=True)

    router = lax.fori_loop(0, D // td, out_step, jnp.zeros((tile, 1), F32))
    extra = jnp.where(lane == info[1], router, 0.0).astype(BF16)
    put(wy_ref, pl.ds(D, HD), extra)

    @pl.loop(0, W // tw)
    def _(t):
        a = pl.ds(pl.multiple_of(t * tw, 128), tw)
        b = pl.ds(pl.multiple_of(W + t * tw, 128), tw)
        d_act = mm_nt(dy[rows, :], down[a, :])
        gate, lift = pre[:, a], pre[:, b]
        sig = 1.0 / (1.0 + jnp.exp(-gate))
        dgu[rows, a] = (d_act * lift * sig * (1.0 + gate * (1.0 - sig))).astype(BF16)
        dgu[rows, b] = (d_act * gate * sig).astype(BF16)

    @pl.loop(0, D // td)
    def _(t):
        a = pl.ds(pl.multiple_of(t * td, 128), td)
        put(din_ref, a, mm_nt(dgu[rows, :], up[a, :]).astype(BF16))

    @pl.when(step == steps - 1)
    def _():
        @pl.loop(0, D // td)
        def _(t):
            a = pl.ds(pl.multiple_of(t * td, 128), td)
            gup[a, :] = mm(x_t[a, :], dgu[...]).astype(BF16)

        @pl.loop(0, W // tw)
        def _(t):
            a = pl.ds(pl.multiple_of(t * tw, 128), tw)
            gdn[a, :] = mm(act_t[a, :], dy[...]).astype(BF16)

        if g_mode == "whole":
            pairs = [(gup, out_refs[0]), (gdn, out_refs[1])]
        else:
            pairs = shard(gup, gdn, info[0], out_refs[0])
            pairs += by_distance(gup, gdn, out_refs[1:], 1)
        copies = copies_of(pairs)
        for copy in copies:
            copy.start()
        for copy in copies:
            copy.wait()


def weight_grad_kernel(
    planes, att_ref, db_ref, x_ref, dq_ref, all_ref, pair_ref, out_ref, total, grads, sems
):
    step = pl.program_id(0)
    D, width = x_ref.shape[1], dq_ref.shape[1]
    td = 256

    @pl.when(step == 0)
    def _():
        total[...] = jnp.zeros_like(total)

        @pl.loop(0, D // td)
        def _(t):
            a = pl.ds(pl.multiple_of(t * td, 128), td)
            grads[a, :D] = mm_tn(att_ref[:, a], db_ref[...]).astype(BF16)
            grads[a, D : D + width] = mm_tn(x_ref[:, a], dq_ref[...]).astype(BF16)

    total[...] += mm_tn(pair_ref[...], all_ref[...])

    @pl.when(step == pl.num_programs(0) - 1)
    def _():
        @pl.loop(0, D // td)
        def _(t):
            a = pl.ds(pl.multiple_of(t * td, 128), td)
            grads[a, D + width :] = total[:, a].T.astype(BF16)

        ctx = sems.shape[0] // planes
        cut = D // (planes * ctx)
        copies = []
        for f in range(planes):
            for c in range(ctx):
                source = grads.at[pl.ds((f * ctx + c) * cut, cut)]
                target = out_ref.at[pl.ds((c * planes + f) * cut, cut)]
                copies.append(pltpu.make_async_copy(source, target, sems.at[len(copies)]))
        for copy in copies:
            copy.start()
        for copy in copies:
            copy.wait()


def weight_grads(att, db, x, dq, every_x, pairs, ctx_count, planes):
    rows, D = x.shape
    width, wide = dq.shape[1], pairs.shape[1]
    return pl.pallas_call(
        lambda *refs: weight_grad_kernel(planes, *refs),
        grid=(ctx_count,),
        in_specs=[
            pl.BlockSpec((rows, D), lambda i: (0, 0)),
            pl.BlockSpec((rows, D), lambda i: (0, 0)),
            pl.BlockSpec((rows, D), lambda i: (0, 0)),
            pl.BlockSpec((rows, width), lambda i: (0, 0)),
            pl.BlockSpec((rows, D), lambda i: (i, 0)),
            pl.BlockSpec((rows, wide), lambda i: (i, 0)),
        ],
        out_specs=pl.BlockSpec(memory_space=pl.ANY),
        out_shape=jax.ShapeDtypeStruct((D, D + width + wide), BF16),
        scratch_shapes=[
            pltpu.VMEM((wide, D), F32),
            pltpu.VMEM((D, D + width + wide), BF16),
            pltpu.SemaphoreType.DMA((planes * ctx_count,)),
        ],
        compiler_params=pltpu.CompilerParams(vmem_limit_bytes=VMEM_LIMIT),
        cost_estimate=pl.CostEstimate(
            flops=4 * rows * D * (D + width + ctx_count * wide),
            bytes_accessed=2 * ctx_count * rows * D,
            transcendentals=0,
        ),
    )(att, db, x, dq, every_x, pairs)


def input_back_kernel(
    dq_ref, terms_ref, w_ref, x_ref, inverse_ref, gain_ref, upstream_ref, out_ref, gain_out
):
    width = dq_ref.shape[1]
    pairs = jnp.sum(terms_ref[:, 0].astype(F32), axis=0).astype(BF16)
    grad = mm_nt(dq_ref[...], w_ref[:, :width]) + mm_nt(pairs, w_ref[:, width:])
    values, inverse = x_ref[...].astype(F32), inverse_ref[...]

    @pl.when(pl.program_id(0) == 0)
    def _():
        gain_out[...] = jnp.zeros_like(gain_out)

    gain_out[...] += jnp.sum(grad * values * inverse, axis=0, keepdims=True)
    scaled = grad * gain_ref[...]
    projected = jnp.mean(scaled * values, axis=-1, keepdims=True)
    out_ref[...] = upstream_ref[...] + inverse * scaled - values * inverse**3 * projected


def input_back(dq, terms, w, x, inverse, gain, upstream):
    ctx_count, nseq, tl, wide = terms.shape
    rows, D = x.shape
    return pl.pallas_call(
        input_back_kernel,
        grid=(nseq,),
        in_specs=[
            pl.BlockSpec((tl, dq.shape[1]), lambda i: (i, 0)),
            pl.BlockSpec((ctx_count, 1, tl, wide), lambda i: (0, i, 0, 0)),
            pl.BlockSpec(w.shape, lambda i: (0, 0)),
            pl.BlockSpec((tl, D), lambda i: (i, 0)),
            pl.BlockSpec((tl, 1), lambda i: (i, 0)),
            pl.BlockSpec((1, D), lambda i: (0, 0)),
            pl.BlockSpec((tl, D), lambda i: (i, 0)),
        ],
        out_specs=[
            pl.BlockSpec((tl, D), lambda i: (i, 0)),
            pl.BlockSpec((1, D), lambda i: (0, 0)),
        ],
        out_shape=[
            jax.ShapeDtypeStruct((rows, D), F32),
            jax.ShapeDtypeStruct((1, D), F32),
        ],
        compiler_params=pltpu.CompilerParams(vmem_limit_bytes=VMEM_LIMIT),
        cost_estimate=pl.CostEstimate(
            flops=8 * rows * w.size, bytes_accessed=16 * rows * D, transcendentals=0
        ),
    )(dq, terms, w, x, inverse, gain, upstream)


def blank(shapes):
    return pl.pallas_call(
        lambda *refs: None,
        out_specs=[pl.BlockSpec(memory_space=pl.ANY)] * len(shapes),
        out_shape=[jax.ShapeDtypeStruct(shape, F32) for shape in shapes],
    )()


MODE_REFS = {"whole": 2, "parts": 7}
GRAD_REFS = {"whole": 2, "parts": 6}


def run_expert(piece, W, ins, weights, info, w_mode, g_mode):
    C, mine, slots, wide = ins[0].shape
    D = (wide - HD) // 2
    sides = len(ins)
    per_step = C
    while per_step > 1 and (per_step * sides * slots > 640 or C % per_step):
        per_step -= 1
    tile = per_step * sides * slots
    rows = C * sides * slots

    def spec(width, at):
        return pl.BlockSpec((per_step, 1, slots, width), lambda i, info: (i, at, 0, 0))

    def out_spec(width):
        return pl.BlockSpec((per_step, sides, slots, width), lambda i, info: (i, 0, 0, 0))

    any_spec = pl.BlockSpec(memory_space=pl.ANY)
    if g_mode == "whole":
        grads = [(D, 2 * W), (W, D)]
    else:
        grads = [(n * W // 4, D) for n in (3, 3, 1, 1, 1, 3)]
    grads = [jax.ShapeDtypeStruct(shape, BF16) for shape in grads]
    return pl.pallas_call(
        lambda *refs: expert_kernel(sides, w_mode, g_mode, *refs),
        grid_spec=pltpu.PrefetchScalarGridSpec(
            num_scalar_prefetch=1,
            grid=(C // per_step,),
            in_specs=[spec(wide, piece)] * sides
            + [any_spec] * len(weights),
            out_specs=[out_spec(D), out_spec(D + HD)] + [any_spec] * len(grads),
            scratch_shapes=[
                pltpu.VMEM((D, 2 * W), BF16),
                pltpu.VMEM((W, D), BF16),
                pltpu.VMEM((D, rows), BF16),
                pltpu.VMEM((W, rows), BF16),
                pltpu.VMEM((rows, 2 * W), BF16),
                pltpu.VMEM((rows, D), BF16),
                pltpu.VMEM((tile, W), BF16),
                pltpu.VMEM((tile, 2 * W), F32),
                pltpu.VMEM((tile, D), BF16),
                pltpu.VMEM((D, 2 * W), BF16),
                pltpu.VMEM((W, D), BF16),
                pltpu.SemaphoreType.DMA((12,)),
            ],
        ),
        out_shape=[jax.ShapeDtypeStruct((C, sides, slots, n), BF16) for n in (D, D + HD)]
        + grads,
        compiler_params=pltpu.CompilerParams(vmem_limit_bytes=VMEM_LIMIT),
        cost_estimate=pl.CostEstimate(
            flops=38 * rows * D * W,
            bytes_accessed=8 * rows * D + 24 * D * W,
            transcendentals=2 * rows * W,
        ),
    )(info, *ins, *weights)


def local(
    tokens,
    lengths,
    expert_picks,
    router_weights,
    first_gain,
    second_gain,
    query_weight,
    key_weight,
    value_weight,
    output_weight,
    up_weight,
    down_weight,
    cotangent,
):
    batches, seqs_here, tl, D = tokens.shape
    C = lax.axis_size("ctx")
    F = lax.axis_size("fsdp")
    c = lax.axis_index("ctx")
    f = lax.axis_index("fsdp")
    split = max(1, C // EXPERTS)
    pieces = up_weight.shape[0]
    W = up_weight.shape[2] // 2
    merged = pieces % 2 == 0 and F == 4 and 2 * W == D
    share = 2 if merged else 1
    mine = pieces // share
    role = f % share
    nseq = batches * seqs_here
    cap = max(2, (5 * tl * TOP + 4 * EXPERTS - 1) // (4 * EXPERTS))
    while nseq * cap % 16:
        cap += 1
    slots = nseq * cap
    rows = nseq * tl
    L = C * tl
    width = H * HD
    Dl = query_weight.shape[0]
    cut = Dl // C

    positions = c * tl + jnp.arange(tl, dtype=jnp.int32)
    tables = angle_tables(positions)
    all_tables = angle_tables(jnp.arange(L, dtype=jnp.int32))
    lens = lengths.reshape(nseq)
    live = (positions[None, :] < lens[:, None]).reshape(rows)
    live_rows = live.astype(F32)[:, None]

    def gate(*values):
        return lax.optimization_barrier(values)

    def shift(block, k):
        return lax.ppermute(block, "fsdp", [(i, (i + k) % F) for i in range(F)])

    def fsdp_gather(block):
        got = [shift(block, k) for k in range(F - 1, 0, -1)]
        ring = jnp.stack(got + [block] + got)
        return lax.dynamic_slice_in_dim(ring, F - 1 - f, F, 0)

    def fsdp_scatter_sum(parts):
        total = lax.dynamic_index_in_dim(parts, f, 0, keepdims=False).astype(F32)
        for k in range(1, F):
            block = lax.dynamic_index_in_dim(parts, (f + k) % F, 0, keepdims=False)
            total = total + shift(block, k).astype(F32)
        return total

    def swap(block):
        return lax.ppermute(block, "fsdp", [(i, i ^ 1) for i in range(F)])

    def exchange(blocks):
        return lax.all_to_all(blocks, "ctx", 0, 0, tiled=True)

    def ctx_gather(lines):
        return lax.all_gather(lines, "ctx", axis=1, tiled=True).reshape(D, -1)

    def part_of(weight):
        return lax.dynamic_slice_in_dim(weight, c * cut, cut, 0)

    key_part, value_part = part_of(key_weight), part_of(value_weight)
    qkv_part = [part_of(query_weight)]
    for h in range(KV):
        qkv_part += [part[:, h * HD : (h + 1) * HD] for part in (key_part, value_part)]
    qkv_part = jnp.concatenate(qkv_part, axis=1)
    out_part, gain_parts = part_of(output_weight), jnp.stack([first_gain, second_gain])
    qkv_lines = fsdp_gather(qkv_part)

    messages, operands = {}, {}
    expert_in = [up_weight, down_weight]

    def shard_of(at):
        return jnp.concatenate(
            [lax.dynamic_index_in_dim(x, at, 0, keepdims=False) for x in expert_in]
        )

    def operand(name):
        if name in operands:
            return operands[name]
        j = "wv".index(name[0])
        block = shard_of((role if name[1] == "2" else 1 - role) * mine + j)
        third = block.shape[0] // 3
        at = "abc".find(name[2:]) * third if name[2:] else 0
        return block[at : at + third] if name[2:] else block

    def send(name, block):
        return shift(block, int(name[1]))

    def step(need, values, go):
        if not merged:
            return lax.optimization_barrier(values)
        fresh = tuple(operand(name) for name in go)
        got, values, fresh = lax.optimization_barrier(
            (tuple(messages[name] for name in need), values, fresh)
        )
        messages.update(zip(need, got))
        messages.update((name, send(name, block)) for name, block in zip(go, fresh))
        return values

    picks = expert_picks.reshape(rows, TOP)
    gates = router_weights.reshape(rows, TOP)
    cot = cotangent.reshape(rows, D)
    expert_ids = jnp.arange(EXPERTS, dtype=jnp.int32)
    hit = picks[:, :, None] == expert_ids
    by_expert = jnp.sum(jnp.where(hit, gates[:, :, None], 0.0), axis=1) * live_rows
    high = by_expert.astype(BF16)
    low = (by_expert - high.astype(F32)).astype(BF16)
    gap = jnp.zeros((rows, HD // 2 - EXPERTS), BF16)
    table = jnp.concatenate([high, gap, low, gap], axis=1)
    number = jnp.arange(C)[:, None] * pieces + role * mine + jnp.arange(mine)[None, :]
    expert_of = (number // split).reshape(C * mine)
    earlier = jnp.tril(jnp.ones((tl, tl), BF16), -1)
    pick_map = (expert_ids[:, None] == expert_of[None, :]).astype(BF16)

    def route(table):
        match = table[:, :EXPERTS] > 0
        ranks = jnp.einsum(
            "ab,sbe->sae",
            earlier,
            match.astype(BF16).reshape(nseq, tl, -1),
            preferred_element_type=F32,
        )
        base = (jnp.arange(nseq) * cap)[:, None, None]
        code = jnp.where(match, (ranks + base).reshape(rows, -1), -1.0).astype(BF16)
        code = mm_tn(pick_map, code.T)
        chosen = code[:, None, :] == jnp.arange(slots, dtype=F32)[None, :, None]
        return chosen.astype(BF16).reshape(C, mine, slots, rows)

    def to_slots(sel, source):
        out = mm(sel.reshape(C * mine * slots, rows), source)
        return out.astype(BF16).reshape(C, mine, slots, -1)

    inputs = tokens.reshape(rows, D).astype(F32)
    step([], (qkv_part,), ["w1"])
    _, gain_parts, table, cot, out_part = gate(qkv_lines, gain_parts, table, cot, out_part)
    gains, out_lines = fsdp_gather(gain_parts), fsdp_gather(out_part)
    sels = [route(table)]
    qkv_full, sels[0], table, out_lines, cot_wide, all_tables = step(
        ["w1"],
        (
            ctx_gather(qkv_lines),
            sels[0],
            table,
            out_lines,
            jnp.concatenate([cot, table], axis=1),
            all_tables,
        ),
        ["w3"],
    )
    first_scale = gains[:, 0].reshape(D).astype(F32)
    second_scale = gains[:, 1].reshape(D).astype(F32)
    normed, inverse_one = norm_forward(inputs, first_scale)
    normed_low = normed.astype(BF16)
    kv_low = key_values(normed_low, qkv_full, tables, nseq)
    kv_all = lax.all_gather(kv_low, "ctx", axis=1, tiled=True)
    _, expert_in, qkv_full, table = gate(kv_low, expert_in, qkv_full, table)
    query_pre = mm(normed_low, qkv_full[:, :width]).reshape(nseq, tl, width)
    info = jnp.concatenate([(c * tl)[None], lens])
    kv_all, query_pre, out_lines, table = step(
        ["w3"], (kv_all, query_pre, out_lines, table), ["w2a"]
    )
    far_table = swap(table) if share == 2 else table
    out_full = ctx_gather(out_lines)
    attended, lse, queries = attention(query_pre, kv_all, info, tables)
    attended, cot_wide, far_table = step(["w2a"], (attended, cot_wide, far_table), [])
    attended_low = attended.reshape(rows, width)
    hidden = inputs + live_rows * mm(attended_low, out_full)
    second, inverse_two = norm_forward(hidden, second_scale)
    second_low = second.astype(BF16)

    second_low, cot_wide = step([], (second_low, cot_wide), ["w2b", "w2c"])
    wide_rows = jnp.concatenate([second_low, cot_wide], axis=1)
    expert_rows = [exchange(to_slots(sels[0], wide_rows))]
    shards = None
    if merged:
        far_rows = swap(wide_rows)
        sels.append(route(far_table))
        shards = list(blank([(pieces, Dl, 2 * W), (pieces, W // F, D)]))
        far_rows, expert_rows[0], sels[1], shards = step(
            ["w2b", "w2c"], (far_rows, expert_rows[0], sels[1], shards), ["v1", "v3", "v2a"]
        )
        expert_rows.append(exchange(to_slots(sels[1], far_rows)))

    def expert(j):
        at = role * mine + j
        expert_info = jnp.stack([f, (c * pieces + at) // split, at])
        if not merged:
            return run_expert(j, W, expert_rows, [up_full, down_full], expert_info, "whole", "whole")
        names = ["wv"[j] + k for k in ("1", "2a", "2b", "2c", "3")]
        weights = [up_weight, down_weight] + [messages[name] for name in names]
        out = run_expert(j, W, expert_rows, weights, expert_info, "parts", "parts")
        for k, grad in zip(("0", "1", "2a", "2b", "2c", "3"), out[2:]):
            operands["pq"[j] + k] = grad
        return out

    if merged:
        expert_rows[1], normed_mine = step(
            ["v1", "v3", "v2a"], (expert_rows[1], normed_low), ["v2b", "v2c"]
        )
        every_normed = lax.all_gather(normed_mine, "ctx", axis=0, tiled=True)
        outs = [expert(0)]
        d_in, mixed = [outs[0][0]], [outs[0][1]]
        d_in[0], expert_rows[0], mixed[0] = step(
            ["v2b", "v2c"], (d_in[0], expert_rows[0], mixed[0]), ["p1", "p2a"]
        )
        d_in[0] = exchange(d_in[0])
        outs.append(expert(1))
        last, d_in[0], later, every_normed = step(
            ["p1", "p2a"], (outs[1][0], d_in[0], outs[1][1], every_normed), ["p3"]
        )
        d_in.append(exchange(last))
        mixed.append(later)
    else:
        up_full = lax.all_gather(up_weight, "fsdp", axis=1, tiled=True)
        down_full = lax.all_gather(down_weight, "fsdp", axis=1, tiled=True)
        outs = [expert(j) for j in range(mine)]
        d_in = [exchange(out[0]) for out in outs]
        mixed = [exchange(out[1]) for out in outs]

    def collect(backs):
        sums = []
        for i, sel in enumerate(sels):
            total = 0.0
            for j, back in enumerate(backs):
                total = total + mm_tn(
                    sel[:, j].reshape(C * slots, rows), back[:, i].reshape(C * slots, -1)
                )
            sums.append(total)
        return sums

    def fill(at, total):
        for i, block in enumerate((total[:Dl], total[Dl:])):
            shards[i] = lax.dynamic_update_slice(shards[i], block[None], (at, 0, 0))

    def pair_sum(first, *others):
        far = jnp.concatenate([messages[name] for name in others])
        return first.astype(F32) + far.astype(F32)

    sums = collect(d_in)
    dispatch_grad = sums[0]
    if share == 2:
        far, mixed[0] = step(["p3"], (sums[1].astype(BF16), mixed[0]), ["p2b"])
        dispatch_grad = dispatch_grad + swap(far).astype(F32)
        mixed[0] = exchange(mixed[0])
        (dispatch_grad,) = step(["p2b"], (dispatch_grad,), [])

    upstream = cot.astype(F32)
    norm_grad, second_grads = norm_backward(hidden, inverse_two, second_scale, dispatch_grad)
    hidden_grad = upstream + norm_grad
    branch_grad = (live_rows * hidden_grad).astype(BF16)
    def by_target(grad):
        return grad.astype(BF16).reshape(F, C, cut, -1).transpose(1, 0, 2, 3)

    def over_ctx(blocks):
        return jnp.sum(exchange(blocks).astype(F32), axis=0).astype(BF16)

    def scatter(blocks):
        (blocks,) = gate(blocks.reshape(D, -1))
        total = lax.psum_scatter(blocks, "ctx", scatter_dimension=0, tiled=True)
        return gate(total)[0].reshape(F, cut, -1)

    d_att = mm_nt(branch_grad, out_full).astype(BF16)
    if merged:
        d_att, mixed[0], mixed[1] = step([], (d_att, mixed[0], mixed[1]), ["p2c"])
        mixed[1] = exchange(mixed[1])
    query_back, terms = attention_back(
        queries, kv_all, d_att.reshape(nseq, tl, width), lse, info, all_tables, C
    )
    query_back = query_back.reshape(rows, width)
    terms, query_back = step(["p2c"], (terms, query_back), ["q2a"])
    if merged:
        own_terms = exchange(terms)
        flat_terms = terms.reshape(C * rows, -1)
        blocks = weight_grads(
            attended_low, branch_grad, normed_low, query_back, every_normed, flat_terms, C, F
        )
        blocks, mixed = step(["q2a"], (blocks, mixed), ["q2b", "q2c"])
        mixed_sums = collect(mixed)
        far = swap(mixed_sums[1].astype(BF16))
        own_terms, shards, far = step(["q2b", "q2c"], (own_terms, shards, far), ["q1"])
    else:
        own_terms = over_ctx(terms)
        pair_grad = mm_tn(normed_low, own_terms.reshape(rows, 2 * KV * HD))
        query_grad = mm_tn(normed_low, query_back)
        projection_grad = mm_tn(attended_low, branch_grad)
        blocks = by_target(jnp.concatenate([projection_grad, query_grad, pair_grad], axis=1))
        mixed_rows = collect(mixed)[0]
    weight_rows = scatter(blocks)
    if not merged:
        own_terms = own_terms.reshape((1,) + terms.shape[1:])
    grad_tokens, first_grads = input_back(
        query_back,
        own_terms,
        qkv_full,
        tokens.reshape(rows, D),
        inverse_one,
        first_scale[None],
        hidden_grad,
    )
    first_grads = first_grads[0]
    if merged:
        fill(role * mine, pair_sum(operands["p0"], "p2a", "p2b", "p2c"))
        fill((1 - role) * mine, pair_sum(messages["p1"], "p3"))
        fill(role * mine + 1, pair_sum(operands["q0"], "q2a", "q2b", "q2c"))
        first_grads, mixed_sums[0], shards = step(["q1"], (first_grads, mixed_sums[0], shards), [])
    gain_columns = jnp.stack([first_grads, second_grads]).reshape(2, F, Dl).transpose(1, 0, 2)
    gain_columns = gain_columns.reshape(F, cut, -1)
    gain_count = gain_columns.shape[2]
    gain_columns = jnp.pad(gain_columns, ((0, 0), (0, 0), (0, -gain_count % HD)))
    weight_rows, gain_columns = gate(weight_rows, gain_columns)
    wide = jnp.concatenate([weight_rows, gain_columns.astype(BF16)], axis=2)
    wide = fsdp_scatter_sum(wide).astype(BF16)
    if merged:
        wide, far = step([], (wide, far), ["q3"])
        mixed_rows = mixed_sums[0] + far.astype(F32)
    wide = lax.all_gather(wide, "ctx", axis=0, tiled=False)
    whole = wide[:, :, : D + width + 2 * KV * HD].reshape(Dl, -1).astype(F32)
    grad_projection, grad_query = whole[:, :D], whole[:, D : D + width]
    grad_pairs = whole[:, D + width :].reshape(Dl, KV, 2, HD)
    gain_at = D + width + 2 * KV * HD
    gain_sums = jnp.sum(wide[:, :, gain_at : gain_at + gain_count].astype(F32), axis=0)
    grad_first, grad_second = gain_sums.reshape(2, Dl)

    grads = (grad_projection, grad_query, grad_pairs, grad_first, grad_second)
    grads = step(["q3"], grads, [])
    grad_projection, grad_query, grad_pairs, grad_first, grad_second = grads
    block_rows = (hidden + mixed_rows[:, :D]).astype(BF16)
    router_by_expert = mixed_rows[:, D : D + EXPERTS]
    grad_router = jnp.sum(jnp.where(hit, router_by_expert[:, None, :], 0.0), axis=2)

    if merged:
        fill((1 - role) * mine + 1, pair_sum(messages["q1"], "q3"))
        grad_up, grad_down = shards
    else:
        grad_up, grad_down = [
            lax.psum_scatter(
                jnp.stack([out[2 + i] for out in outs]), "fsdp", scatter_dimension=1, tiled=True
            ).astype(F32)
            for i in range(2)
        ]

    shape = (batches, seqs_here, tl)
    return (
        block_rows.reshape(shape + (D,)),
        grad_tokens.reshape(shape + (D,)),
        grad_router.reshape(shape + (TOP,)),
        grad_first,
        grad_second,
        grad_query,
        grad_pairs[:, :, 0].reshape(Dl, KV * HD),
        grad_pairs[:, :, 1].reshape(Dl, KV * HD),
        grad_projection,
        grad_up,
        grad_down,
    )


def solution(mesh):
    rows = P(None, "fsdp", "ctx", None)
    weight = P("fsdp", None)
    expert = P("ctx", "fsdp", None)
    placed = (rows, P(None, "fsdp"), rows, rows, P("fsdp"), P("fsdp"))
    placed = placed + (weight,) * 4 + (expert,) * 2 + (rows,)
    outs = (rows, rows, rows, P("fsdp"), P("fsdp")) + (weight,) * 4 + (expert,) * 2
    return jax.shard_map(local, mesh=mesh, in_specs=placed, out_specs=outs, check_vma=False)
```

```python
import jax
import jax.numpy as jnp
from jax import lax
from jax.experimental import pallas as pl
from jax.experimental.pallas import tpu as pltpu
from jax.sharding import PartitionSpec as P

H = 12
KV = 2
HD = 128
TOP = 4
EXPERTS = 32
EPSILON = 1e-06
ROPE_BASE = 10000.0
NEGATIVE = -1e30
F32 = jnp.float32
BF16 = jnp.bfloat16


def angle_tables(positions):
    frequency = ROPE_BASE ** (-(jnp.arange(HD // 2, dtype=F32) * 2.0 / HD))
    angles = positions.astype(F32)[:, None] * frequency[None, :]
    cosine, sine = jnp.cos(angles), jnp.sin(angles)
    return jnp.concatenate([cosine, cosine], 1), jnp.concatenate([-sine, sine], 1)


def turn(vectors, cosine, sine):
    return vectors * cosine + pltpu.roll(vectors, HD // 2, 1) * sine


def norm_forward(values, gain_row):
    inverse = lax.rsqrt(jnp.mean(values * values, axis=-1, keepdims=True) + EPSILON)
    return values * inverse * gain_row, inverse


def norm_backward(values, inverse, gain_row, upstream):
    gain_grad = jnp.sum(upstream * values * inverse, axis=0)
    scaled = upstream * gain_row
    projected = jnp.mean(scaled * values, axis=-1, keepdims=True)
    return inverse * scaled - values * inverse**3 * projected, gain_grad


def mm(a, b):
    return jnp.dot(a, b, preferred_element_type=F32)


def mm_nt(a, b):
    return lax.dot_general(a, b, (((1,), (1,)), ((), ())), preferred_element_type=F32)


def mm_tn(a, b):
    return lax.dot_general(a, b, (((0,), (0,)), ((), ())), preferred_element_type=F32)


VMEM_LIMIT = 60 * 1024 * 1024


def stack_heads(block, groups):
    return jnp.concatenate([block[:, h * HD : (h + 1) * HD] for h in range(groups)], axis=0)


def masked_scores(stacked, keys, first, length, groups):
    tl = stacked.shape[0] // groups
    total = keys.shape[0]
    scores = mm_nt(stacked, keys) * HD ** (-0.5)
    key_at = lax.broadcasted_iota(jnp.int32, (tl, total), 1)
    query_at = lax.broadcasted_iota(jnp.int32, (tl, total), 0) + first
    allowed = (key_at <= query_at) & (key_at < length)
    scores = scores.reshape(groups, tl, total)
    return jnp.where(allowed[None], scores, NEGATIVE).reshape(groups * tl, total)


def key_value_kernel(x_ref, w_ref, cos_ref, sin_ref, out_ref):
    both = mm(x_ref[...], w_ref[...])
    cosine, sine = cos_ref[...], sin_ref[...]
    for h in range(KV):
        key = turn(both[:, 2 * h * HD : (2 * h + 1) * HD], cosine, sine)
        out_ref[0, :, 2 * h * HD : (2 * h + 1) * HD] = key.astype(BF16)
        value = both[:, (2 * h + 1) * HD : (2 * h + 2) * HD]
        out_ref[0, :, (2 * h + 1) * HD : (2 * h + 2) * HD] = value.astype(BF16)


def key_values(normed_low, qkv_full, tables, nseq):
    rows, D = normed_low.shape
    tl, wide = rows // nseq, 2 * KV * HD
    return pl.pallas_call(
        key_value_kernel,
        grid=(nseq,),
        in_specs=[
            pl.BlockSpec((tl, D), lambda s: (s, 0)),
            pl.BlockSpec((D, wide), lambda s: (0, H * HD // wide)),
            pl.BlockSpec((tl, HD), lambda s: (0, 0)),
            pl.BlockSpec((tl, HD), lambda s: (0, 0)),
        ],
        out_specs=pl.BlockSpec((1, tl, wide), lambda s: (s, 0, 0)),
        out_shape=jax.ShapeDtypeStruct((nseq, tl, wide), BF16),
        compiler_params=pltpu.CompilerParams(vmem_limit_bytes=VMEM_LIMIT),
        cost_estimate=pl.CostEstimate(
            flops=4 * rows * D * wide, bytes_accessed=2 * D * wide, transcendentals=0
        ),
    )(normed_low, qkv_full, *tables)


def attend_kernel(groups, info, q_ref, kv_ref, cos_ref, sin_ref, att_ref, lse_ref, turned_ref):
    tl = q_ref.shape[1]
    cosine, sine = cos_ref[...], sin_ref[...]
    for h in range(groups):
        at = slice(h * HD, (h + 1) * HD)
        turned_ref[0, :, at] = turn(q_ref[0, :, at], cosine, sine).astype(BF16)
    stacked = stack_heads(turned_ref[0], groups)
    scores = masked_scores(
        stacked, kv_ref[0, :, :HD], info[0], info[1 + pl.program_id(0)], groups
    )
    top = jnp.max(scores, axis=-1, keepdims=True)
    shares = jnp.exp(scores - top)
    total = jnp.sum(shares, axis=-1, keepdims=True)
    out = mm(shares.astype(BF16), kv_ref[0, :, HD:]) / total
    lse = top + jnp.log(total)
    for h in range(groups):
        at = slice(h * tl, (h + 1) * tl)
        att_ref[0, :, h * HD : (h + 1) * HD] = out[at].astype(BF16)
        lse_ref[0, 0, :, h : h + 1] = lse[at]


def attend_back_kernel(
    groups, info, q_ref, kv_ref, da_ref, lse_ref, cos_ref, sin_ref, dq_ref, dkv_ref
):
    tl = q_ref.shape[1]
    keys, values = kv_ref[0, :, :HD], kv_ref[0, :, HD:]
    stacked = stack_heads(q_ref[0], groups)
    scores = masked_scores(stacked, keys, info[0], info[1 + pl.program_id(0)], groups)
    lse = jnp.concatenate([lse_ref[0, 0, :, h : h + 1] for h in range(groups)], axis=0)
    probs = jnp.exp(scores - lse)
    grads = stack_heads(da_ref[0], groups)
    d_probs = mm_nt(grads, values)
    delta = jnp.sum(probs * d_probs, axis=-1, keepdims=True)
    d_scores = (probs * (d_probs - delta)).astype(BF16)
    dq = mm(d_scores, keys) * HD ** (-0.5)
    here = pl.ds(pl.multiple_of(info[0], 8), tl)
    cosine, sine = cos_ref[here, :], -sin_ref[here, :]
    for h in range(groups):
        turned = turn(dq[h * tl : (h + 1) * tl], cosine, sine)
        dq_ref[0, :, h * HD : (h + 1) * HD] = turned.astype(BF16)
    dk = mm_tn(d_scores, stacked) * HD ** (-0.5)
    dk = turn(dk, cos_ref[...], -sin_ref[...])
    dv = mm_tn(probs.astype(BF16), grads)
    shape = dkv_ref.shape[:1] + (tl, HD)
    dkv_ref[:, 0, :, :HD] = dk.reshape(shape).astype(BF16)
    dkv_ref[:, 0, :, HD:] = dv.reshape(shape).astype(BF16)


def attention(queries, kv_all, info, tables):
    nseq, tl, width = queries.shape
    total = kv_all.shape[1]
    groups = H // KV
    return pl.pallas_call(
        lambda *refs: attend_kernel(groups, *refs),
        grid_spec=pltpu.PrefetchScalarGridSpec(
            num_scalar_prefetch=1,
            grid=(nseq, KV),
            in_specs=[
                pl.BlockSpec((1, tl, groups * HD), lambda s, n, info: (s, 0, n)),
                pl.BlockSpec((1, total, 2 * HD), lambda s, n, info: (s, 0, n)),
                pl.BlockSpec((tl, HD), lambda s, n, info: (0, 0)),
                pl.BlockSpec((tl, HD), lambda s, n, info: (0, 0)),
            ],
            out_specs=[
                pl.BlockSpec((1, tl, groups * HD), lambda s, n, info: (s, 0, n)),
                pl.BlockSpec((1, 1, tl, HD), lambda s, n, info: (s, n, 0, 0)),
                pl.BlockSpec((1, tl, groups * HD), lambda s, n, info: (s, 0, n)),
            ],
        ),
        out_shape=[
            jax.ShapeDtypeStruct((nseq, tl, width), BF16),
            jax.ShapeDtypeStruct((nseq, KV, tl, HD), F32),
            jax.ShapeDtypeStruct((nseq, tl, width), BF16),
        ],
        compiler_params=pltpu.CompilerParams(vmem_limit_bytes=VMEM_LIMIT),
        cost_estimate=pl.CostEstimate(
            flops=28 * nseq * tl * width * total,
            bytes_accessed=4 * queries.size * 2 + 2 * kv_all.size,
            transcendentals=nseq * H * tl * total,
        ),
    )(info, queries, kv_all, *tables)


def attention_back(queries, kv_all, d_att, lse, info, tables, ctx_count):
    nseq, tl, width = queries.shape
    total = kv_all.shape[1]
    groups = H // KV
    return pl.pallas_call(
        lambda *refs: attend_back_kernel(groups, *refs),
        grid_spec=pltpu.PrefetchScalarGridSpec(
            num_scalar_prefetch=1,
            grid=(nseq, KV),
            in_specs=[
                pl.BlockSpec((1, tl, groups * HD), lambda s, n, info: (s, 0, n)),
                pl.BlockSpec((1, total, 2 * HD), lambda s, n, info: (s, 0, n)),
                pl.BlockSpec((1, tl, groups * HD), lambda s, n, info: (s, 0, n)),
                pl.BlockSpec((1, 1, tl, HD), lambda s, n, info: (s, n, 0, 0)),
                pl.BlockSpec((total, HD), lambda s, n, info: (0, 0)),
                pl.BlockSpec((total, HD), lambda s, n, info: (0, 0)),
            ],
            out_specs=[
                pl.BlockSpec((1, tl, groups * HD), lambda s, n, info: (s, 0, n)),
                pl.BlockSpec((ctx_count, 1, tl, 2 * HD), lambda s, n, info: (0, s, 0, n)),
            ],
        ),
        out_shape=[
            jax.ShapeDtypeStruct((nseq, tl, width), BF16),
            jax.ShapeDtypeStruct((ctx_count, nseq, tl, KV * 2 * HD), BF16),
        ],
        compiler_params=pltpu.CompilerParams(vmem_limit_bytes=VMEM_LIMIT),
        cost_estimate=pl.CostEstimate(
            flops=36 * nseq * tl * width * total,
            bytes_accessed=6 * queries.size * 2 + 4 * kv_all.size,
            transcendentals=nseq * H * tl * total,
        ),
    )(info, queries, kv_all, d_att, lse, *tables)


def expert_kernel(sides, w_mode, g_mode, *refs):
    info = refs[0]
    ins = refs[1 : 1 + sides]
    count = MODE_REFS[w_mode]
    weights = refs[1 + sides : 1 + sides + count]
    at = 1 + sides + count
    din_ref, wy_ref = refs[at : at + 2]
    at = at + 2
    out_refs = refs[at : at + GRAD_REFS[g_mode]]
    at = at + GRAD_REFS[g_mode]
    up, down, x_t, act_t, dgu, dy, act_s, pre, wide, gup, gdn, sems = refs[at:]
    step, steps = pl.program_id(0), pl.num_programs(0)
    D, W = up.shape[0], down.shape[0]
    tile = wide.shape[0]
    tw = 256 if W % 256 == 0 else 128
    td = 256

    wl = W // 4
    dl = 2 * wl

    def shard(up_side, down_side, source, block, first=0):
        pairs, count = [], block.shape[0]
        ups = min(count, dl - first)
        if ups > 0:
            at = pl.ds(pl.multiple_of(source * dl + first, 16), ups)
            pairs.append((up_side.at[at], block.at[pl.ds(0, ups)]))
        if ups < count:
            skip = max(0, ups)
            at = pl.ds(pl.multiple_of(source * wl + first + skip - dl, 16), count - skip)
            pairs.append((down_side.at[at], block.at[pl.ds(skip, count - skip)]))
        return pairs

    def by_distance(up_side, down_side, blocks, sign):
        pairs = []
        for block, k, first in zip(blocks, (1, 2, 2, 2, 3), (0, 0, wl, 2 * wl, 0)):
            source = lax.rem(info[0] + 4 + sign * k, 4)
            pairs += shard(up_side, down_side, source, block, first)
        return pairs

    def copies_of(pairs):
        return [pltpu.make_async_copy(a, b, sems.at[i]) for i, (a, b) in enumerate(pairs)]

    def loads():
        if w_mode == "whole":
            return copies_of([(weights[0].at[info[2]], up), (weights[1].at[info[2]], down)])
        pairs = by_distance(up, down, weights[2:], -1)
        own_up = up.at[pl.ds(pl.multiple_of(info[0] * dl, 16), dl)]
        own_down = down.at[pl.ds(pl.multiple_of(info[0] * wl, 16), wl)]
        pairs += [(own_up, weights[0].at[info[2]]), (own_down, weights[1].at[info[2]])]
        return copies_of([(b, a) for a, b in pairs])

    def put(ref, columns, block):
        per = tile // sides
        shape = (ref.shape[0], ref.shape[2], block.shape[1])
        for i in range(sides):
            ref[:, i, :, columns] = block[i * per : (i + 1) * per].reshape(shape)

    @pl.when(step == 0)
    def _():
        copies = loads()
        for copy in copies:
            copy.start()
        for copy in copies:
            copy.wait()

    rows = pl.ds(pl.multiple_of(step * tile, 128), tile)
    x = jnp.concatenate([r[:, :, :, :D].reshape(-1, D) for r in ins], axis=0)
    g_aug = jnp.concatenate([r[:, :, :, D:].reshape(-1, D + HD) for r in ins], axis=0)
    x_t[:, rows] = x.T
    lane = lax.broadcasted_iota(jnp.int32, (tile, HD), 1)
    picked = (lane == info[1]) | (lane == info[1] + HD // 2)
    w = jnp.sum(jnp.where(picked, g_aug[:, D:].astype(F32), 0.0), axis=1, keepdims=True)
    wide[...] = g_aug[:, :D]
    dy[rows, :] = (g_aug[:, :D].astype(F32) * w).astype(BF16)

    @pl.loop(0, W // tw)
    def _(t):
        a = pl.ds(pl.multiple_of(t * tw, 128), tw)
        b = pl.ds(pl.multiple_of(W + t * tw, 128), tw)
        gate = mm(x, up[:, a])
        lift = mm(x, up[:, b])
        pre[:, a] = gate
        pre[:, b] = lift
        act = gate / (1.0 + jnp.exp(-gate)) * lift
        act = act.astype(BF16)
        act_s[:, a] = act
        act_t[a, rows] = act.T

    def out_step(t, total):
        a = pl.ds(pl.multiple_of(t * td, 128), td)
        y = mm(act_s[...], down[:, a])
        put(wy_ref, a, (y * w).astype(BF16))
        return total + jnp.sum(y * wide[:, a].astype(F32), axis=1, keepdims=True)

    router = lax.fori_loop(0, D // td, out_step, jnp.zeros((tile, 1), F32))
    extra = jnp.where(lane == info[1], router, 0.0).astype(BF16)
    put(wy_ref, pl.ds(D, HD), extra)

    @pl.loop(0, W // tw)
    def _(t):
        a = pl.ds(pl.multiple_of(t * tw, 128), tw)
        b = pl.ds(pl.multiple_of(W + t * tw, 128), tw)
        d_act = mm_nt(dy[rows, :], down[a, :])
        gate, lift = pre[:, a], pre[:, b]
        sig = 1.0 / (1.0 + jnp.exp(-gate))
        dgu[rows, a] = (d_act * lift * sig * (1.0 + gate * (1.0 - sig))).astype(BF16)
        dgu[rows, b] = (d_act * gate * sig).astype(BF16)

    @pl.loop(0, D // td)
    def _(t):
        a = pl.ds(pl.multiple_of(t * td, 128), td)
        put(din_ref, a, mm_nt(dgu[rows, :], up[a, :]).astype(BF16))

    @pl.when(step == steps - 1)
    def _():
        @pl.loop(0, D // td)
        def _(t):
            a = pl.ds(pl.multiple_of(t * td, 128), td)
            gup[a, :] = mm(x_t[a, :], dgu[...]).astype(BF16)

        @pl.loop(0, W // tw)
        def _(t):
            a = pl.ds(pl.multiple_of(t * tw, 128), tw)
            gdn[a, :] = mm(act_t[a, :], dy[...]).astype(BF16)

        if g_mode == "whole":
            pairs = [(gup, out_refs[0]), (gdn, out_refs[1])]
        else:
            pairs = shard(gup, gdn, info[0], out_refs[0])
            pairs += by_distance(gup, gdn, out_refs[1:], 1)
        copies = copies_of(pairs)
        for copy in copies:
            copy.start()
        for copy in copies:
            copy.wait()


def weight_grad_kernel(
    planes, att_ref, db_ref, x_ref, dq_ref, all_ref, pair_ref, out_ref, total, grads, sems
):
    step = pl.program_id(0)
    D, width = x_ref.shape[1], dq_ref.shape[1]
    td = 256

    @pl.when(step == 0)
    def _():
        total[...] = jnp.zeros_like(total)

        @pl.loop(0, D // td)
        def _(t):
            a = pl.ds(pl.multiple_of(t * td, 128), td)
            grads[a, :D] = mm_tn(att_ref[:, a], db_ref[...]).astype(BF16)
            grads[a, D : D + width] = mm_tn(x_ref[:, a], dq_ref[...]).astype(BF16)

    total[...] += mm_tn(pair_ref[...], all_ref[...])

    @pl.when(step == pl.num_programs(0) - 1)
    def _():
        @pl.loop(0, D // td)
        def _(t):
            a = pl.ds(pl.multiple_of(t * td, 128), td)
            grads[a, D + width :] = total[:, a].T.astype(BF16)

        ctx = sems.shape[0] // planes
        cut = D // (planes * ctx)
        copies = []
        for f in range(planes):
            for c in range(ctx):
                source = grads.at[pl.ds((f * ctx + c) * cut, cut)]
                target = out_ref.at[pl.ds((c * planes + f) * cut, cut)]
                copies.append(pltpu.make_async_copy(source, target, sems.at[len(copies)]))
        for copy in copies:
            copy.start()
        for copy in copies:
            copy.wait()


def weight_grads(att, db, x, dq, every_x, pairs, ctx_count, planes):
    rows, D = x.shape
    width, wide = dq.shape[1], pairs.shape[1]
    return pl.pallas_call(
        lambda *refs: weight_grad_kernel(planes, *refs),
        grid=(ctx_count,),
        in_specs=[
            pl.BlockSpec((rows, D), lambda i: (0, 0)),
            pl.BlockSpec((rows, D), lambda i: (0, 0)),
            pl.BlockSpec((rows, D), lambda i: (0, 0)),
            pl.BlockSpec((rows, width), lambda i: (0, 0)),
            pl.BlockSpec((rows, D), lambda i: (i, 0)),
            pl.BlockSpec((rows, wide), lambda i: (i, 0)),
        ],
        out_specs=pl.BlockSpec(memory_space=pl.ANY),
        out_shape=jax.ShapeDtypeStruct((D, D + width + wide), BF16),
        scratch_shapes=[
            pltpu.VMEM((wide, D), F32),
            pltpu.VMEM((D, D + width + wide), BF16),
            pltpu.SemaphoreType.DMA((planes * ctx_count,)),
        ],
        compiler_params=pltpu.CompilerParams(vmem_limit_bytes=VMEM_LIMIT),
        cost_estimate=pl.CostEstimate(
            flops=4 * rows * D * (D + width + ctx_count * wide),
            bytes_accessed=2 * ctx_count * rows * D,
            transcendentals=0,
        ),
    )(att, db, x, dq, every_x, pairs)


def input_back_kernel(
    dq_ref, terms_ref, w_ref, x_ref, inverse_ref, gain_ref, upstream_ref, out_ref, gain_out
):
    width = dq_ref.shape[1]
    pairs = jnp.sum(terms_ref[:, 0].astype(F32), axis=0).astype(BF16)
    grad = mm_nt(dq_ref[...], w_ref[:, :width]) + mm_nt(pairs, w_ref[:, width:])
    values, inverse = x_ref[...].astype(F32), inverse_ref[...]

    @pl.when(pl.program_id(0) == 0)
    def _():
        gain_out[...] = jnp.zeros_like(gain_out)

    gain_out[...] += jnp.sum(grad * values * inverse, axis=0, keepdims=True)
    scaled = grad * gain_ref[...]
    projected = jnp.mean(scaled * values, axis=-1, keepdims=True)
    out_ref[...] = upstream_ref[...] + inverse * scaled - values * inverse**3 * projected


def input_back(dq, terms, w, x, inverse, gain, upstream):
    ctx_count, nseq, tl, wide = terms.shape
    rows, D = x.shape
    return pl.pallas_call(
        input_back_kernel,
        grid=(nseq,),
        in_specs=[
            pl.BlockSpec((tl, dq.shape[1]), lambda i: (i, 0)),
            pl.BlockSpec((ctx_count, 1, tl, wide), lambda i: (0, i, 0, 0)),
            pl.BlockSpec(w.shape, lambda i: (0, 0)),
            pl.BlockSpec((tl, D), lambda i: (i, 0)),
            pl.BlockSpec((tl, 1), lambda i: (i, 0)),
            pl.BlockSpec((1, D), lambda i: (0, 0)),
            pl.BlockSpec((tl, D), lambda i: (i, 0)),
        ],
        out_specs=[
            pl.BlockSpec((tl, D), lambda i: (i, 0)),
            pl.BlockSpec((1, D), lambda i: (0, 0)),
        ],
        out_shape=[
            jax.ShapeDtypeStruct((rows, D), F32),
            jax.ShapeDtypeStruct((1, D), F32),
        ],
        compiler_params=pltpu.CompilerParams(vmem_limit_bytes=VMEM_LIMIT),
        cost_estimate=pl.CostEstimate(
            flops=8 * rows * w.size, bytes_accessed=16 * rows * D, transcendentals=0
        ),
    )(dq, terms, w, x, inverse, gain, upstream)


def blank(shapes):
    return pl.pallas_call(
        lambda *refs: None,
        out_specs=[pl.BlockSpec(memory_space=pl.ANY)] * len(shapes),
        out_shape=[jax.ShapeDtypeStruct(shape, F32) for shape in shapes],
    )()


MODE_REFS = {"whole": 2, "parts": 7}
GRAD_REFS = {"whole": 2, "parts": 6}


def run_expert(piece, W, ins, weights, info, w_mode, g_mode):
    C, mine, slots, wide = ins[0].shape
    D = (wide - HD) // 2
    sides = len(ins)
    per_step = C
    while per_step > 1 and (per_step * sides * slots > 640 or C % per_step):
        per_step -= 1
    tile = per_step * sides * slots
    rows = C * sides * slots

    def spec(width, at):
        return pl.BlockSpec((per_step, 1, slots, width), lambda i, info: (i, at, 0, 0))

    def out_spec(width):
        return pl.BlockSpec((per_step, sides, slots, width), lambda i, info: (i, 0, 0, 0))

    any_spec = pl.BlockSpec(memory_space=pl.ANY)
    if g_mode == "whole":
        grads = [(D, 2 * W), (W, D)]
    else:
        grads = [(n * W // 4, D) for n in (3, 3, 1, 1, 1, 3)]
    grads = [jax.ShapeDtypeStruct(shape, BF16) for shape in grads]
    return pl.pallas_call(
        lambda *refs: expert_kernel(sides, w_mode, g_mode, *refs),
        grid_spec=pltpu.PrefetchScalarGridSpec(
            num_scalar_prefetch=1,
            grid=(C // per_step,),
            in_specs=[spec(wide, piece)] * sides
            + [any_spec] * len(weights),
            out_specs=[out_spec(D), out_spec(D + HD)] + [any_spec] * len(grads),
            scratch_shapes=[
                pltpu.VMEM((D, 2 * W), BF16),
                pltpu.VMEM((W, D), BF16),
                pltpu.VMEM((D, rows), BF16),
                pltpu.VMEM((W, rows), BF16),
                pltpu.VMEM((rows, 2 * W), BF16),
                pltpu.VMEM((rows, D), BF16),
                pltpu.VMEM((tile, W), BF16),
                pltpu.VMEM((tile, 2 * W), F32),
                pltpu.VMEM((tile, D), BF16),
                pltpu.VMEM((D, 2 * W), BF16),
                pltpu.VMEM((W, D), BF16),
                pltpu.SemaphoreType.DMA((12,)),
            ],
        ),
        out_shape=[jax.ShapeDtypeStruct((C, sides, slots, n), BF16) for n in (D, D + HD)]
        + grads,
        compiler_params=pltpu.CompilerParams(vmem_limit_bytes=VMEM_LIMIT),
        cost_estimate=pl.CostEstimate(
            flops=38 * rows * D * W,
            bytes_accessed=8 * rows * D + 24 * D * W,
            transcendentals=2 * rows * W,
        ),
    )(info, *ins, *weights)


def local(
    tokens,
    lengths,
    expert_picks,
    router_weights,
    first_gain,
    second_gain,
    query_weight,
    key_weight,
    value_weight,
    output_weight,
    up_weight,
    down_weight,
    cotangent,
):
    batches, seqs_here, tl, D = tokens.shape
    C = lax.axis_size("ctx")
    F = lax.axis_size("fsdp")
    c = lax.axis_index("ctx")
    f = lax.axis_index("fsdp")
    split = max(1, C // EXPERTS)
    pieces = up_weight.shape[0]
    W = up_weight.shape[2] // 2
    merged = pieces % 2 == 0 and F == 4 and 2 * W == D
    share = 2 if merged else 1
    mine = pieces // share
    role = f % share
    nseq = batches * seqs_here
    cap = max(2, (5 * tl * TOP + 4 * EXPERTS - 1) // (4 * EXPERTS))
    while nseq * cap % 16:
        cap += 1
    slots = nseq * cap
    rows = nseq * tl
    L = C * tl
    width = H * HD
    Dl = query_weight.shape[0]
    cut = Dl // C

    positions = c * tl + jnp.arange(tl, dtype=jnp.int32)
    tables = angle_tables(positions)
    all_tables = angle_tables(jnp.arange(L, dtype=jnp.int32))
    lens = lengths.reshape(nseq)
    live = (positions[None, :] < lens[:, None]).reshape(rows)
    live_rows = live.astype(F32)[:, None]

    def gate(*values):
        return lax.optimization_barrier(values)

    def shift(block, k):
        return lax.ppermute(block, "fsdp", [(i, (i + k) % F) for i in range(F)])

    def fsdp_gather(block):
        got = [shift(block, k) for k in range(F - 1, 0, -1)]
        ring = jnp.stack(got + [block] + got)
        return lax.dynamic_slice_in_dim(ring, F - 1 - f, F, 0)

    def fsdp_scatter_sum(parts):
        total = lax.dynamic_index_in_dim(parts, f, 0, keepdims=False).astype(F32)
        for k in range(1, F):
            block = lax.dynamic_index_in_dim(parts, (f + k) % F, 0, keepdims=False)
            total = total + shift(block, k).astype(F32)
        return total

    def swap(block):
        return lax.ppermute(block, "fsdp", [(i, i ^ 1) for i in range(F)])

    def exchange(blocks):
        return lax.all_to_all(blocks, "ctx", 0, 0, tiled=True)

    def ctx_gather(lines):
        return lax.all_gather(lines, "ctx", axis=1, tiled=True).reshape(D, -1)

    def part_of(weight):
        return lax.dynamic_slice_in_dim(weight, c * cut, cut, 0)

    key_part, value_part = part_of(key_weight), part_of(value_weight)
    qkv_part = [part_of(query_weight)]
    for h in range(KV):
        qkv_part += [part[:, h * HD : (h + 1) * HD] for part in (key_part, value_part)]
    qkv_part = jnp.concatenate(qkv_part, axis=1)
    out_part, gain_parts = part_of(output_weight), jnp.stack([first_gain, second_gain])
    qkv_lines = fsdp_gather(qkv_part)

    messages, operands = {}, {}
    expert_in = [up_weight, down_weight]

    def shard_of(at):
        return jnp.concatenate(
            [lax.dynamic_index_in_dim(x, at, 0, keepdims=False) for x in expert_in]
        )

    def operand(name):
        if name in operands:
            return operands[name]
        j = "wv".index(name[0])
        block = shard_of((role if name[1] == "2" else 1 - role) * mine + j)
        third = block.shape[0] // 3
        at = "abc".find(name[2:]) * third if name[2:] else 0
        return block[at : at + third] if name[2:] else block

    def send(name, block):
        return shift(block, int(name[1]))

    def step(need, values, go):
        if not merged:
            return lax.optimization_barrier(values)
        fresh = tuple(operand(name) for name in go)
        got, values, fresh = lax.optimization_barrier(
            (tuple(messages[name] for name in need), values, fresh)
        )
        messages.update(zip(need, got))
        messages.update((name, send(name, block)) for name, block in zip(go, fresh))
        return values

    picks = expert_picks.reshape(rows, TOP)
    gates = router_weights.reshape(rows, TOP)
    cot = cotangent.reshape(rows, D)
    expert_ids = jnp.arange(EXPERTS, dtype=jnp.int32)
    hit = picks[:, :, None] == expert_ids
    by_expert = jnp.sum(jnp.where(hit, gates[:, :, None], 0.0), axis=1) * live_rows
    high = by_expert.astype(BF16)
    low = (by_expert - high.astype(F32)).astype(BF16)
    gap = jnp.zeros((rows, HD // 2 - EXPERTS), BF16)
    table = jnp.concatenate([high, gap, low, gap], axis=1)
    number = jnp.arange(C)[:, None] * pieces + role * mine + jnp.arange(mine)[None, :]
    expert_of = (number // split).reshape(C * mine)
    earlier = jnp.tril(jnp.ones((tl, tl), BF16), -1)
    pick_map = (expert_ids[:, None] == expert_of[None, :]).astype(BF16)

    def route(table):
        match = table[:, :EXPERTS] > 0
        ranks = jnp.einsum(
            "ab,sbe->sae",
            earlier,
            match.astype(BF16).reshape(nseq, tl, -1),
            preferred_element_type=F32,
        )
        base = (jnp.arange(nseq) * cap)[:, None, None]
        code = jnp.where(match, (ranks + base).reshape(rows, -1), -1.0).astype(BF16)
        code = mm_tn(pick_map, code.T)
        chosen = code[:, None, :] == jnp.arange(slots, dtype=F32)[None, :, None]
        return chosen.astype(BF16).reshape(C, mine, slots, rows)

    def to_slots(sel, source):
        out = mm(sel.reshape(C * mine * slots, rows), source)
        return out.astype(BF16).reshape(C, mine, slots, -1)

    inputs = tokens.reshape(rows, D).astype(F32)
    step([], (qkv_part,), ["w1"])
    _, gain_parts, table, cot, out_part = gate(qkv_lines, gain_parts, table, cot, out_part)
    gains, out_lines = fsdp_gather(gain_parts), fsdp_gather(out_part)
    sels = [route(table)]
    qkv_full, sels[0], table, out_lines, cot_wide, all_tables = step(
        ["w1"],
        (
            ctx_gather(qkv_lines),
            sels[0],
            table,
            out_lines,
            jnp.concatenate([cot, table], axis=1),
            all_tables,
        ),
        ["w3"],
    )
    first_scale = gains[:, 0].reshape(D).astype(F32)
    second_scale = gains[:, 1].reshape(D).astype(F32)
    normed, inverse_one = norm_forward(inputs, first_scale)
    normed_low = normed.astype(BF16)
    kv_low = key_values(normed_low, qkv_full, tables, nseq)
    kv_all = lax.all_gather(kv_low, "ctx", axis=1, tiled=True)
    _, expert_in, qkv_full, table = gate(kv_low, expert_in, qkv_full, table)
    query_pre = mm(normed_low, qkv_full[:, :width]).reshape(nseq, tl, width)
    info = jnp.concatenate([(c * tl)[None], lens])
    kv_all, query_pre, out_lines, table = step(
        ["w3"], (kv_all, query_pre, out_lines, table), ["w2a"]
    )
    far_table = swap(table) if share == 2 else table
    out_full = ctx_gather(out_lines)
    attended, lse, queries = attention(query_pre, kv_all, info, tables)
    attended, cot_wide, far_table = step(["w2a"], (attended, cot_wide, far_table), [])
    attended_low = attended.reshape(rows, width)
    hidden = inputs + live_rows * mm(attended_low, out_full)
    second, inverse_two = norm_forward(hidden, second_scale)
    second_low = second.astype(BF16)

    second_low, cot_wide = step([], (second_low, cot_wide), ["w2b", "w2c", "v2a"])
    wide_rows = jnp.concatenate([second_low, cot_wide], axis=1)
    expert_rows = [exchange(to_slots(sels[0], wide_rows))]
    shards = None
    if merged:
        far_rows = swap(wide_rows)
        sels.append(route(far_table))
        shards = list(blank([(pieces, Dl, 2 * W), (pieces, W // F, D)]))
        far_rows, expert_rows[0], sels[1], shards = step(
            ["w2b", "w2c", "v2a"], (far_rows, expert_rows[0], sels[1], shards), ["v1", "v3"]
        )
        expert_rows.append(exchange(to_slots(sels[1], far_rows)))

    def expert(j):
        at = role * mine + j
        expert_info = jnp.stack([f, (c * pieces + at) // split, at])
        if not merged:
            return run_expert(j, W, expert_rows, [up_full, down_full], expert_info, "whole", "whole")
        names = ["wv"[j] + k for k in ("1", "2a", "2b", "2c", "3")]
        weights = [up_weight, down_weight] + [messages[name] for name in names]
        out = run_expert(j, W, expert_rows, weights, expert_info, "parts", "parts")
        for k, grad in zip(("0", "1", "2a", "2b", "2c", "3"), out[2:]):
            operands["pq"[j] + k] = grad
        return out

    if merged:
        expert_rows[1], normed_mine = step(
            ["v1", "v3"], (expert_rows[1], normed_low), ["v2b", "v2c"]
        )
        every_normed = lax.all_gather(normed_mine, "ctx", axis=0, tiled=True)
        outs = [expert(0)]
        d_in, mixed = [outs[0][0]], [outs[0][1]]
        d_in[0], expert_rows[0], mixed[0] = step(
            ["v2b", "v2c"], (d_in[0], expert_rows[0], mixed[0]), ["p1", "p2a"]
        )
        d_in[0] = exchange(d_in[0])
        outs.append(expert(1))
        last, d_in[0], later, every_normed = step(
            ["p1", "p2a"], (outs[1][0], d_in[0], outs[1][1], every_normed), ["p3"]
        )
        d_in.append(exchange(last))
        mixed.append(later)
    else:
        up_full = lax.all_gather(up_weight, "fsdp", axis=1, tiled=True)
        down_full = lax.all_gather(down_weight, "fsdp", axis=1, tiled=True)
        outs = [expert(j) for j in range(mine)]
        d_in = [exchange(out[0]) for out in outs]
        mixed = [exchange(out[1]) for out in outs]

    def collect(backs):
        sums = []
        for i, sel in enumerate(sels):
            total = 0.0
            for j, back in enumerate(backs):
                total = total + mm_tn(
                    sel[:, j].reshape(C * slots, rows), back[:, i].reshape(C * slots, -1)
                )
            sums.append(total)
        return sums

    def fill(at, total):
        for i, block in enumerate((total[:Dl], total[Dl:])):
            shards[i] = lax.dynamic_update_slice(shards[i], block[None], (at, 0, 0))

    def pair_sum(first, *others):
        far = jnp.concatenate([messages[name] for name in others])
        return first.astype(F32) + far.astype(F32)

    sums = collect(d_in)
    dispatch_grad = sums[0]
    if share == 2:
        far, mixed[0] = step(["p3"], (sums[1].astype(BF16), mixed[0]), ["p2b"])
        dispatch_grad = dispatch_grad + swap(far).astype(F32)
        mixed[0] = exchange(mixed[0])
        (dispatch_grad,) = step(["p2b"], (dispatch_grad,), [])

    upstream = cot.astype(F32)
    norm_grad, second_grads = norm_backward(hidden, inverse_two, second_scale, dispatch_grad)
    hidden_grad = upstream + norm_grad
    branch_grad = (live_rows * hidden_grad).astype(BF16)
    def by_target(grad):
        return grad.astype(BF16).reshape(F, C, cut, -1).transpose(1, 0, 2, 3)

    def over_ctx(blocks):
        return jnp.sum(exchange(blocks).astype(F32), axis=0).astype(BF16)

    def scatter(blocks):
        (blocks,) = gate(blocks.reshape(D, -1))
        total = lax.psum_scatter(blocks, "ctx", scatter_dimension=0, tiled=True)
        return gate(total)[0].reshape(F, cut, -1)

    d_att = mm_nt(branch_grad, out_full).astype(BF16)
    if merged:
        d_att, mixed[0], mixed[1] = step([], (d_att, mixed[0], mixed[1]), ["p2c"])
        mixed[1] = exchange(mixed[1])
    query_back, terms = attention_back(
        queries, kv_all, d_att.reshape(nseq, tl, width), lse, info, all_tables, C
    )
    query_back = query_back.reshape(rows, width)
    terms, query_back = step(["p2c"], (terms, query_back), ["q2a"])
    if merged:
        own_terms = exchange(terms)
        flat_terms = terms.reshape(C * rows, -1)
        blocks = weight_grads(
            attended_low, branch_grad, normed_low, query_back, every_normed, flat_terms, C, F
        )
        blocks, mixed = step(["q2a"], (blocks, mixed), ["q2b", "q2c"])
        mixed_sums = collect(mixed)
        far = swap(mixed_sums[1].astype(BF16))
        own_terms, shards, far = step(["q2b", "q2c"], (own_terms, shards, far), ["q1"])
    else:
        own_terms = over_ctx(terms)
        pair_grad = mm_tn(normed_low, own_terms.reshape(rows, 2 * KV * HD))
        query_grad = mm_tn(normed_low, query_back)
        projection_grad = mm_tn(attended_low, branch_grad)
        blocks = by_target(jnp.concatenate([projection_grad, query_grad, pair_grad], axis=1))
        mixed_rows = collect(mixed)[0]
    weight_rows = scatter(blocks)
    if not merged:
        own_terms = own_terms.reshape((1,) + terms.shape[1:])
    grad_tokens, first_grads = input_back(
        query_back,
        own_terms,
        qkv_full,
        tokens.reshape(rows, D),
        inverse_one,
        first_scale[None],
        hidden_grad,
    )
    first_grads = first_grads[0]
    if merged:
        fill(role * mine, pair_sum(operands["p0"], "p2a", "p2b", "p2c"))
        fill((1 - role) * mine, pair_sum(messages["p1"], "p3"))
        fill(role * mine + 1, pair_sum(operands["q0"], "q2a", "q2b", "q2c"))
        first_grads, mixed_sums[0], shards = step(["q1"], (first_grads, mixed_sums[0], shards), [])
    gain_columns = jnp.stack([first_grads, second_grads]).reshape(2, F, Dl).transpose(1, 0, 2)
    gain_columns = gain_columns.reshape(F, cut, -1)
    gain_count = gain_columns.shape[2]
    gain_columns = jnp.pad(gain_columns, ((0, 0), (0, 0), (0, -gain_count % HD)))
    weight_rows, gain_columns = gate(weight_rows, gain_columns)
    wide = jnp.concatenate([weight_rows, gain_columns.astype(BF16)], axis=2)
    wide = fsdp_scatter_sum(wide).astype(BF16)
    if merged:
        wide, far = step([], (wide, far), ["q3"])
        mixed_rows = mixed_sums[0] + far.astype(F32)
    wide = lax.all_gather(wide, "ctx", axis=0, tiled=False)
    whole = wide[:, :, : D + width + 2 * KV * HD].reshape(Dl, -1).astype(F32)
    grad_projection, grad_query = whole[:, :D], whole[:, D : D + width]
    grad_pairs = whole[:, D + width :].reshape(Dl, KV, 2, HD)
    gain_at = D + width + 2 * KV * HD
    gain_sums = jnp.sum(wide[:, :, gain_at : gain_at + gain_count].astype(F32), axis=0)
    grad_first, grad_second = gain_sums.reshape(2, Dl)

    grad_key = grad_pairs[:, :, 0].reshape(Dl, KV * HD)
    grad_value = grad_pairs[:, :, 1].reshape(Dl, KV * HD)
    grads = (grad_projection, grad_query, grad_key, grad_value, grad_first, grad_second)
    grads = step(["q3"], grads, [])
    grad_projection, grad_query, grad_key, grad_value, grad_first, grad_second = grads
    block_rows = (hidden + mixed_rows[:, :D]).astype(BF16)
    router_by_expert = mixed_rows[:, D : D + EXPERTS]
    grad_router = jnp.sum(jnp.where(hit, router_by_expert[:, None, :], 0.0), axis=2)

    if merged:
        fill((1 - role) * mine + 1, pair_sum(messages["q1"], "q3"))
        grad_up, grad_down = shards
    else:
        grad_up, grad_down = [
            lax.psum_scatter(
                jnp.stack([out[2 + i] for out in outs]), "fsdp", scatter_dimension=1, tiled=True
            ).astype(F32)
            for i in range(2)
        ]

    shape = (batches, seqs_here, tl)
    return (
        block_rows.reshape(shape + (D,)),
        grad_tokens.reshape(shape + (D,)),
        grad_router.reshape(shape + (TOP,)),
        grad_first,
        grad_second,
        grad_query,
        grad_key,
        grad_value,
        grad_projection,
        grad_up,
        grad_down,
    )


def solution(mesh):
    rows = P(None, "fsdp", "ctx", None)
    weight = P("fsdp", None)
    expert = P("ctx", "fsdp", None)
    placed = (rows, P(None, "fsdp"), rows, rows, P("fsdp"), P("fsdp"))
    placed = placed + (weight,) * 4 + (expert,) * 2 + (rows,)
    outs = (rows, rows, rows, P("fsdp"), P("fsdp")) + (weight,) * 4 + (expert,) * 2
    return jax.shard_map(local, mesh=mesh, in_specs=placed, out_specs=outs, check_vma=False)
```

```python
import jax
import jax.numpy as jnp
from jax import lax
from jax.experimental import pallas as pl
from jax.experimental.pallas import tpu as pltpu
from jax.sharding import PartitionSpec as P

H = 12
KV = 2
HD = 128
TOP = 4
EXPERTS = 32
EPSILON = 1e-06
ROPE_BASE = 10000.0
NEGATIVE = -1e30
F32 = jnp.float32
BF16 = jnp.bfloat16


def angle_tables(positions):
    frequency = ROPE_BASE ** (-(jnp.arange(HD // 2, dtype=F32) * 2.0 / HD))
    angles = positions.astype(F32)[:, None] * frequency[None, :]
    cosine, sine = jnp.cos(angles), jnp.sin(angles)
    return jnp.concatenate([cosine, cosine], 1), jnp.concatenate([-sine, sine], 1)


def turn(vectors, cosine, sine):
    return vectors * cosine + pltpu.roll(vectors, HD // 2, 1) * sine


def norm_forward(values, gain_row):
    inverse = lax.rsqrt(jnp.mean(values * values, axis=-1, keepdims=True) + EPSILON)
    return values * inverse * gain_row, inverse


def norm_backward(values, inverse, gain_row, upstream):
    gain_grad = jnp.sum(upstream * values * inverse, axis=0)
    scaled = upstream * gain_row
    projected = jnp.mean(scaled * values, axis=-1, keepdims=True)
    return inverse * scaled - values * inverse**3 * projected, gain_grad


def mm(a, b):
    return jnp.dot(a, b, preferred_element_type=F32)


def mm_nt(a, b):
    return lax.dot_general(a, b, (((1,), (1,)), ((), ())), preferred_element_type=F32)


def mm_tn(a, b):
    return lax.dot_general(a, b, (((0,), (0,)), ((), ())), preferred_element_type=F32)


VMEM_LIMIT = 60 * 1024 * 1024


def stack_heads(block, groups):
    return jnp.concatenate([block[:, h * HD : (h + 1) * HD] for h in range(groups)], axis=0)


def masked_scores(stacked, keys, first, length, groups):
    tl = stacked.shape[0] // groups
    total = keys.shape[0]
    scores = mm_nt(stacked, keys) * HD ** (-0.5)
    key_at = lax.broadcasted_iota(jnp.int32, (tl, total), 1)
    query_at = lax.broadcasted_iota(jnp.int32, (tl, total), 0) + first
    allowed = (key_at <= query_at) & (key_at < length)
    scores = scores.reshape(groups, tl, total)
    return jnp.where(allowed[None], scores, NEGATIVE).reshape(groups * tl, total)


def key_value_kernel(x_ref, w_ref, cos_ref, sin_ref, out_ref):
    both = mm(x_ref[...], w_ref[...])
    cosine, sine = cos_ref[...], sin_ref[...]
    for h in range(KV):
        key = turn(both[:, 2 * h * HD : (2 * h + 1) * HD], cosine, sine)
        out_ref[0, :, 2 * h * HD : (2 * h + 1) * HD] = key.astype(BF16)
        value = both[:, (2 * h + 1) * HD : (2 * h + 2) * HD]
        out_ref[0, :, (2 * h + 1) * HD : (2 * h + 2) * HD] = value.astype(BF16)


def key_values(normed_low, qkv_full, tables, nseq):
    rows, D = normed_low.shape
    tl, wide = rows // nseq, 2 * KV * HD
    return pl.pallas_call(
        key_value_kernel,
        grid=(nseq,),
        in_specs=[
            pl.BlockSpec((tl, D), lambda s: (s, 0)),
            pl.BlockSpec((D, wide), lambda s: (0, H * HD // wide)),
            pl.BlockSpec((tl, HD), lambda s: (0, 0)),
            pl.BlockSpec((tl, HD), lambda s: (0, 0)),
        ],
        out_specs=pl.BlockSpec((1, tl, wide), lambda s: (s, 0, 0)),
        out_shape=jax.ShapeDtypeStruct((nseq, tl, wide), BF16),
        compiler_params=pltpu.CompilerParams(vmem_limit_bytes=VMEM_LIMIT),
        cost_estimate=pl.CostEstimate(
            flops=4 * rows * D * wide, bytes_accessed=2 * D * wide, transcendentals=0
        ),
    )(normed_low, qkv_full, *tables)


def attend_kernel(groups, info, q_ref, kv_ref, cos_ref, sin_ref, att_ref, lse_ref, turned_ref):
    tl = q_ref.shape[1]
    cosine, sine = cos_ref[...], sin_ref[...]
    for h in range(groups):
        at = slice(h * HD, (h + 1) * HD)
        turned_ref[0, :, at] = turn(q_ref[0, :, at], cosine, sine).astype(BF16)
    stacked = stack_heads(turned_ref[0], groups)
    scores = masked_scores(
        stacked, kv_ref[0, :, :HD], info[0], info[1 + pl.program_id(0)], groups
    )
    top = jnp.max(scores, axis=-1, keepdims=True)
    shares = jnp.exp(scores - top)
    total = jnp.sum(shares, axis=-1, keepdims=True)
    out = mm(shares.astype(BF16), kv_ref[0, :, HD:]) / total
    lse = top + jnp.log(total)
    for h in range(groups):
        at = slice(h * tl, (h + 1) * tl)
        att_ref[0, :, h * HD : (h + 1) * HD] = out[at].astype(BF16)
        lse_ref[0, 0, :, h : h + 1] = lse[at]


def attend_back_kernel(
    groups, info, q_ref, kv_ref, da_ref, lse_ref, cos_ref, sin_ref, dq_ref, dkv_ref
):
    tl = q_ref.shape[1]
    keys, values = kv_ref[0, :, :HD], kv_ref[0, :, HD:]
    stacked = stack_heads(q_ref[0], groups)
    scores = masked_scores(stacked, keys, info[0], info[1 + pl.program_id(0)], groups)
    lse = jnp.concatenate([lse_ref[0, 0, :, h : h + 1] for h in range(groups)], axis=0)
    probs = jnp.exp(scores - lse)
    grads = stack_heads(da_ref[0], groups)
    d_probs = mm_nt(grads, values)
    delta = jnp.sum(probs * d_probs, axis=-1, keepdims=True)
    d_scores = (probs * (d_probs - delta)).astype(BF16)
    dq = mm(d_scores, keys) * HD ** (-0.5)
    here = pl.ds(pl.multiple_of(info[0], 8), tl)
    cosine, sine = cos_ref[here, :], -sin_ref[here, :]
    for h in range(groups):
        turned = turn(dq[h * tl : (h + 1) * tl], cosine, sine)
        dq_ref[0, :, h * HD : (h + 1) * HD] = turned.astype(BF16)
    dk = mm_tn(d_scores, stacked) * HD ** (-0.5)
    dk = turn(dk, cos_ref[...], -sin_ref[...])
    dv = mm_tn(probs.astype(BF16), grads)
    shape = dkv_ref.shape[:1] + (tl, HD)
    dkv_ref[:, 0, :, :HD] = dk.reshape(shape).astype(BF16)
    dkv_ref[:, 0, :, HD:] = dv.reshape(shape).astype(BF16)


def attention(queries, kv_all, info, tables):
    nseq, tl, width = queries.shape
    total = kv_all.shape[1]
    groups = H // KV
    return pl.pallas_call(
        lambda *refs: attend_kernel(groups, *refs),
        grid_spec=pltpu.PrefetchScalarGridSpec(
            num_scalar_prefetch=1,
            grid=(nseq, KV),
            in_specs=[
                pl.BlockSpec((1, tl, groups * HD), lambda s, n, info: (s, 0, n)),
                pl.BlockSpec((1, total, 2 * HD), lambda s, n, info: (s, 0, n)),
                pl.BlockSpec((tl, HD), lambda s, n, info: (0, 0)),
                pl.BlockSpec((tl, HD), lambda s, n, info: (0, 0)),
            ],
            out_specs=[
                pl.BlockSpec((1, tl, groups * HD), lambda s, n, info: (s, 0, n)),
                pl.BlockSpec((1, 1, tl, HD), lambda s, n, info: (s, n, 0, 0)),
                pl.BlockSpec((1, tl, groups * HD), lambda s, n, info: (s, 0, n)),
            ],
        ),
        out_shape=[
            jax.ShapeDtypeStruct((nseq, tl, width), BF16),
            jax.ShapeDtypeStruct((nseq, KV, tl, HD), F32),
            jax.ShapeDtypeStruct((nseq, tl, width), BF16),
        ],
        compiler_params=pltpu.CompilerParams(vmem_limit_bytes=VMEM_LIMIT),
        cost_estimate=pl.CostEstimate(
            flops=28 * nseq * tl * width * total,
            bytes_accessed=4 * queries.size * 2 + 2 * kv_all.size,
            transcendentals=nseq * H * tl * total,
        ),
    )(info, queries, kv_all, *tables)


def attention_back(queries, kv_all, d_att, lse, info, tables, ctx_count):
    nseq, tl, width = queries.shape
    total = kv_all.shape[1]
    groups = H // KV
    return pl.pallas_call(
        lambda *refs: attend_back_kernel(groups, *refs),
        grid_spec=pltpu.PrefetchScalarGridSpec(
            num_scalar_prefetch=1,
            grid=(nseq, KV),
            in_specs=[
                pl.BlockSpec((1, tl, groups * HD), lambda s, n, info: (s, 0, n)),
                pl.BlockSpec((1, total, 2 * HD), lambda s, n, info: (s, 0, n)),
                pl.BlockSpec((1, tl, groups * HD), lambda s, n, info: (s, 0, n)),
                pl.BlockSpec((1, 1, tl, HD), lambda s, n, info: (s, n, 0, 0)),
                pl.BlockSpec((total, HD), lambda s, n, info: (0, 0)),
                pl.BlockSpec((total, HD), lambda s, n, info: (0, 0)),
            ],
            out_specs=[
                pl.BlockSpec((1, tl, groups * HD), lambda s, n, info: (s, 0, n)),
                pl.BlockSpec((ctx_count, 1, tl, 2 * HD), lambda s, n, info: (0, s, 0, n)),
            ],
        ),
        out_shape=[
            jax.ShapeDtypeStruct((nseq, tl, width), BF16),
            jax.ShapeDtypeStruct((ctx_count, nseq, tl, KV * 2 * HD), BF16),
        ],
        compiler_params=pltpu.CompilerParams(vmem_limit_bytes=VMEM_LIMIT),
        cost_estimate=pl.CostEstimate(
            flops=36 * nseq * tl * width * total,
            bytes_accessed=6 * queries.size * 2 + 4 * kv_all.size,
            transcendentals=nseq * H * tl * total,
        ),
    )(info, queries, kv_all, d_att, lse, *tables)


def expert_kernel(sides, w_mode, g_mode, *refs):
    info = refs[0]
    ins = refs[1 : 1 + sides]
    count = MODE_REFS[w_mode]
    weights = refs[1 + sides : 1 + sides + count]
    at = 1 + sides + count
    din_ref, wy_ref = refs[at : at + 2]
    at = at + 2
    out_refs = refs[at : at + GRAD_REFS[g_mode]]
    at = at + GRAD_REFS[g_mode]
    up, down, x_t, act_t, dgu, dy, act_s, pre, wide, gup, gdn, sems = refs[at:]
    step, steps = pl.program_id(0), pl.num_programs(0)
    D, W = up.shape[0], down.shape[0]
    tile = wide.shape[0]
    tw = 256 if W % 256 == 0 else 128
    td = 256

    wl = W // 4
    dl = 2 * wl

    def shard(up_side, down_side, source, block, first=0):
        pairs, count = [], block.shape[0]
        ups = min(count, dl - first)
        if ups > 0:
            at = pl.ds(pl.multiple_of(source * dl + first, 16), ups)
            pairs.append((up_side.at[at], block.at[pl.ds(0, ups)]))
        if ups < count:
            skip = max(0, ups)
            at = pl.ds(pl.multiple_of(source * wl + first + skip - dl, 16), count - skip)
            pairs.append((down_side.at[at], block.at[pl.ds(skip, count - skip)]))
        return pairs

    def by_distance(up_side, down_side, blocks, sign):
        pairs = []
        for block, k, first in zip(blocks, (1, 2, 2, 2, 3), (0, 0, wl, 2 * wl, 0)):
            source = lax.rem(info[0] + 4 + sign * k, 4)
            pairs += shard(up_side, down_side, source, block, first)
        return pairs

    def copies_of(pairs):
        return [pltpu.make_async_copy(a, b, sems.at[i]) for i, (a, b) in enumerate(pairs)]

    def loads():
        if w_mode == "whole":
            return copies_of([(weights[0].at[info[2]], up), (weights[1].at[info[2]], down)])
        pairs = by_distance(up, down, weights[2:], -1)
        own_up = up.at[pl.ds(pl.multiple_of(info[0] * dl, 16), dl)]
        own_down = down.at[pl.ds(pl.multiple_of(info[0] * wl, 16), wl)]
        pairs += [(own_up, weights[0].at[info[2]]), (own_down, weights[1].at[info[2]])]
        return copies_of([(b, a) for a, b in pairs])

    def put(ref, columns, block):
        per = tile // sides
        shape = (ref.shape[0], ref.shape[2], block.shape[1])
        for i in range(sides):
            ref[:, i, :, columns] = block[i * per : (i + 1) * per].reshape(shape)

    @pl.when(step == 0)
    def _():
        copies = loads()
        for copy in copies:
            copy.start()
        for copy in copies:
            copy.wait()

    rows = pl.ds(pl.multiple_of(step * tile, 128), tile)
    x = jnp.concatenate([r[:, :, :, :D].reshape(-1, D) for r in ins], axis=0)
    g_aug = jnp.concatenate([r[:, :, :, D:].reshape(-1, D + HD) for r in ins], axis=0)
    x_t[:, rows] = x.T
    lane = lax.broadcasted_iota(jnp.int32, (tile, HD), 1)
    picked = (lane == info[1]) | (lane == info[1] + HD // 2)
    w = jnp.sum(jnp.where(picked, g_aug[:, D:].astype(F32), 0.0), axis=1, keepdims=True)
    wide[...] = g_aug[:, :D]
    dy[rows, :] = (g_aug[:, :D].astype(F32) * w).astype(BF16)

    @pl.loop(0, W // tw)
    def _(t):
        a = pl.ds(pl.multiple_of(t * tw, 128), tw)
        b = pl.ds(pl.multiple_of(W + t * tw, 128), tw)
        gate = mm(x, up[:, a])
        lift = mm(x, up[:, b])
        pre[:, a] = gate
        pre[:, b] = lift
        act = gate / (1.0 + jnp.exp(-gate)) * lift
        act = act.astype(BF16)
        act_s[:, a] = act
        act_t[a, rows] = act.T

    def out_step(t, total):
        a = pl.ds(pl.multiple_of(t * td, 128), td)
        y = mm(act_s[...], down[:, a])
        put(wy_ref, a, (y * w).astype(BF16))
        return total + jnp.sum(y * wide[:, a].astype(F32), axis=1, keepdims=True)

    router = lax.fori_loop(0, D // td, out_step, jnp.zeros((tile, 1), F32))
    extra = jnp.where(lane == info[1], router, 0.0).astype(BF16)
    put(wy_ref, pl.ds(D, HD), extra)

    @pl.loop(0, W // tw)
    def _(t):
        a = pl.ds(pl.multiple_of(t * tw, 128), tw)
        b = pl.ds(pl.multiple_of(W + t * tw, 128), tw)
        d_act = mm_nt(dy[rows, :], down[a, :])
        gate, lift = pre[:, a], pre[:, b]
        sig = 1.0 / (1.0 + jnp.exp(-gate))
        dgu[rows, a] = (d_act * lift * sig * (1.0 + gate * (1.0 - sig))).astype(BF16)
        dgu[rows, b] = (d_act * gate * sig).astype(BF16)

    @pl.loop(0, D // td)
    def _(t):
        a = pl.ds(pl.multiple_of(t * td, 128), td)
        put(din_ref, a, mm_nt(dgu[rows, :], up[a, :]).astype(BF16))

    @pl.when(step == steps - 1)
    def _():
        @pl.loop(0, D // td)
        def _(t):
            a = pl.ds(pl.multiple_of(t * td, 128), td)
            gup[a, :] = mm(x_t[a, :], dgu[...]).astype(BF16)

        @pl.loop(0, W // tw)
        def _(t):
            a = pl.ds(pl.multiple_of(t * tw, 128), tw)
            gdn[a, :] = mm(act_t[a, :], dy[...]).astype(BF16)

        if g_mode == "whole":
            pairs = [(gup, out_refs[0]), (gdn, out_refs[1])]
        else:
            pairs = shard(gup, gdn, info[0], out_refs[0])
            pairs += by_distance(gup, gdn, out_refs[1:], 1)
        copies = copies_of(pairs)
        for copy in copies:
            copy.start()
        for copy in copies:
            copy.wait()


def weight_grad_kernel(
    planes, att_ref, db_ref, x_ref, dq_ref, all_ref, pair_ref, out_ref, total, grads, sems
):
    step = pl.program_id(0)
    D, width = x_ref.shape[1], dq_ref.shape[1]
    td = 256

    @pl.when(step == 0)
    def _():
        total[...] = jnp.zeros_like(total)

        @pl.loop(0, D // td)
        def _(t):
            a = pl.ds(pl.multiple_of(t * td, 128), td)
            grads[a, :D] = mm_tn(att_ref[:, a], db_ref[...]).astype(BF16)
            grads[a, D : D + width] = mm_tn(x_ref[:, a], dq_ref[...]).astype(BF16)

    total[...] += mm_tn(pair_ref[...], all_ref[...])

    @pl.when(step == pl.num_programs(0) - 1)
    def _():
        @pl.loop(0, D // td)
        def _(t):
            a = pl.ds(pl.multiple_of(t * td, 128), td)
            grads[a, D + width :] = total[:, a].T.astype(BF16)

        ctx = sems.shape[0] // planes
        cut = D // (planes * ctx)
        copies = []
        for f in range(planes):
            for c in range(ctx):
                source = grads.at[pl.ds((f * ctx + c) * cut, cut)]
                target = out_ref.at[pl.ds((c * planes + f) * cut, cut)]
                copies.append(pltpu.make_async_copy(source, target, sems.at[len(copies)]))
        for copy in copies:
            copy.start()
        for copy in copies:
            copy.wait()


def weight_grads(att, db, x, dq, every_x, pairs, ctx_count, planes):
    rows, D = x.shape
    width, wide = dq.shape[1], pairs.shape[1]
    return pl.pallas_call(
        lambda *refs: weight_grad_kernel(planes, *refs),
        grid=(ctx_count,),
        in_specs=[
            pl.BlockSpec((rows, D), lambda i: (0, 0)),
            pl.BlockSpec((rows, D), lambda i: (0, 0)),
            pl.BlockSpec((rows, D), lambda i: (0, 0)),
            pl.BlockSpec((rows, width), lambda i: (0, 0)),
            pl.BlockSpec((rows, D), lambda i: (i, 0)),
            pl.BlockSpec((rows, wide), lambda i: (i, 0)),
        ],
        out_specs=pl.BlockSpec(memory_space=pl.ANY),
        out_shape=jax.ShapeDtypeStruct((D, D + width + wide), BF16),
        scratch_shapes=[
            pltpu.VMEM((wide, D), F32),
            pltpu.VMEM((D, D + width + wide), BF16),
            pltpu.SemaphoreType.DMA((planes * ctx_count,)),
        ],
        compiler_params=pltpu.CompilerParams(vmem_limit_bytes=VMEM_LIMIT),
        cost_estimate=pl.CostEstimate(
            flops=4 * rows * D * (D + width + ctx_count * wide),
            bytes_accessed=2 * ctx_count * rows * D,
            transcendentals=0,
        ),
    )(att, db, x, dq, every_x, pairs)


def input_back_kernel(
    dq_ref, terms_ref, w_ref, x_ref, inverse_ref, gain_ref, upstream_ref, out_ref, gain_out
):
    width = dq_ref.shape[1]
    pairs = jnp.sum(terms_ref[:, 0].astype(F32), axis=0).astype(BF16)
    grad = mm_nt(dq_ref[...], w_ref[:, :width]) + mm_nt(pairs, w_ref[:, width:])
    values, inverse = x_ref[...].astype(F32), inverse_ref[...]

    @pl.when(pl.program_id(0) == 0)
    def _():
        gain_out[...] = jnp.zeros_like(gain_out)

    gain_out[...] += jnp.sum(grad * values * inverse, axis=0, keepdims=True)
    scaled = grad * gain_ref[...]
    projected = jnp.mean(scaled * values, axis=-1, keepdims=True)
    out_ref[...] = upstream_ref[...] + inverse * scaled - values * inverse**3 * projected


def input_back(dq, terms, w, x, inverse, gain, upstream):
    ctx_count, nseq, tl, wide = terms.shape
    rows, D = x.shape
    return pl.pallas_call(
        input_back_kernel,
        grid=(nseq,),
        in_specs=[
            pl.BlockSpec((tl, dq.shape[1]), lambda i: (i, 0)),
            pl.BlockSpec((ctx_count, 1, tl, wide), lambda i: (0, i, 0, 0)),
            pl.BlockSpec(w.shape, lambda i: (0, 0)),
            pl.BlockSpec((tl, D), lambda i: (i, 0)),
            pl.BlockSpec((tl, 1), lambda i: (i, 0)),
            pl.BlockSpec((1, D), lambda i: (0, 0)),
            pl.BlockSpec((tl, D), lambda i: (i, 0)),
        ],
        out_specs=[
            pl.BlockSpec((tl, D), lambda i: (i, 0)),
            pl.BlockSpec((1, D), lambda i: (0, 0)),
        ],
        out_shape=[
            jax.ShapeDtypeStruct((rows, D), F32),
            jax.ShapeDtypeStruct((1, D), F32),
        ],
        compiler_params=pltpu.CompilerParams(vmem_limit_bytes=VMEM_LIMIT),
        cost_estimate=pl.CostEstimate(
            flops=8 * rows * w.size, bytes_accessed=16 * rows * D, transcendentals=0
        ),
    )(dq, terms, w, x, inverse, gain, upstream)


def blank(shapes):
    return pl.pallas_call(
        lambda *refs: None,
        out_specs=[pl.BlockSpec(memory_space=pl.ANY)] * len(shapes),
        out_shape=[jax.ShapeDtypeStruct(shape, F32) for shape in shapes],
    )()


MODE_REFS = {"whole": 2, "parts": 7}
GRAD_REFS = {"whole": 2, "parts": 6}


def run_expert(piece, W, ins, weights, info, w_mode, g_mode):
    C, mine, slots, wide = ins[0].shape
    D = (wide - HD) // 2
    sides = len(ins)
    per_step = C
    while per_step > 1 and (per_step * sides * slots > 640 or C % per_step):
        per_step -= 1
    tile = per_step * sides * slots
    rows = C * sides * slots

    def spec(width, at):
        return pl.BlockSpec((per_step, 1, slots, width), lambda i, info: (i, at, 0, 0))

    def out_spec(width):
        return pl.BlockSpec((per_step, sides, slots, width), lambda i, info: (i, 0, 0, 0))

    any_spec = pl.BlockSpec(memory_space=pl.ANY)
    if g_mode == "whole":
        grads = [(D, 2 * W), (W, D)]
    else:
        grads = [(n * W // 4, D) for n in (3, 3, 1, 1, 1, 3)]
    grads = [jax.ShapeDtypeStruct(shape, BF16) for shape in grads]
    return pl.pallas_call(
        lambda *refs: expert_kernel(sides, w_mode, g_mode, *refs),
        grid_spec=pltpu.PrefetchScalarGridSpec(
            num_scalar_prefetch=1,
            grid=(C // per_step,),
            in_specs=[spec(wide, piece)] * sides
            + [any_spec] * len(weights),
            out_specs=[out_spec(D), out_spec(D + HD)] + [any_spec] * len(grads),
            scratch_shapes=[
                pltpu.VMEM((D, 2 * W), BF16),
                pltpu.VMEM((W, D), BF16),
                pltpu.VMEM((D, rows), BF16),
                pltpu.VMEM((W, rows), BF16),
                pltpu.VMEM((rows, 2 * W), BF16),
                pltpu.VMEM((rows, D), BF16),
                pltpu.VMEM((tile, W), BF16),
                pltpu.VMEM((tile, 2 * W), F32),
                pltpu.VMEM((tile, D), BF16),
                pltpu.VMEM((D, 2 * W), BF16),
                pltpu.VMEM((W, D), BF16),
                pltpu.SemaphoreType.DMA((12,)),
            ],
        ),
        out_shape=[jax.ShapeDtypeStruct((C, sides, slots, n), BF16) for n in (D, D + HD)]
        + grads,
        compiler_params=pltpu.CompilerParams(vmem_limit_bytes=VMEM_LIMIT),
        cost_estimate=pl.CostEstimate(
            flops=38 * rows * D * W,
            bytes_accessed=8 * rows * D + 24 * D * W,
            transcendentals=2 * rows * W,
        ),
    )(info, *ins, *weights)


def local(
    tokens,
    lengths,
    expert_picks,
    router_weights,
    first_gain,
    second_gain,
    query_weight,
    key_weight,
    value_weight,
    output_weight,
    up_weight,
    down_weight,
    cotangent,
):
    batches, seqs_here, tl, D = tokens.shape
    C = lax.axis_size("ctx")
    F = lax.axis_size("fsdp")
    c = lax.axis_index("ctx")
    f = lax.axis_index("fsdp")
    split = max(1, C // EXPERTS)
    pieces = up_weight.shape[0]
    W = up_weight.shape[2] // 2
    merged = pieces % 2 == 0 and F == 4 and 2 * W == D
    share = 2 if merged else 1
    mine = pieces // share
    role = f % share
    nseq = batches * seqs_here
    cap = max(2, (5 * tl * TOP + 4 * EXPERTS - 1) // (4 * EXPERTS))
    while nseq * cap % 16:
        cap += 1
    slots = nseq * cap
    rows = nseq * tl
    L = C * tl
    width = H * HD
    Dl = query_weight.shape[0]
    cut = Dl // C

    positions = c * tl + jnp.arange(tl, dtype=jnp.int32)
    tables = angle_tables(positions)
    all_tables = angle_tables(jnp.arange(L, dtype=jnp.int32))
    lens = lengths.reshape(nseq)
    live = (positions[None, :] < lens[:, None]).reshape(rows)
    live_rows = live.astype(F32)[:, None]

    def gate(*values):
        return lax.optimization_barrier(values)

    def shift(block, k):
        return lax.ppermute(block, "fsdp", [(i, (i + k) % F) for i in range(F)])

    def fsdp_gather(block):
        got = [shift(block, k) for k in range(F - 1, 0, -1)]
        ring = jnp.stack(got + [block] + got)
        return lax.dynamic_slice_in_dim(ring, F - 1 - f, F, 0)

    def fsdp_scatter_sum(parts):
        total = lax.dynamic_index_in_dim(parts, f, 0, keepdims=False).astype(F32)
        for k in range(1, F):
            block = lax.dynamic_index_in_dim(parts, (f + k) % F, 0, keepdims=False)
            total = total + shift(block, k).astype(F32)
        return total

    def swap(block):
        return lax.ppermute(block, "fsdp", [(i, i ^ 1) for i in range(F)])

    def exchange(blocks):
        return lax.all_to_all(blocks, "ctx", 0, 0, tiled=True)

    def ctx_gather(lines):
        return lax.all_gather(lines, "ctx", axis=1, tiled=True).reshape(D, -1)

    def part_of(weight):
        return lax.dynamic_slice_in_dim(weight, c * cut, cut, 0)

    key_part, value_part = part_of(key_weight), part_of(value_weight)
    qkv_part = [part_of(query_weight)]
    for h in range(KV):
        qkv_part += [part[:, h * HD : (h + 1) * HD] for part in (key_part, value_part)]
    qkv_part = jnp.concatenate(qkv_part, axis=1)
    out_part, gain_parts = part_of(output_weight), jnp.stack([first_gain, second_gain])
    qkv_lines = fsdp_gather(qkv_part)

    messages, operands = {}, {}
    expert_in = [up_weight, down_weight]

    def shard_of(at):
        return jnp.concatenate(
            [lax.dynamic_index_in_dim(x, at, 0, keepdims=False) for x in expert_in]
        )

    def operand(name):
        if name in operands:
            return operands[name]
        j = "wv".index(name[0])
        block = shard_of((role if name[1] == "2" else 1 - role) * mine + j)
        third = block.shape[0] // 3
        at = "abc".find(name[2:]) * third if name[2:] else 0
        return block[at : at + third] if name[2:] else block

    def send(name, block):
        return shift(block, int(name[1]))

    def step(need, values, go):
        if not merged:
            return lax.optimization_barrier(values)
        fresh = tuple(operand(name) for name in go)
        got, values, fresh = lax.optimization_barrier(
            (tuple(messages[name] for name in need), values, fresh)
        )
        messages.update(zip(need, got))
        messages.update((name, send(name, block)) for name, block in zip(go, fresh))
        return values

    picks = expert_picks.reshape(rows, TOP)
    gates = router_weights.reshape(rows, TOP)
    cot = cotangent.reshape(rows, D)
    expert_ids = jnp.arange(EXPERTS, dtype=jnp.int32)
    hit = picks[:, :, None] == expert_ids
    by_expert = jnp.sum(jnp.where(hit, gates[:, :, None], 0.0), axis=1) * live_rows
    high = by_expert.astype(BF16)
    low = (by_expert - high.astype(F32)).astype(BF16)
    gap = jnp.zeros((rows, HD // 2 - EXPERTS), BF16)
    table = jnp.concatenate([high, gap, low, gap], axis=1)
    number = jnp.arange(C)[:, None] * pieces + role * mine + jnp.arange(mine)[None, :]
    expert_of = (number // split).reshape(C * mine)
    earlier = jnp.tril(jnp.ones((tl, tl), BF16), -1)
    pick_map = (expert_ids[:, None] == expert_of[None, :]).astype(BF16)

    def route(table):
        match = table[:, :EXPERTS] > 0
        ranks = jnp.einsum(
            "ab,sbe->sae",
            earlier,
            match.astype(BF16).reshape(nseq, tl, -1),
            preferred_element_type=F32,
        )
        base = (jnp.arange(nseq) * cap)[:, None, None]
        code = jnp.where(match, (ranks + base).reshape(rows, -1), -1.0).astype(BF16)
        code = mm_tn(pick_map, code.T)
        chosen = code[:, None, :] == jnp.arange(slots, dtype=F32)[None, :, None]
        return chosen.astype(BF16).reshape(C, mine, slots, rows)

    def to_slots(sel, source):
        out = mm(sel.reshape(C * mine * slots, rows), source)
        return out.astype(BF16).reshape(C, mine, slots, -1)

    inputs = tokens.reshape(rows, D).astype(F32)
    step([], (qkv_part,), ["w1"])
    _, gain_parts, table, cot, out_part = gate(qkv_lines, gain_parts, table, cot, out_part)
    gains, out_lines = fsdp_gather(gain_parts), fsdp_gather(out_part)
    sels = [route(table)]
    qkv_full, sels[0], table, out_lines, cot_wide, all_tables = step(
        ["w1"],
        (
            ctx_gather(qkv_lines),
            sels[0],
            table,
            out_lines,
            jnp.concatenate([cot, table], axis=1),
            all_tables,
        ),
        ["w3"],
    )
    first_scale = gains[:, 0].reshape(D).astype(F32)
    second_scale = gains[:, 1].reshape(D).astype(F32)
    normed, inverse_one = norm_forward(inputs, first_scale)
    normed_low = normed.astype(BF16)
    kv_low = key_values(normed_low, qkv_full, tables, nseq)
    kv_all = lax.all_gather(kv_low, "ctx", axis=1, tiled=True)
    _, expert_in, qkv_full, table = gate(kv_low, expert_in, qkv_full, table)
    query_pre = mm(normed_low, qkv_full[:, :width]).reshape(nseq, tl, width)
    info = jnp.concatenate([(c * tl)[None], lens])
    kv_all, query_pre, out_lines, table = step(
        ["w3"], (kv_all, query_pre, out_lines, table), ["w2a"]
    )
    far_table = swap(table) if share == 2 else table
    out_full = ctx_gather(out_lines)
    attended, lse, queries = attention(query_pre, kv_all, info, tables)
    attended, cot_wide, far_table = step(["w2a"], (attended, cot_wide, far_table), [])
    attended_low = attended.reshape(rows, width)
    hidden = inputs + live_rows * mm(attended_low, out_full)
    second, inverse_two = norm_forward(hidden, second_scale)
    second_low = second.astype(BF16)

    second_low, cot_wide = step([], (second_low, cot_wide), ["w2b", "w2c", "v2a"])
    wide_rows = jnp.concatenate([second_low, cot_wide], axis=1)
    expert_rows = [exchange(to_slots(sels[0], wide_rows))]
    shards = None
    if merged:
        far_rows = swap(wide_rows)
        sels.append(route(far_table))
        shards = list(blank([(pieces, Dl, 2 * W), (pieces, W // F, D)]))
        far_rows, expert_rows[0], sels[1], shards = step(
            ["w2b", "w2c", "v2a"], (far_rows, expert_rows[0], sels[1], shards), ["v1", "v3"]
        )
        expert_rows.append(exchange(to_slots(sels[1], far_rows)))

    def expert(j):
        at = role * mine + j
        expert_info = jnp.stack([f, (c * pieces + at) // split, at])
        if not merged:
            return run_expert(j, W, expert_rows, [up_full, down_full], expert_info, "whole", "whole")
        names = ["wv"[j] + k for k in ("1", "2a", "2b", "2c", "3")]
        weights = [up_weight, down_weight] + [messages[name] for name in names]
        out = run_expert(j, W, expert_rows, weights, expert_info, "parts", "parts")
        for k, grad in zip(("0", "1", "2a", "2b", "2c", "3"), out[2:]):
            operands["pq"[j] + k] = grad
        return out

    if merged:
        expert_rows[1], normed_mine = step(
            ["v1", "v3"], (expert_rows[1], normed_low), ["v2b", "v2c"]
        )
        every_normed = lax.all_gather(normed_mine, "ctx", axis=0, tiled=True)
        outs = [expert(0)]
        d_in, mixed = [outs[0][0]], [outs[0][1]]
        d_in[0], expert_rows[0], mixed[0] = step(
            ["v2b", "v2c"], (d_in[0], expert_rows[0], mixed[0]), ["p1", "p2a"]
        )
        d_in[0] = exchange(d_in[0])
        outs.append(expert(1))
        last, d_in[0], later, every_normed = step(
            ["p1", "p2a"], (outs[1][0], d_in[0], outs[1][1], every_normed), ["p3"]
        )
        d_in.append(exchange(last))
        mixed.append(later)
    else:
        up_full = lax.all_gather(up_weight, "fsdp", axis=1, tiled=True)
        down_full = lax.all_gather(down_weight, "fsdp", axis=1, tiled=True)
        outs = [expert(j) for j in range(mine)]
        d_in = [exchange(out[0]) for out in outs]
        mixed = [exchange(out[1]) for out in outs]

    def collect(backs):
        sums = []
        for i, sel in enumerate(sels):
            total = 0.0
            for j, back in enumerate(backs):
                total = total + mm_tn(
                    sel[:, j].reshape(C * slots, rows), back[:, i].reshape(C * slots, -1)
                )
            sums.append(total)
        return sums

    def fill(at, total):
        for i, block in enumerate((total[:Dl], total[Dl:])):
            shards[i] = lax.dynamic_update_slice(shards[i], block[None], (at, 0, 0))

    def pair_sum(first, *others):
        far = jnp.concatenate([messages[name] for name in others])
        return first.astype(F32) + far.astype(F32)

    sums = collect(d_in)
    dispatch_grad = sums[0]
    if share == 2:
        far, mixed[0] = step(["p3"], (sums[1].astype(BF16), mixed[0]), ["p2b"])
        dispatch_grad = dispatch_grad + swap(far).astype(F32)
        mixed[0] = exchange(mixed[0])
        (dispatch_grad,) = step(["p2b"], (dispatch_grad,), [])

    upstream = cot.astype(F32)
    norm_grad, second_grads = norm_backward(hidden, inverse_two, second_scale, dispatch_grad)
    hidden_grad = upstream + norm_grad
    branch_grad = (live_rows * hidden_grad).astype(BF16)
    def by_target(grad):
        return grad.astype(BF16).reshape(F, C, cut, -1).transpose(1, 0, 2, 3)

    def over_ctx(blocks):
        return jnp.sum(exchange(blocks).astype(F32), axis=0).astype(BF16)

    def scatter(blocks):
        (blocks,) = gate(blocks.reshape(D, -1))
        total = lax.psum_scatter(blocks, "ctx", scatter_dimension=0, tiled=True)
        return gate(total)[0].reshape(F, cut, -1)

    d_att = mm_nt(branch_grad, out_full).astype(BF16)
    if merged:
        d_att, mixed[0], mixed[1] = step([], (d_att, mixed[0], mixed[1]), ["p2c"])
        mixed[1] = exchange(mixed[1])
    query_back, terms = attention_back(
        queries, kv_all, d_att.reshape(nseq, tl, width), lse, info, all_tables, C
    )
    query_back = query_back.reshape(rows, width)
    terms, query_back = step(["p2c"], (terms, query_back), ["q2a"])
    if merged:
        own_terms = exchange(terms)
        flat_terms = terms.reshape(C * rows, -1)
        blocks = weight_grads(
            attended_low, branch_grad, normed_low, query_back, every_normed, flat_terms, C, F
        )
        blocks, mixed = step(["q2a"], (blocks, mixed), ["q2b", "q2c"])
        mixed_sums = collect(mixed)
        far = swap(mixed_sums[1].astype(BF16))
        own_terms, shards, far = step(["q2b", "q2c"], (own_terms, shards, far), ["q1"])
    else:
        own_terms = over_ctx(terms)
        pair_grad = mm_tn(normed_low, own_terms.reshape(rows, 2 * KV * HD))
        query_grad = mm_tn(normed_low, query_back)
        projection_grad = mm_tn(attended_low, branch_grad)
        blocks = by_target(jnp.concatenate([projection_grad, query_grad, pair_grad], axis=1))
        mixed_rows = collect(mixed)[0]
    weight_rows = scatter(blocks)
    if not merged:
        own_terms = own_terms.reshape((1,) + terms.shape[1:])
    grad_tokens, first_grads = input_back(
        query_back,
        own_terms,
        qkv_full,
        tokens.reshape(rows, D),
        inverse_one,
        first_scale[None],
        hidden_grad,
    )
    first_grads = first_grads[0]
    if merged:
        fill(role * mine, pair_sum(operands["p0"], "p2a", "p2b", "p2c"))
        fill((1 - role) * mine, pair_sum(messages["p1"], "p3"))
        fill(role * mine + 1, pair_sum(operands["q0"], "q2a", "q2b", "q2c"))
        first_grads, mixed_sums[0], shards = step(["q1"], (first_grads, mixed_sums[0], shards), [])
    gain_columns = jnp.stack([first_grads, second_grads]).reshape(2, F, Dl).transpose(1, 0, 2)
    gain_columns = gain_columns.reshape(F, cut, -1)
    gain_count = gain_columns.shape[2]
    gain_columns = jnp.pad(gain_columns, ((0, 0), (0, 0), (0, -gain_count % HD)))
    weight_rows, gain_columns = gate(weight_rows, gain_columns)
    wide = jnp.concatenate([weight_rows, gain_columns.astype(BF16)], axis=2)
    wide = fsdp_scatter_sum(wide).astype(BF16)
    if merged:
        mixed_rows = mixed_sums[0] + far.astype(F32)
    block_rows = (hidden + mixed_rows[:, :D]).astype(BF16)
    router_by_expert = mixed_rows[:, D : D + EXPERTS]
    grad_router = jnp.sum(jnp.where(hit, router_by_expert[:, None, :], 0.0), axis=2)
    wide, block_rows, grad_router = step([], (wide, block_rows, grad_router), ["q3"])
    wide = lax.all_gather(wide, "ctx", axis=0, tiled=False)
    whole = wide[:, :, : D + width + 2 * KV * HD].reshape(Dl, -1).astype(F32)
    grad_projection, grad_query = whole[:, :D], whole[:, D : D + width]
    grad_pairs = whole[:, D + width :].reshape(Dl, KV, 2, HD)
    gain_at = D + width + 2 * KV * HD
    gain_sums = jnp.sum(wide[:, :, gain_at : gain_at + gain_count].astype(F32), axis=0)
    grad_first, grad_second = gain_sums.reshape(2, Dl)

    grad_key = grad_pairs[:, :, 0].reshape(Dl, KV * HD)
    grad_value = grad_pairs[:, :, 1].reshape(Dl, KV * HD)
    grads = (grad_projection, grad_query, grad_key, grad_value, grad_first, grad_second)
    grads = step(["q3"], grads, [])
    grad_projection, grad_query, grad_key, grad_value, grad_first, grad_second = grads
    if merged:
        fill((1 - role) * mine + 1, pair_sum(messages["q1"], "q3"))
        grad_up, grad_down = shards
    else:
        grad_up, grad_down = [
            lax.psum_scatter(
                jnp.stack([out[2 + i] for out in outs]), "fsdp", scatter_dimension=1, tiled=True
            ).astype(F32)
            for i in range(2)
        ]

    shape = (batches, seqs_here, tl)
    return (
        block_rows.reshape(shape + (D,)),
        grad_tokens.reshape(shape + (D,)),
        grad_router.reshape(shape + (TOP,)),
        grad_first,
        grad_second,
        grad_query,
        grad_key,
        grad_value,
        grad_projection,
        grad_up,
        grad_down,
    )


def solution(mesh):
    rows = P(None, "fsdp", "ctx", None)
    weight = P("fsdp", None)
    expert = P("ctx", "fsdp", None)
    placed = (rows, P(None, "fsdp"), rows, rows, P("fsdp"), P("fsdp"))
    placed = placed + (weight,) * 4 + (expert,) * 2 + (rows,)
    outs = (rows, rows, rows, P("fsdp"), P("fsdp")) + (weight,) * 4 + (expert,) * 2
    return jax.shard_map(local, mesh=mesh, in_specs=placed, out_specs=outs, check_vma=False)
```
